32 devices in a mesh: groups: 2 (over x), xy: 16 (over z, y, core).
Axes of the slice: x: 2, y: 2, z: 4, core: 2. Of those that a mesh axis runs over, the one named last changes fastest.
Arguments:
- field: bfloat16 [128, 512, 512], P(('groups', 'xy')), parts along dimension 0, may hold values from -6 to 6
- spectral_weight: bfloat16 [24, 24, 2048], replicated, may hold values from -9 to 9
- local_weight: bfloat16 [32, 32], replicated, may hold values from -1 to 1
- bias: float32 [32], replicated, may hold values from -3 to 3
- cotangent: bfloat16 [128, 512, 512], P(('groups', 'xy')), parts along dimension 0, may hold values from -6 to 6
Outputs:
- output_field: bfloat16 [128, 512, 512], P(('groups', 'xy')), parts along dimension 0
- field_grad: bfloat16 [128, 512, 512], P(('groups', 'xy')), parts along dimension 0
- spectral_grad: bfloat16 [48, 24, 2048], P('groups'), parts along dimension 0
- local_grad: float32 [64, 32], P('groups'), parts along dimension 0
- bias_grad: float32 [64], P('groups'), parts along dimension 0
The draws below stay inside these ranges and needn't reach their ends.
There are 2 independent parts, one for each index of `groups`. The reference program is written for one: setup_inputs(seed, part) draws one part's arguments, and reference() takes and returns one part's arrays. A program takes and returns all parts, laid end to end along the dimension named above; an argument that names none is the same for every part. Nothing has to cross between parts.
All inputs are finite; a program needn't handle non-finite values.
Results may differ from the reference program's by a relative error of at most 0.012.
The reference program's roundings to bfloat16 on the way count: a program that leaves them out, or rounds other values in their place, can miss the bound.
Values may be sent and summed in bfloat16 or wider, within the bound.
No kernel may reach another device: no remote copies, remote signals or barrier semaphores. Data moves between devices by JAX's collectives and lax.ppermute only.
A program may use at most 128 MiB of HBM per device.

```python
import math
import jax
import jax.numpy as jnp
from jax import lax

C = 32
KX = 24
KY = 24
NY = 512
P_SIZE = 16
NX = 64


def block_scale(rng, shape, split, smallest, top_value):
    level, own = 1.0, jax.random.fold_in(rng, 6)
    for position, blocks in split:
        steps = jnp.exp(jax.random.uniform(jax.random.fold_in(own, position), (blocks,), jnp.float32, smallest / len(split), top_value / len(split)))
        level = level * jnp.repeat(steps, shape[position] // blocks).reshape([-1 if axis == position else 1 for axis in range(len(shape))])
    return level


def noise(own_key, shape, width, reach, shards=(), kind=jnp.bfloat16):
    level = block_scale(own_key, shape, shards, -0.22, 0.18) if shards else 1.0
    entries = jax.random.normal(own_key, shape, jnp.float32) * width * level
    return jnp.minimum(jnp.maximum(entries, -reach), reach).astype(kind)


def setup_inputs(seed: int = 0, part: int = 0) -> dict:
    seeds = jax.random.split(jax.random.key(seed), 6)
    part_splits = jax.random.split(jax.random.fold_in(seeds[5], part), 6)
    field = noise(part_splits[0], (NX, NY, P_SIZE * C), 1.0, 6.0, ((0, 16),))
    spectral_weight = noise(seeds[1], (KX, KY, 2 * C * C), 1.5, 9.0)
    local_weight = noise(seeds[2], (C, C), C ** -0.5, 1.0)
    bias = noise(seeds[3], (C,), 0.5, 3.0, (), jnp.float32)
    cotangent = noise(part_splits[4], (NX, NY, P_SIZE * C), 1.0, 6.0, ((0, 16),))
    return {"field": field, "spectral_weight": spectral_weight, "local_weight": local_weight, "bias": bias, "cotangent": cotangent}


def ytable(count, length, weighted):
    modes = jnp.arange(count, dtype=jnp.int32)
    places = jnp.arange(length, dtype=jnp.int32)
    phase = 2.0 * math.pi * (modes[:, None] * places[None, :] % length).astype(jnp.float32) / length
    factor = jnp.where(modes == 0, 1.0, 2.0).astype(jnp.float32) if weighted else jnp.ones((count,), jnp.float32)
    scale = factor[:, None] / math.sqrt(length)
    return jnp.stack([scale * jnp.cos(phase), -scale * jnp.sin(phase)]).astype(jnp.bfloat16)

def xtable(count, length, places):
    index = jnp.arange(count, dtype=jnp.int32)
    modes = jnp.where(index < count // 2, index, length - count + index)
    phase = 2.0 * math.pi * (modes[:, None] * places[None, :] % length).astype(jnp.float32) / length
    return (jnp.stack([jnp.cos(phase), jnp.sin(phase)]) / math.sqrt(length)).astype(jnp.bfloat16)

def mult(form, left, right):
    return jnp.einsum(form, left.astype(jnp.float32), right.astype(jnp.float32), precision=lax.Precision.HIGHEST)

def to_slab(flat, table, planes):
    rows = flat.shape[0]
    count = table.shape[1]
    chans = flat.shape[2] // planes
    coeff = mult('smy,xyq->xsmq', table, flat).astype(jnp.bfloat16)
    coeff = coeff.reshape(rows, 2, count, planes, chans).transpose(0, 2, 3, 1, 4)
    return coeff.reshape(rows, count * planes, 2, chans)

def from_slab(slab, table, planes):
    rows = slab.shape[0]
    count = table.shape[1]
    chans = slab.shape[3]
    spread = slab.reshape(rows, count, planes, 2, chans)
    return mult('smy,xmpsc->xypc', table, spread).reshape(rows, table.shape[2], planes * chans)

def forward_x(table, pencil):
    proj = mult('ajx,xnsc->ajnsc', table, pencil)
    real_part = proj[0, :, :, 0] + proj[1, :, :, 1]
    imag_part = proj[0, :, :, 1] - proj[1, :, :, 0]
    return jnp.stack([real_part, imag_part], axis=2).astype(jnp.bfloat16)

def inverse_x(table, modes):
    proj = mult('ajx,jnsc->axnsc', table, modes)
    real_part = proj[0, :, :, 0] - proj[1, :, :, 1]
    imag_part = proj[0, :, :, 1] + proj[1, :, :, 0]
    return jnp.stack([real_part, imag_part], axis=2).astype(jnp.bfloat16)

def mix_modes(spectrum, weights):
    real_part = mult('jnc,jnco->jno', spectrum[:, :, 0], weights[:, :, 0]) - mult('jnc,jnco->jno', spectrum[:, :, 1], weights[:, :, 1])
    imag_part = mult('jnc,jnco->jno', spectrum[:, :, 0], weights[:, :, 1]) + mult('jnc,jnco->jno', spectrum[:, :, 1], weights[:, :, 0])
    return jnp.stack([real_part, imag_part], axis=2).astype(jnp.bfloat16)

def adjoint_mix(grads, weights):
    real_part = mult('jnco,jno->jnc', weights[:, :, 0], grads[:, :, 0]) + mult('jnco,jno->jnc', weights[:, :, 1], grads[:, :, 1])
    imag_part = mult('jnco,jno->jnc', weights[:, :, 0], grads[:, :, 1]) - mult('jnco,jno->jnc', weights[:, :, 1], grads[:, :, 0])
    return jnp.stack([real_part, imag_part], axis=2).astype(jnp.bfloat16)

def pair_grad(spectrum, grads):
    real_part = mult('jmpc,jmpo->jmco', spectrum[:, :, :, 0], grads[:, :, :, 0]) + mult('jmpc,jmpo->jmco', spectrum[:, :, :, 1], grads[:, :, :, 1])
    imag_part = mult('jmpc,jmpo->jmco', spectrum[:, :, :, 0], grads[:, :, :, 1]) - mult('jmpc,jmpo->jmco', spectrum[:, :, :, 1], grads[:, :, :, 0])
    return jnp.stack([real_part, imag_part], axis=2)

def reference(field, spectral_weight, local_weight, bias, cotangent):
    length_x, length_y, width_all = field.shape
    chans = local_weight.shape[0]
    planes = width_all // chans
    modes_x, modes_y = (spectral_weight.shape[0], spectral_weight.shape[1])
    table_y = ytable(modes_y, length_y, False)
    table_yw = ytable(modes_y, length_y, True)
    table_x = xtable(modes_x, length_x, jnp.arange(length_x, dtype=jnp.int32))
    weight_all = spectral_weight.reshape(modes_x, modes_y, 2, chans, chans)
    weight_pairs = jnp.repeat(weight_all, planes, axis=1)
    spectrum = forward_x(table_x, to_slab(field, table_y, planes))
    mixed = mix_modes(spectrum, weight_pairs)
    spatial = from_slab(inverse_x(table_x, mixed), table_yw, planes)
    field4 = field.reshape(length_x, length_y, planes, chans)
    local_term = mult('xypc,co->xypo', field4, local_weight)
    preact = spatial.reshape(length_x, length_y, planes, chans) + local_term + bias
    output_field = jax.nn.gelu(preact).astype(jnp.bfloat16).reshape(length_x, length_y, width_all)
    unused, pullback = jax.vjp(jax.nn.gelu, preact)
    grad_pre = pullback(cotangent.reshape(length_x, length_y, planes, chans).astype(jnp.float32))[0].astype(jnp.bfloat16)
    bias_grad = lax.optimization_barrier(jnp.sum(grad_pre.astype(jnp.float32), axis=(0, 1, 2)))
    local_grad = mult('xypc,xypo->co', field4, grad_pre)
    back_local = mult('xypo,co->xypc', grad_pre, local_weight)
    grad_modes = forward_x(table_x, to_slab(grad_pre.reshape(length_x, length_y, width_all), table_yw, planes))
    grad_spec = adjoint_mix(grad_modes, weight_pairs)
    back_spec = from_slab(inverse_x(table_x, grad_spec), table_y, planes)
    field_grad = (back_spec + back_local.reshape(length_x, length_y, width_all)).astype(jnp.bfloat16)
    total = pair_grad(spectrum.reshape(modes_x, modes_y, planes, 2, chans), grad_modes.reshape(modes_x, modes_y, planes, 2, chans))
    spectral_grad = total.reshape(modes_x, modes_y, 2 * chans * chans).astype(jnp.bfloat16)
    return (output_field, field_grad, spectral_grad, local_grad, bias_grad)
```

```python
import math

import jax
import jax.numpy as jnp
import ml_dtypes
import numpy as np
from jax import lax
from jax.experimental import pallas as pl
from jax.experimental.pallas import tpu as pltpu
from jax.sharding import PartitionSpec as P


def ytable(count, length, weighted):
    modes = jnp.arange(count, dtype=jnp.int32)
    places = jnp.arange(length, dtype=jnp.int32)
    phase = 2.0 * math.pi * (modes[:, None] * places[None, :] % length).astype(jnp.float32) / length
    factor = (
        jnp.where(modes == 0, 1.0, 2.0).astype(jnp.float32)
        if weighted
        else jnp.ones((count,), jnp.float32)
    )
    scale = factor[:, None] / math.sqrt(length)
    return jnp.stack([scale * jnp.cos(phase), -scale * jnp.sin(phase)]).astype(jnp.bfloat16)


def xtable(count, length, places):
    index = jnp.arange(count, dtype=jnp.int32)
    modes = jnp.where(index < count // 2, index, length - count + index)
    phase = 2.0 * math.pi * (modes[:, None] * places[None, :] % length).astype(jnp.float32) / length
    return (jnp.stack([jnp.cos(phase), jnp.sin(phase)]) / math.sqrt(length)).astype(jnp.bfloat16)


def mult(form, left, right):
    return jnp.einsum(form, left, right, preferred_element_type=jnp.float32)


def to_slab(flat, table, planes):
    rows = flat.shape[0]
    count = table.shape[1]
    chans = flat.shape[2] // planes
    coeff = mult("smy,xyq->xsmq", table, flat).astype(jnp.bfloat16)
    coeff = coeff.reshape(rows, 2, count, planes, chans).transpose(0, 2, 3, 1, 4)
    return coeff.reshape(rows, count * planes, 2 * chans)


def from_slab(slab, table, planes):
    rows = slab.shape[0]
    count = table.shape[1]
    chans = slab.shape[2] // 2
    spread = slab.reshape(rows, count, planes, 2, chans)
    return mult("smy,xmpsc->xypc", table, spread).reshape(rows, table.shape[2], planes * chans)


def forward_x(table, pencil):
    proj = mult("ajx,xnsc->ajnsc", table, pencil)
    real_part = proj[0, :, :, 0] + proj[1, :, :, 1]
    imag_part = proj[0, :, :, 1] - proj[1, :, :, 0]
    return jnp.stack([real_part, imag_part], axis=2).astype(jnp.bfloat16)


def inverse_x(table, modes):
    proj = mult("ajx,jnsc->axnsc", table, modes)
    real_part = proj[0, :, :, 0] - proj[1, :, :, 1]
    imag_part = proj[0, :, :, 1] + proj[1, :, :, 0]
    return jnp.stack([real_part, imag_part], axis=2).astype(jnp.bfloat16)


def mix_modes(spectrum, weights):
    real_part = mult("jnc,jnco->jno", spectrum[:, :, 0], weights[:, :, 0]) - mult(
        "jnc,jnco->jno", spectrum[:, :, 1], weights[:, :, 1]
    )
    imag_part = mult("jnc,jnco->jno", spectrum[:, :, 0], weights[:, :, 1]) + mult(
        "jnc,jnco->jno", spectrum[:, :, 1], weights[:, :, 0]
    )
    return jnp.stack([real_part, imag_part], axis=2).astype(jnp.bfloat16)


def adjoint_mix(grads, weights):
    real_part = mult("jnco,jno->jnc", weights[:, :, 0], grads[:, :, 0]) + mult(
        "jnco,jno->jnc", weights[:, :, 1], grads[:, :, 1]
    )
    imag_part = mult("jnco,jno->jnc", weights[:, :, 0], grads[:, :, 1]) - mult(
        "jnco,jno->jnc", weights[:, :, 1], grads[:, :, 0]
    )
    return jnp.stack([real_part, imag_part], axis=2).astype(jnp.bfloat16)


def pair_grad(spectrum, grads):
    real_part = mult("jmpc,jmpo->jmco", spectrum[:, :, :, 0], grads[:, :, :, 0]) + mult(
        "jmpc,jmpo->jmco", spectrum[:, :, :, 1], grads[:, :, :, 1]
    )
    imag_part = mult("jmpc,jmpo->jmco", spectrum[:, :, :, 0], grads[:, :, :, 1]) - mult(
        "jmpc,jmpo->jmco", spectrum[:, :, :, 1], grads[:, :, :, 0]
    )
    return jnp.stack([real_part, imag_part], axis=2)


def to_modes(slab, table_full):
    count = table_full.shape[1]
    pencil = lax.all_to_all(slab, "xy", split_axis=1, concat_axis=0, tiled=True)
    chans = pencil.shape[2] // 2
    items = pencil.shape[1]
    spread = pencil.reshape(pencil.shape[0], items, 2, chans)
    return forward_x(table_full, spread).reshape(count, items, 2 * chans)


def to_space(modes, table_full):
    count, pairs_dev, twice, chans = modes.shape
    pencil = inverse_x(table_full, modes)
    moved = lax.all_to_all(
        pencil.reshape(pencil.shape[0], pairs_dev, 2 * chans),
        "xy",
        split_axis=0,
        concat_axis=1,
        tiled=True,
    )
    return moved


def general_shards(field, spectral_weight, local_weight, bias, cotangent):
    rows, length_y, width_all = field.shape
    chans = local_weight.shape[0]
    planes = width_all // chans
    modes_x, modes_y = (spectral_weight.shape[0], spectral_weight.shape[1])
    devices = lax.axis_size("xy")
    length_x = rows * devices
    pairs_dev = modes_y * planes // devices
    offset = lax.axis_index("xy")
    table_y = ytable(modes_y, length_y, False)
    table_yw = ytable(modes_y, length_y, True)
    table_x = xtable(modes_x, length_x, jnp.arange(length_x, dtype=jnp.int32))
    weight_all = spectral_weight.reshape(modes_x, modes_y, 2, chans, chans)
    ky_index = (offset * pairs_dev + jnp.arange(pairs_dev, dtype=jnp.int32)) // planes
    weight_pairs = jnp.take(weight_all, ky_index, axis=1)
    spectrum = to_modes(to_slab(field, table_y, planes), table_x).reshape(
        modes_x, pairs_dev, 2, chans
    )
    mixed = mix_modes(spectrum, weight_pairs)
    spatial = from_slab(to_space(mixed, table_x), table_yw, planes)
    field4 = field.reshape(rows, length_y, planes, chans)
    local_term = mult("xypc,co->xypo", field4, local_weight)
    preact = spatial.reshape(rows, length_y, planes, chans) + local_term + bias
    output_field = jax.nn.gelu(preact).astype(jnp.bfloat16).reshape(rows, length_y, width_all)
    unused, pullback = jax.vjp(jax.nn.gelu, preact)
    grad_pre = pullback(cotangent.reshape(rows, length_y, planes, chans).astype(jnp.float32))[
        0
    ].astype(jnp.bfloat16)
    bias_part = jnp.sum(grad_pre.astype(jnp.float32), axis=(0, 1, 2))
    weight_part = mult("xypc,xypo->co", field4, grad_pre)
    back_local = mult("xypo,co->xypc", grad_pre, local_weight)
    grad_slab = to_slab(grad_pre.reshape(rows, length_y, width_all), table_yw, planes)
    grad_modes = to_modes(grad_slab, table_x).reshape(modes_x, pairs_dev, 2, chans)
    grad_spec = adjoint_mix(grad_modes, weight_pairs)
    back_spec = from_slab(to_space(grad_spec, table_x), table_y, planes)
    field_grad = (back_spec + back_local.reshape(rows, length_y, width_all)).astype(jnp.bfloat16)
    per_pair = pair_grad(
        spectrum.reshape(modes_x, pairs_dev, 1, 2, chans),
        grad_modes.reshape(modes_x, pairs_dev, 1, 2, chans),
    )
    onehot = (ky_index[:, None] == jnp.arange(modes_y, dtype=jnp.int32)[None, :]).astype(
        jnp.float32
    )
    partial_grad = jnp.einsum("jnsco,nm->jmsco", per_pair, onehot, precision=lax.Precision.HIGHEST)
    total, local_grad, bias_grad = lax.psum((partial_grad, weight_part, bias_part), "xy")
    spectral_grad = total.reshape(modes_x, modes_y, 2 * chans * chans).astype(jnp.bfloat16)
    return (output_field, field_grad, spectral_grad, local_grad, bias_grad)


F32 = jnp.float32
BF16 = jnp.bfloat16
LANES = 128
VMEM_LIMIT = 48 * 1024 * 1024


def dot(left, right):
    return jnp.dot(left, right, preferred_element_type=F32)


def params(**kwargs):
    return pltpu.CompilerParams(vmem_limit_bytes=VMEM_LIMIT, **kwargs)


def cost(flops, bytes_accessed):
    return pl.CostEstimate(flops=flops, bytes_accessed=bytes_accessed, transcendentals=0)


def np_ytable(count, length, weighted):
    modes = np.arange(count)
    places = np.arange(length)
    phase = np.float32(2.0 * math.pi) * (modes[:, None] * places[None, :] % length).astype(np.float32) / np.float32(length)
    factor = np.where(modes == 0, 1.0, 2.0).astype(np.float32) if weighted else np.ones((count,), np.float32)
    scale = (factor / np.float32(math.sqrt(length)))[:, None]
    both = np.stack([scale * np.cos(phase), -scale * np.sin(phase)]).astype(ml_dtypes.bfloat16)
    return both.reshape(2 * count, length)


def np_xtables(count, length):
    index = np.arange(count)
    modes = np.where(index < count // 2, index, length - count + index)
    places = np.arange(length)
    phase = np.float32(2.0 * math.pi) * (modes[:, None] * places[None, :] % length).astype(np.float32) / np.float32(length)
    norm = np.float32(math.sqrt(length))
    cosines = np.cos(phase) / norm
    sines = np.sin(phase) / norm
    forward = np.stack([np.stack([cosines, sines], -1), np.stack([-sines, cosines], -1)])
    forward = forward.reshape(2 * count, 2 * length).astype(ml_dtypes.bfloat16)
    return forward, np.ascontiguousarray(forward.T)


def np_spread(chans):
    groups = LANES // chans
    out = np.zeros((groups, chans, chans, groups, chans), np.float32)
    for g in range(groups):
        for k in range(chans):
            out[g, k, k, g, :] = 1
    return out.reshape(LANES, chans * LANES).astype(ml_dtypes.bfloat16)


def np_tile(chans):
    groups = LANES // chans
    out = np.zeros((groups, chans, groups, groups, chans), np.float32)
    for g in range(groups):
        for k in range(chans):
            out[g, k, g, :, k] = 1
    return out.reshape(LANES, groups * LANES).astype(ml_dtypes.bfloat16)


def np_widen(chans):
    groups = LANES // chans
    step = 2 * LANES // chans
    parts = chans // step
    out = np.zeros((parts, groups, chans, groups, step, chans), np.float32)
    for a in range(parts):
        for g in range(groups):
            for k in range(step):
                out[a, g, a * step + k, g, k, :] = 1
    return out.reshape(parts, LANES, groups * step * chans).astype(ml_dtypes.bfloat16)


def scatter_rows(dst, sums, place, chips, half):
    tiles = half // LANES
    for s in range(2):
        for core in range(2):
            where = pl.ds(core * 8 + 2 * place + s, chips, stride=16)
            own = (3 * s + 2 * core) * chips
            shared = (3 * s + 1) * chips
            for k in range(2 * tiles):
                dst[k, where, :] = sums[own : own + chips, k * LANES : (k + 1) * LANES]
            for k in range(tiles):
                at = (core * tiles + k) * LANES
                dst[2 * tiles + k, where, :] = sums[shared : shared + chips, at : at + LANES]


def gather_rows(src, place, chips, half):
    tiles = half // LANES
    out = []
    for s in range(2):
        one = pl.ds(2 * place + s, chips, stride=16)
        two = pl.ds(8 + 2 * place + s, chips, stride=16)
        own = range(2 * tiles)
        shared = range(2 * tiles, 3 * tiles)
        out.append(jnp.concatenate([src[k, one, :] for k in own], axis=1))
        out.append(jnp.concatenate([src[k, w, :] for w in (one, two) for k in shared], axis=1))
        out.append(jnp.concatenate([src[k, two, :] for k in own], axis=1))
    return jnp.concatenate(out, axis=0).astype(BF16)


def cut_lanes(dst, src):
    for k in range(dst.shape[0]):
        dst[k] = src[:, k * LANES : (k + 1) * LANES].astype(F32)


def join_lanes(dst, src):
    for k in range(src.shape[0]):
        dst[:, k * LANES : (k + 1) * LANES] = src[k].astype(BF16)


def cut_shape(shape):
    return (shape[1] // LANES, shape[0], LANES)


def rows_to_modes(field, table, chips, half):
    rows, length, width = field.shape

    def kernel(u_ref, t_ref, out_ref, scr):
        place = pl.program_id(0)
        scatter_rows(scr, dot(t_ref[...], u_ref[0]), place, chips, half)

        @pl.when(place == rows - 1)
        def _():
            join_lanes(out_ref, scr)

    shape = (chips * 16, 3 * half)
    return pl.pallas_call(
        kernel,
        grid=(rows,),
        in_specs=[
            pl.BlockSpec((1, length, width), lambda i: (i, 0, 0)),
            pl.BlockSpec(table.shape, lambda i: (0, 0)),
        ],
        out_specs=pl.BlockSpec(shape, lambda i: (0, 0)),
        out_shape=jax.ShapeDtypeStruct(shape, BF16),
        scratch_shapes=[pltpu.VMEM(cut_shape(shape), F32)],
        compiler_params=params(),
        cost_estimate=cost(2 * table.size * rows * width, field.size * 2),
        name="rows_to_modes",
    )(field, table)


def spread_weights(weights, tile):
    rows, width = weights.shape
    groups = width // LANES

    def kernel(w_ref, t_ref, out_ref):
        for g in range(groups):
            out_ref[g] = dot(w_ref[:, g * LANES : (g + 1) * LANES], t_ref[...])

    shape = (groups, rows, tile.shape[1])
    return pl.pallas_call(
        kernel,
        out_shape=jax.ShapeDtypeStruct(shape, F32),
        compiler_params=params(),
        cost_estimate=cost(2 * rows * width * tile.shape[1], rows * width * 2),
        name="spread_weights",
    )(weights, tile)


def mode_step(pencil, spread_w, spread, forward, inverse, modes_x, adjoint):
    wide = pencil.shape[1]
    tiles = wide // LANES
    chans = spread.shape[1] // LANES
    groups = LANES // chans

    def kernel(p_ref, w_ref, e_ref, f_ref, i_ref, spec_ref, out_ref):
        spec = dot(f_ref[...], p_ref[...]).astype(BF16)
        spec_ref[...] = spec
        stack = jnp.concatenate([spec[:, k * LANES : (k + 1) * LANES] for k in range(tiles)], axis=0)
        real = [None] * tiles
        imag = [None] * tiles
        for pair in range(chans // 2):
            wide_rows = dot(stack, e_ref[:, pair * 2 * LANES : (pair + 1) * 2 * LANES])
            for c in (2 * pair, 2 * pair + 1):
                lanes = slice((c % 2) * LANES, (c % 2 + 1) * LANES)
                wl = slice((c % groups) * LANES, (c % groups + 1) * LANES)
                for k in range(tiles):
                    own = 0 if k < 2 * tiles // 3 else 1
                    base = 2 * own * modes_x
                    wr = w_ref[c // groups, base : base + modes_x, wl]
                    wi = w_ref[c // groups, base + modes_x : base + 2 * modes_x, wl]
                    xr = wide_rows[2 * k * modes_x : (2 * k + 1) * modes_x, lanes]
                    xi = wide_rows[(2 * k + 1) * modes_x : (2 * k + 2) * modes_x, lanes]
                    if adjoint:
                        r, i = xr * wr + xi * wi, xi * wr - xr * wi
                    else:
                        r, i = xr * wr - xi * wi, xr * wi + xi * wr
                    real[k] = r if real[k] is None else real[k] + r
                    imag[k] = i if imag[k] is None else imag[k] + i
        mixed = jnp.concatenate([jnp.concatenate(real, axis=1), jnp.concatenate(imag, axis=1)], axis=0)
        out_ref[...] = dot(i_ref[...], mixed.astype(BF16)).astype(BF16)

    return pl.pallas_call(
        kernel,
        out_shape=(
            jax.ShapeDtypeStruct((2 * modes_x, wide), BF16),
            jax.ShapeDtypeStruct(pencil.shape, BF16),
        ),
        compiler_params=params(),
        cost_estimate=cost(2 * 48 * 6 * 128 * 4096, spread_w.size * 4),
        name="adjoint_step" if adjoint else "mode_step",
    )(pencil, spread_w, spread, forward, inverse)


def pointwise(field, cotangent, pencil, table_t, table, block_weight, bias_row, chips, half):
    rows, length, width = field.shape
    chunk = 64

    def kernel(u_ref, c_ref, p_ref, tt_ref, t_ref, w_ref, b_ref, out_ref, dpre_ref, send_ref, bscr, dscr):
        place = pl.program_id(0)

        @pl.when(place == 0)
        def _():
            cut_lanes(bscr, p_ref)

        coeff = gather_rows(bscr, place, chips, half)
        bias = b_ref[...]
        root = math.sqrt(2.0 / math.pi)
        for k in range(length // chunk):
            where = pl.ds(k * chunk, chunk)
            u = u_ref[0, where, :]
            spec = dot(tt_ref[where, :], coeff)
            for h in range(2):
                lanes = slice(h * half, (h + 1) * half)
                pre = spec[:, lanes] + dot(u[:, lanes], w_ref[...]) + bias[:, lanes]
                square = pre * pre
                th = jnp.tanh(pre * (root + (root * 0.044715) * square))
                cdf = 0.5 * th + 0.5
                out_ref[0, where, lanes] = (pre * cdf).astype(BF16)
                slope = pre * (root + (3.0 * root * 0.044715) * square)
                grad = cdf + slope * (0.5 - 0.5 * (th * th))
                dpre_ref[0, where, lanes] = (c_ref[0, where, lanes].astype(F32) * grad).astype(BF16)
        scatter_rows(dscr, dot(t_ref[...], dpre_ref[0]), place, chips, half)

        @pl.when(place == rows - 1)
        def _():
            join_lanes(send_ref, dscr)

    slab = pl.BlockSpec((1, length, width), lambda i: (i, 0, 0))

    def whole(a):
        return pl.BlockSpec(a.shape, lambda i: (0,) * a.ndim)

    return pl.pallas_call(
        kernel,
        grid=(rows,),
        in_specs=[slab, slab] + [whole(a) for a in (pencil, table_t, table, block_weight, bias_row)],
        out_specs=[slab, slab, whole(pencil)],
        out_shape=[
            jax.ShapeDtypeStruct(field.shape, BF16),
            jax.ShapeDtypeStruct(field.shape, BF16),
            jax.ShapeDtypeStruct(pencil.shape, BF16),
        ],
        scratch_shapes=[pltpu.VMEM(cut_shape(pencil.shape), F32), pltpu.VMEM(cut_shape(pencil.shape), F32)],
        compiler_params=params(),
        cost_estimate=cost(field.size * 1000, field.size * 8),
        name="pointwise",
    )(field, cotangent, pencil, table_t, table, block_weight, bias_row)


def local_sums(field, dpre, chans, half):
    rows, length, width = field.shape
    slices = half // chans

    def kernel(u_ref, d_ref, out_ref, acc, bacc):
        place = pl.program_id(0)
        for h in range(2):
            lanes = slice(h * half, (h + 1) * half)
            part = lax.dot_general(
                u_ref[0, :, lanes], d_ref[0, :, lanes], (((0,), (0,)), ((), ())), preferred_element_type=F32
            )
            acc[h] = jnp.where(place == 0, part, acc[h] + part)
        ones = jnp.ones((16, length), BF16)
        part = dot(ones, d_ref[0])[0:8]
        bacc[...] = jnp.where(place == 0, part, bacc[...] + part)

        @pl.when(place == rows - 1)
        def _():
            group = lax.broadcasted_iota(jnp.int32, (chans, half), 1) // chans
            both = acc[0] + acc[1]
            total = jnp.zeros((chans, half), F32)
            for p in range(slices):
                total = jnp.where(group == p, both[p * chans : (p + 1) * chans], total)
            total = sum(total[:, k * LANES : (k + 1) * LANES] for k in range(half // LANES))
            bias = sum(bacc[:, k * LANES : (k + 1) * LANES] for k in range(width // LANES))
            shift = LANES // 2
            while shift >= chans:
                total = total + pltpu.roll(total, shift, 1)
                bias = bias + pltpu.roll(bias, shift, 1)
                shift //= 2
            group8 = lax.broadcasted_iota(jnp.int32, (8, LANES), 1) // chans
            folded = jnp.zeros((8, LANES), F32)
            for k in range(chans // 8):
                folded = jnp.where(group8 == k, total[8 * k : 8 * k + 8], folded)
            value = jnp.concatenate([folded, bias], axis=0)
            high = value.astype(BF16).astype(F32)
            mid = (value - high).astype(BF16).astype(F32)
            low = value - high - mid
            left = jnp.concatenate([high, mid[0:8]], axis=0)
            right = jnp.concatenate([mid[8:16], low], axis=0)
            out_ref[...] = jnp.concatenate([left, right], axis=1).astype(BF16)

    slab = pl.BlockSpec((1, length, width), lambda i: (i, 0, 0))
    return pl.pallas_call(
        kernel,
        grid=(rows,),
        in_specs=[slab, slab],
        out_specs=pl.BlockSpec((24, 2 * LANES), lambda i: (0, 0)),
        out_shape=jax.ShapeDtypeStruct((24, 2 * LANES), BF16),
        scratch_shapes=[pltpu.VMEM((2, half, half), F32), pltpu.VMEM((8, width), F32)],
        compiler_params=params(),
        cost_estimate=cost(field.size * 1000, field.size * 4),
        name="local_sums",
    )(field, dpre)


def weight_sums(core, spectrum, grads, widen, tile, modes_x, chans):
    wide = spectrum.shape[1]
    tiles = wide // LANES
    groups = LANES // chans
    parts = widen.shape[0]
    step = 2 * LANES
    full = chans * chans

    def kernel(core_ref, u_ref, d_ref, f_ref, h_ref, own_ref, keep_ref, send_ref):
        def stack(ref):
            return jnp.concatenate([ref[:, k * LANES : (k + 1) * LANES] for k in range(tiles)], axis=0)

        first = core_ref[0] == 0
        left = stack(u_ref)
        right = dot(stack(d_ref), h_ref[...])
        for a in range(parts):
            sums = {}
            for g in range(groups):
                spread_u = dot(left, f_ref[a, :, g * step : (g + 1) * step])
                for k in range(tiles):
                    kind = 0 if k < 2 * tiles // 3 else 1
                    re = slice(2 * k * modes_x, (2 * k + 1) * modes_x)
                    im = slice((2 * k + 1) * modes_x, (2 * k + 2) * modes_x)
                    for z in range(2):
                        lanes = slice(z * LANES, (z + 1) * LANES)
                        ur, ui = spread_u[re, lanes], spread_u[im, lanes]
                        dr = right[re, g * LANES : (g + 1) * LANES]
                        di = right[im, g * LANES : (g + 1) * LANES]
                        for t, term in ((0, ur * dr + ui * di), (1, ur * di - ui * dr)):
                            key = (kind, t, z)
                            sums[key] = term if key not in sums else sums[key] + term
            for t in range(2):
                own = jnp.concatenate([sums[0, t, 0], sums[0, t, 1]], axis=1)
                own_ref[:, t * full + a * step : t * full + (a + 1) * step] = own.astype(BF16)
                shared = jnp.concatenate([sums[1, t, 0], sums[1, t, 1]], axis=1)
                at = t * (full // 2) + (a % (parts // 2)) * step
                low = a < parts // 2

                @pl.when(first if low else jnp.logical_not(first))
                def _():
                    keep_ref[:, at : at + step] = shared

                @pl.when(jnp.logical_not(first) if low else first)
                def _():
                    send_ref[:, at : at + step] = shared

    half_shape = jax.ShapeDtypeStruct((modes_x, full), F32)
    vmem = pl.BlockSpec(memory_space=pltpu.VMEM)
    return pl.pallas_call(
        kernel,
        in_specs=[pl.BlockSpec(memory_space=pltpu.SMEM)] + [vmem] * 4,
        out_shape=(jax.ShapeDtypeStruct((modes_x, 2 * full), BF16), half_shape, half_shape),
        compiler_params=params(),
        cost_estimate=cost(2 * 288 * 128 * 4096, 4 * 1024 * 1024),
        name="weight_sums",
    )(core, spectrum, grads, widen, tile)


def make_shard(own, keep, other, stats):
    rows, full2 = own.shape
    full = keep.shape[1]
    width = full2 + full + stats.shape[1]

    def kernel(o_ref, k_ref, r_ref, s_ref, out_ref):
        out_ref[:, 0:full2] = o_ref[...]
        out_ref[:, full2 : full2 + full] = (k_ref[...] + r_ref[...]).astype(BF16)
        out_ref[:, full2 + full :] = s_ref[...]

    return pl.pallas_call(
        kernel,
        out_shape=jax.ShapeDtypeStruct((rows, width), BF16),
        compiler_params=params(),
        name="make_shard",
    )(own, keep, other, stats)


def assemble(owners, shards_all, modes_y, chans, chips):
    rows = shards_all[0].shape[0]
    full = chans * chans
    count = len(shards_all)

    def kernel(owner_ref, *refs):
        ins, (g_ref, l_ref, b_ref, scr, stat) = refs[:count], refs[count:]
        for n in range(count):
            owner = owner_ref[n]
            chip, core = owner // 2, owner % 2
            ref = ins[n]
            own = pl.ds(chip + 2 * chips * core, rows, stride=modes_y)
            scr_shared = pl.ds(chip + chips, rows, stride=modes_y)
            for k in range(2 * full // LANES):
                lanes = slice(k * LANES, (k + 1) * LANES)
                scr[k, own, :] = ref[:, lanes].astype(F32)
            for t in range(2):
                for k in range(full // 2 // LANES):
                    at = 2 * full + t * (full // 2) + k * LANES
                    block = t * (full // LANES) + core * (full // 2 // LANES) + k
                    scr[block, scr_shared, :] = ref[:, at : at + LANES].astype(F32)
            left = ref[:, 3 * full : 3 * full + LANES].astype(F32)
            right = ref[:, 3 * full + LANES :].astype(F32)
            middle = jnp.concatenate([left[16:24], right[0:8]], axis=0)
            stat[owner] = left[0:16] + middle + right[8:24]
        for k in range(2 * full // LANES):
            for j in range(rows):
                g_ref[j, :, k * LANES : (k + 1) * LANES] = scr[k, j * modes_y : (j + 1) * modes_y, :].astype(BF16)
        total = stat[0]
        for n in range(1, count):
            total = total + stat[n]
        for k in range(chans // 8):
            piece = total[0:8] if k == 0 else pltpu.roll(total[0:8], LANES - k * chans, 1)
            l_ref[8 * k : 8 * k + 8, :] = piece[:, 0:chans]
        b_ref[...] = total[8:9, 0:chans]

    vmem = pl.BlockSpec(memory_space=pltpu.VMEM)
    return pl.pallas_call(
        kernel,
        in_specs=[pl.BlockSpec(memory_space=pltpu.SMEM)] + [vmem] * count,
        out_shape=(
            jax.ShapeDtypeStruct((rows, modes_y, 2 * full), BF16),
            jax.ShapeDtypeStruct((chans, chans), F32),
            jax.ShapeDtypeStruct((1, chans), F32),
        ),
        scratch_shapes=[
            pltpu.VMEM((2 * full // LANES, rows * modes_y, LANES), F32),
            pltpu.VMEM((count, 16, LANES), F32),
        ],
        compiler_params=params(),
        cost_estimate=cost(1000000, 8 * 1024 * 1024),
        name="assemble",
    )(owners, *shards_all)


def back_to_field(dpre, pencil, table_t, block_weight, chips, half):
    rows, length, width = dpre.shape
    chunk = 128

    def kernel(d_ref, p_ref, tt_ref, w_ref, out_ref, bscr):
        place = pl.program_id(0)

        @pl.when(place == 0)
        def _():
            cut_lanes(bscr, p_ref)

        coeff = gather_rows(bscr, place, chips, half)
        for k in range(length // chunk):
            where = pl.ds(k * chunk, chunk)
            d = d_ref[0, where, :]
            spec = dot(tt_ref[where, :], coeff)
            for h in range(2):
                lanes = slice(h * half, (h + 1) * half)
                out_ref[0, where, lanes] = (spec[:, lanes] + dot(d[:, lanes], w_ref[...])).astype(BF16)

    slab = pl.BlockSpec((1, length, width), lambda i: (i, 0, 0))

    def whole(a):
        return pl.BlockSpec(a.shape, lambda i: (0,) * a.ndim)

    return pl.pallas_call(
        kernel,
        grid=(rows,),
        in_specs=[slab] + [whole(a) for a in (pencil, table_t, block_weight)],
        out_specs=slab,
        out_shape=jax.ShapeDtypeStruct(dpre.shape, BF16),
        scratch_shapes=[pltpu.VMEM(cut_shape(pencil.shape), F32)],
        compiler_params=params(),
        cost_estimate=cost(dpre.size * 500, dpre.size * 4),
        name="back_to_field",
    )(dpre, pencil, table_t, block_weight)


def exchange(pencil):
    return lax.all_to_all(pencil, "xy", split_axis=0, concat_axis=0, tiled=True)


def ring_order(chips):
    return [2 * z for z in range(chips // 2)] + [2 * z + 1 for z in reversed(range(chips // 2))]


def gather_ring(shard, chips):
    order = ring_order(chips)
    me = lax.axis_index("xy")
    core = me % 2
    turn = jnp.asarray(np.array(order), jnp.int32)
    spot = jnp.asarray(np.argsort(np.array(order)), jnp.int32)[me // 2]

    def hop(way):
        return [
            (2 * order[i] + c, 2 * order[(i + way) % chips] + c) for i in range(chips) for c in range(2)
        ]

    swap = [(i, i ^ 1) for i in range(2 * chips)]
    ahead = back = shard
    parts, owners = [shard], [me]
    for step in range(1, chips // 2 + 1):
        ahead = lax.ppermute(ahead, "xy", hop(1))
        parts.append(ahead)
        owners.append(2 * turn[(spot - step) % chips] + core)
        if step < chips // 2:
            back = lax.ppermute(back, "xy", hop(-1))
            parts.append(back)
            owners.append(2 * turn[(spot + step) % chips] + core)
    other = [lax.ppermute(p, "xy", swap) for p in parts]
    owners = owners + [o ^ 1 for o in owners]
    return jnp.stack(owners).astype(jnp.int32), parts + other


def fast_shards(field, spectral_weight, local_weight, bias, cotangent):
    rows, length_y, width = field.shape
    chans = local_weight.shape[0]
    planes = width // chans
    modes_x, modes_y = spectral_weight.shape[:2]
    devices = lax.axis_size("xy")
    chips = devices // 2
    half = width // 2
    full = chans * chans
    me = lax.axis_index("xy")
    chip, core = me // 2, me % 2
    table_y = np_ytable(modes_y, length_y, False)
    table_yw = np_ytable(modes_y, length_y, True)
    table_y_t, table_yw_t = (np.ascontiguousarray(t.T) for t in (table_y, table_yw))
    forward, inverse = np_xtables(modes_x, rows * devices)
    spread, tile, widen = np_spread(chans), np_tile(chans), np_widen(chans)

    send = rows_to_modes(field, table_y, chips, half)
    pencil = exchange(send)

    mine = [
        lax.dynamic_index_in_dim(spectral_weight, m, axis=1, keepdims=False)
        for m in (chip + 2 * chips * core, chip + chips)
    ]
    weights = jnp.stack(mine).reshape(2, modes_x, 2, chans, chans).transpose(0, 2, 1, 3, 4)
    plain = weights.reshape(4 * modes_x, full)
    turned = weights.swapaxes(3, 4).reshape(4 * modes_x, full)
    spread_plain = spread_weights(plain, tile)
    spread_turned = spread_weights(turned, tile)

    eye = jnp.eye(half // chans, dtype=BF16)
    block = jnp.einsum("pq,co->pcqo", eye, local_weight).reshape(half, half)
    block_t = block.T
    bias_row = jnp.tile(bias, planes)[None, :]

    spectrum, send = mode_step(pencil, spread_plain, spread, forward, inverse, modes_x, False)
    pencil = exchange(send)
    output_field, dpre, send = pointwise(
        field, cotangent, pencil, table_yw_t, table_yw, block, bias_row, chips, half
    )
    pencil = exchange(send)
    stats = local_sums(field, dpre, chans, half)
    grads, send = mode_step(pencil, spread_turned, spread, forward, inverse, modes_x, True)
    core_id = core.astype(jnp.int32)[None]
    own, keep, give = weight_sums(core_id, spectrum, grads, widen, tile, modes_x, chans)
    got = lax.ppermute(give, "xy", [(i, i ^ 1) for i in range(devices)])
    shard = make_shard(own, keep, got, stats)
    owners, parts = gather_ring(shard, chips)
    pencil = exchange(send)
    field_grad = back_to_field(dpre, pencil, table_y_t, block_t, chips, half)
    spectral_grad, local_grad, bias_grad = assemble(owners, parts, modes_y, chans, chips)
    return output_field, field_grad, spectral_grad, local_grad, bias_grad.reshape(chans)


def fits(field, spectral_weight, local_weight, devices):
    rows, length_y, width = field.shape
    chans = local_weight.shape[0]
    modes_x, modes_y = spectral_weight.shape[:2]
    return (
        rows == 4
        and chans == 32
        and width == 512
        and length_y % 128 == 0
        and modes_x == 24
        and devices == 16
        and 2 * modes_y == 3 * devices
    )


def shards(field, spectral_weight, local_weight, bias, cotangent):
    if fits(field, spectral_weight, local_weight, lax.axis_size("xy")):
        return fast_shards(field, spectral_weight, local_weight, bias, cotangent)
    return general_shards(field, spectral_weight, local_weight, bias, cotangent)


def solution(mesh):
    return jax.shard_map(
        shards,
        mesh=mesh,
        in_specs=(P(("groups", "xy"), None, None), P(), P(), P(), P(("groups", "xy"), None, None)),
        out_specs=(
            P(("groups", "xy"), None, None),
            P(("groups", "xy"), None, None),
            P("groups", None, None),
            P("groups", None),
            P("groups"),
        ),
        check_vma=False,
    )
```

```python
import math

import jax
import jax.numpy as jnp
import ml_dtypes
import numpy as np
from jax import lax
from jax.experimental import pallas as pl
from jax.experimental.pallas import tpu as pltpu
from jax.sharding import PartitionSpec as P


def ytable(count, length, weighted):
    modes = jnp.arange(count, dtype=jnp.int32)
    places = jnp.arange(length, dtype=jnp.int32)
    phase = 2.0 * math.pi * (modes[:, None] * places[None, :] % length).astype(jnp.float32) / length
    factor = (
        jnp.where(modes == 0, 1.0, 2.0).astype(jnp.float32)
        if weighted
        else jnp.ones((count,), jnp.float32)
    )
    scale = factor[:, None] / math.sqrt(length)
    return jnp.stack([scale * jnp.cos(phase), -scale * jnp.sin(phase)]).astype(jnp.bfloat16)


def xtable(count, length, places):
    index = jnp.arange(count, dtype=jnp.int32)
    modes = jnp.where(index < count // 2, index, length - count + index)
    phase = 2.0 * math.pi * (modes[:, None] * places[None, :] % length).astype(jnp.float32) / length
    return (jnp.stack([jnp.cos(phase), jnp.sin(phase)]) / math.sqrt(length)).astype(jnp.bfloat16)


def mult(form, left, right):
    return jnp.einsum(form, left, right, preferred_element_type=jnp.float32)


def to_slab(flat, table, planes):
    rows = flat.shape[0]
    count = table.shape[1]
    chans = flat.shape[2] // planes
    coeff = mult("smy,xyq->xsmq", table, flat).astype(jnp.bfloat16)
    coeff = coeff.reshape(rows, 2, count, planes, chans).transpose(0, 2, 3, 1, 4)
    return coeff.reshape(rows, count * planes, 2 * chans)


def from_slab(slab, table, planes):
    rows = slab.shape[0]
    count = table.shape[1]
    chans = slab.shape[2] // 2
    spread = slab.reshape(rows, count, planes, 2, chans)
    return mult("smy,xmpsc->xypc", table, spread).reshape(rows, table.shape[2], planes * chans)


def forward_x(table, pencil):
    proj = mult("ajx,xnsc->ajnsc", table, pencil)
    real_part = proj[0, :, :, 0] + proj[1, :, :, 1]
    imag_part = proj[0, :, :, 1] - proj[1, :, :, 0]
    return jnp.stack([real_part, imag_part], axis=2).astype(jnp.bfloat16)


def inverse_x(table, modes):
    proj = mult("ajx,jnsc->axnsc", table, modes)
    real_part = proj[0, :, :, 0] - proj[1, :, :, 1]
    imag_part = proj[0, :, :, 1] + proj[1, :, :, 0]
    return jnp.stack([real_part, imag_part], axis=2).astype(jnp.bfloat16)


def mix_modes(spectrum, weights):
    real_part = mult("jnc,jnco->jno", spectrum[:, :, 0], weights[:, :, 0]) - mult(
        "jnc,jnco->jno", spectrum[:, :, 1], weights[:, :, 1]
    )
    imag_part = mult("jnc,jnco->jno", spectrum[:, :, 0], weights[:, :, 1]) + mult(
        "jnc,jnco->jno", spectrum[:, :, 1], weights[:, :, 0]
    )
    return jnp.stack([real_part, imag_part], axis=2).astype(jnp.bfloat16)


def adjoint_mix(grads, weights):
    real_part = mult("jnco,jno->jnc", weights[:, :, 0], grads[:, :, 0]) + mult(
        "jnco,jno->jnc", weights[:, :, 1], grads[:, :, 1]
    )
    imag_part = mult("jnco,jno->jnc", weights[:, :, 0], grads[:, :, 1]) - mult(
        "jnco,jno->jnc", weights[:, :, 1], grads[:, :, 0]
    )
    return jnp.stack([real_part, imag_part], axis=2).astype(jnp.bfloat16)


def pair_grad(spectrum, grads):
    real_part = mult("jmpc,jmpo->jmco", spectrum[:, :, :, 0], grads[:, :, :, 0]) + mult(
        "jmpc,jmpo->jmco", spectrum[:, :, :, 1], grads[:, :, :, 1]
    )
    imag_part = mult("jmpc,jmpo->jmco", spectrum[:, :, :, 0], grads[:, :, :, 1]) - mult(
        "jmpc,jmpo->jmco", spectrum[:, :, :, 1], grads[:, :, :, 0]
    )
    return jnp.stack([real_part, imag_part], axis=2)


def to_modes(slab, table_full):
    count = table_full.shape[1]
    pencil = lax.all_to_all(slab, "xy", split_axis=1, concat_axis=0, tiled=True)
    chans = pencil.shape[2] // 2
    items = pencil.shape[1]
    spread = pencil.reshape(pencil.shape[0], items, 2, chans)
    return forward_x(table_full, spread).reshape(count, items, 2 * chans)


def to_space(modes, table_full):
    count, pairs_dev, twice, chans = modes.shape
    pencil = inverse_x(table_full, modes)
    moved = lax.all_to_all(
        pencil.reshape(pencil.shape[0], pairs_dev, 2 * chans),
        "xy",
        split_axis=0,
        concat_axis=1,
        tiled=True,
    )
    return moved


def general_shards(field, spectral_weight, local_weight, bias, cotangent):
    rows, length_y, width_all = field.shape
    chans = local_weight.shape[0]
    planes = width_all // chans
    modes_x, modes_y = (spectral_weight.shape[0], spectral_weight.shape[1])
    devices = lax.axis_size("xy")
    length_x = rows * devices
    pairs_dev = modes_y * planes // devices
    offset = lax.axis_index("xy")
    table_y = ytable(modes_y, length_y, False)
    table_yw = ytable(modes_y, length_y, True)
    table_x = xtable(modes_x, length_x, jnp.arange(length_x, dtype=jnp.int32))
    weight_all = spectral_weight.reshape(modes_x, modes_y, 2, chans, chans)
    ky_index = (offset * pairs_dev + jnp.arange(pairs_dev, dtype=jnp.int32)) // planes
    weight_pairs = jnp.take(weight_all, ky_index, axis=1)
    spectrum = to_modes(to_slab(field, table_y, planes), table_x).reshape(
        modes_x, pairs_dev, 2, chans
    )
    mixed = mix_modes(spectrum, weight_pairs)
    spatial = from_slab(to_space(mixed, table_x), table_yw, planes)
    field4 = field.reshape(rows, length_y, planes, chans)
    local_term = mult("xypc,co->xypo", field4, local_weight)
    preact = spatial.reshape(rows, length_y, planes, chans) + local_term + bias
    output_field = jax.nn.gelu(preact).astype(jnp.bfloat16).reshape(rows, length_y, width_all)
    unused, pullback = jax.vjp(jax.nn.gelu, preact)
    grad_pre = pullback(cotangent.reshape(rows, length_y, planes, chans).astype(jnp.float32))[
        0
    ].astype(jnp.bfloat16)
    bias_part = jnp.sum(grad_pre.astype(jnp.float32), axis=(0, 1, 2))
    weight_part = mult("xypc,xypo->co", field4, grad_pre)
    back_local = mult("xypo,co->xypc", grad_pre, local_weight)
    grad_slab = to_slab(grad_pre.reshape(rows, length_y, width_all), table_yw, planes)
    grad_modes = to_modes(grad_slab, table_x).reshape(modes_x, pairs_dev, 2, chans)
    grad_spec = adjoint_mix(grad_modes, weight_pairs)
    back_spec = from_slab(to_space(grad_spec, table_x), table_y, planes)
    field_grad = (back_spec + back_local.reshape(rows, length_y, width_all)).astype(jnp.bfloat16)
    per_pair = pair_grad(
        spectrum.reshape(modes_x, pairs_dev, 1, 2, chans),
        grad_modes.reshape(modes_x, pairs_dev, 1, 2, chans),
    )
    onehot = (ky_index[:, None] == jnp.arange(modes_y, dtype=jnp.int32)[None, :]).astype(
        jnp.float32
    )
    partial_grad = jnp.einsum("jnsco,nm->jmsco", per_pair, onehot, precision=lax.Precision.HIGHEST)
    total, local_grad, bias_grad = lax.psum((partial_grad, weight_part, bias_part), "xy")
    spectral_grad = total.reshape(modes_x, modes_y, 2 * chans * chans).astype(jnp.bfloat16)
    return (output_field, field_grad, spectral_grad, local_grad, bias_grad)


F32 = jnp.float32
BF16 = jnp.bfloat16
LANES = 128
VMEM_LIMIT = 24 * 1024 * 1024


def dot(left, right):
    return jnp.dot(left, right, preferred_element_type=F32)


def params(**kwargs):
    return pltpu.CompilerParams(vmem_limit_bytes=VMEM_LIMIT, **kwargs)


def cost(flops, bytes_accessed):
    return pl.CostEstimate(flops=flops, bytes_accessed=bytes_accessed, transcendentals=0)


def np_ytable(count, length, weighted):
    modes = np.arange(count)
    places = np.arange(length)
    phase = np.float32(2.0 * math.pi) * (modes[:, None] * places[None, :] % length).astype(np.float32) / np.float32(length)
    factor = np.where(modes == 0, 1.0, 2.0).astype(np.float32) if weighted else np.ones((count,), np.float32)
    scale = (factor / np.float32(math.sqrt(length)))[:, None]
    both = np.stack([scale * np.cos(phase), -scale * np.sin(phase)]).astype(ml_dtypes.bfloat16)
    return both.reshape(2 * count, length)


def np_xtables(count, length):
    index = np.arange(count)
    modes = np.where(index < count // 2, index, length - count + index)
    places = np.arange(length)
    phase = np.float32(2.0 * math.pi) * (modes[:, None] * places[None, :] % length).astype(np.float32) / np.float32(length)
    norm = np.float32(math.sqrt(length))
    cosines = np.cos(phase) / norm
    sines = np.sin(phase) / norm
    forward = np.stack([np.stack([cosines, sines], -1), np.stack([-sines, cosines], -1)])
    forward = forward.reshape(2 * count, 2 * length).astype(ml_dtypes.bfloat16)
    return forward, np.ascontiguousarray(forward.T)


def lane_equals(rows, lanes, divide, offset):
    row = lax.broadcasted_iota(jnp.int32, (rows, lanes), 0)
    lane = lax.broadcasted_iota(jnp.int32, (rows, lanes), 1)
    return jnp.where(row - divide(lane) == offset, 1.0, 0.0).astype(BF16)


def start_all(pairs, sem):
    copies = [pltpu.make_async_copy(src, dst, sem.at[n]) for n, (src, dst) in enumerate(pairs)]
    for copy in copies:
        copy.start()
    return copies


def hbm():
    return pl.BlockSpec(memory_space=pltpu.HBM)


def in_hbm(*arrays):
    return [pltpu.with_memory_space_constraint(a, pltpu.HBM) for a in arrays]


def vmem():
    return pl.BlockSpec(memory_space=pltpu.VMEM)


def smem():
    return pl.BlockSpec(memory_space=pltpu.SMEM)


def scatter_rows(dst, sums, place, chips, half):
    tiles = half // LANES
    for s in range(2):
        for core in range(2):
            where = pl.ds(core * 8 + 2 * place + s, chips, stride=16)
            own = (3 * s + 2 * core) * chips
            shared = (3 * s + 1) * chips
            for k in range(2 * tiles):
                dst[k, where, :] = sums[own : own + chips, k * LANES : (k + 1) * LANES]
            for k in range(tiles):
                at = (core * tiles + k) * LANES
                dst[2 * tiles + k, where, :] = sums[shared : shared + chips, at : at + LANES]


def gather_rows(src, place, chips, half):
    tiles = half // LANES
    out = []
    for s in range(2):
        one = pl.ds(2 * place + s, chips, stride=16)
        two = pl.ds(8 + 2 * place + s, chips, stride=16)
        own = range(2 * tiles)
        shared = range(2 * tiles, 3 * tiles)
        out.append(jnp.concatenate([src[k, one, :] for k in own], axis=1))
        out.append(jnp.concatenate([src[k, w, :] for w in (one, two) for k in shared], axis=1))
        out.append(jnp.concatenate([src[k, two, :] for k in own], axis=1))
    return jnp.concatenate(out, axis=0).astype(BF16)


def cut_lanes(dst, src):
    for k in range(dst.shape[0]):
        dst[k] = src[:, k * LANES : (k + 1) * LANES].astype(F32)


def join_lanes(dst, src):
    for k in range(src.shape[0]):
        dst[:, k * LANES : (k + 1) * LANES] = src[k].astype(BF16)


def cut_shape(shape):
    return (shape[1] // LANES, shape[0], LANES)


def rows_to_modes(field, table, chips, half):
    rows, length, width = field.shape
    shape = (chips * 16, 3 * half)

    def kernel(u_hbm, t_hbm, out_hbm, u_ref, t_ref, scr, out_ref, sem, out_sem):
        copies = start_all([(t_hbm, t_ref)] + [(u_hbm.at[x], u_ref.at[x]) for x in range(rows)], sem)
        copies[0].wait()
        for x in range(rows):
            copies[1 + x].wait()
            scatter_rows(scr, dot(t_ref[...], u_ref[x]), x, chips, half)
        join_lanes(out_ref, scr)
        copy = pltpu.make_async_copy(out_ref, out_hbm, out_sem)
        copy.start()
        copy.wait()

    return pl.pallas_call(
        kernel,
        in_specs=[hbm(), hbm()],
        out_specs=hbm(),
        out_shape=pltpu.HBM(shape, BF16),
        scratch_shapes=[
            pltpu.VMEM(field.shape, BF16),
            pltpu.VMEM(table.shape, BF16),
            pltpu.VMEM(cut_shape(shape), F32),
            pltpu.VMEM(shape, BF16),
            pltpu.SemaphoreType.DMA((1 + rows,)),
            pltpu.SemaphoreType.DMA,
        ],
        compiler_params=params(),
        cost_estimate=cost(2 * table.size * rows * width, field.size * 2),
        name="rows_to_modes",
    )(*in_hbm(field, table))


def prepare(me, weights, local_weight, bias, chips, half):
    modes_x, modes_y, full2 = weights.shape
    chans = local_weight.shape[0]
    tiles = full2 // LANES
    rows = 4 * modes_x
    groups = full2 // 2 // LANES
    batch = 6

    def kernel(
        me_ref, w_hbm, l_ref, b_ref, plain_hbm, turned_hbm, block_hbm, block_t_hbm, bias_hbm,
        w_ref, scr, pick, one, two, plain_ref, turned_ref, block_ref, block_t_ref, bias_ref, sem, out_sem,
    ):
        cuts = [pl.ds(j, batch) for j in range(0, modes_x, batch)]
        copies = start_all([(w_hbm.at[cut], w_ref.at[cut]) for cut in cuts], sem)

        spread = lane_equals(chans, half, lambda l: l % chans, 0)
        row = lax.broadcasted_iota(jnp.int32, (half, half), 0) // chans
        lane = lax.broadcasted_iota(jnp.int32, (half, half), 1) // chans
        local = l_ref[...]
        for ref, dims in ((block_ref, 1), (block_t_ref, 0)):
            wide = lax.dot_general(local, spread, (((dims,), (0,)), ((), ())), preferred_element_type=F32)
            wide = jnp.concatenate([wide] * (half // chans), axis=0)
            ref[...] = jnp.where(row == lane, wide, 0.0).astype(BF16)
        value = jnp.concatenate([b_ref[...]] * 8, axis=0)
        high = value.astype(BF16)
        mid = (value - high.astype(F32)).astype(BF16)
        low = (value - high.astype(F32) - mid.astype(F32)).astype(BF16)
        wide = dot(high, spread) + dot(mid, spread) + dot(low, spread)
        bias_ref[...] = jnp.concatenate([wide, wide], axis=1)
        out_copies = start_all(
            [(block_ref, block_hbm), (block_t_ref, block_t_hbm), (bias_ref, bias_hbm)], out_sem
        )

        for n, first in enumerate(range(0, modes_x, batch)):
            copies[n].wait()
            for j in range(first, first + batch):
                for k in range(tiles):
                    scr[k, j * modes_y : (j + 1) * modes_y, :] = w_ref[j, :, k * LANES : (k + 1) * LANES].astype(F32)
        chip, core = me_ref[0] // 2, me_ref[0] % 2
        for w, mode in enumerate((chip + 2 * chips * core, chip + chips)):
            for k in range(tiles):
                s, g = divmod(k, groups)
                base = (2 * w + s) * modes_x
                pick[g, base : base + modes_x, :] = scr[k, pl.ds(mode, modes_x, stride=modes_y), :]
        per = LANES // chans
        repeat = jnp.concatenate(
            [lane_equals(LANES, LANES, lambda l: l % chans, chans * g) for g in range(per)], axis=1
        )
        pad = jnp.zeros((LANES - rows, LANES), F32)
        for g in range(groups):
            plain_ref[g] = dot(pick[g].astype(BF16), repeat).astype(BF16)
            one[g * LANES : (g + 1) * LANES, :] = jnp.transpose(jnp.concatenate([pick[g], pad]))
        out_copies.append(pltpu.make_async_copy(plain_ref, plain_hbm, out_sem.at[3]))
        out_copies[-1].start()
        for b in range(chans):
            two[b * chans : (b + 1) * chans, :] = one[pl.ds(b, chans, stride=chans), :]
        for g in range(groups):
            part = jnp.transpose(two[g * LANES : (g + 1) * LANES, :])[0:rows]
            turned_ref[g] = dot(part.astype(BF16), repeat).astype(BF16)
        out_copies.append(pltpu.make_async_copy(turned_ref, turned_hbm, out_sem.at[4]))
        out_copies[-1].start()
        for copy in out_copies:
            copy.wait()

    shape = (groups, rows, LANES * LANES // chans)
    wide = pltpu.HBM(shape, BF16)
    block = pltpu.HBM((half, half), BF16)
    return pl.pallas_call(
        kernel,
        in_specs=[smem(), hbm(), vmem(), vmem()],
        out_specs=(hbm(),) * 5,
        out_shape=(wide, wide, block, block, pltpu.HBM((8, 2 * half), F32)),
        scratch_shapes=[
            pltpu.VMEM(weights.shape, BF16),
            pltpu.VMEM((tiles, modes_x * modes_y, LANES), F32),
            pltpu.VMEM((groups, rows, LANES), F32),
            pltpu.VMEM((full2 // 2, LANES), F32),
            pltpu.VMEM((full2 // 2, LANES), F32),
            pltpu.VMEM(shape, BF16),
            pltpu.VMEM(shape, BF16),
            pltpu.VMEM((half, half), BF16),
            pltpu.VMEM((half, half), BF16),
            pltpu.VMEM((8, 2 * half), F32),
            pltpu.SemaphoreType.DMA((modes_x // batch,)),
            pltpu.SemaphoreType.DMA((5,)),
        ],
        compiler_params=params(),
        cost_estimate=cost(1000000, 4 * 1024 * 1024),
        name="prepare",
    )(me, *in_hbm(weights), local_weight, bias)


def weigh(spec, w_ref, chans, modes_x, adjoint):
    tiles = spec.shape[1] // LANES
    groups = LANES // chans
    stack = jnp.concatenate([spec[:, k * LANES : (k + 1) * LANES] for k in range(tiles)], axis=0)
    real = [None] * tiles
    imag = [None] * tiles
    for pair in range(chans // 2):
        two = [lane_equals(LANES, LANES, lambda l: l // chans * chans, c) for c in (2 * pair, 2 * pair + 1)]
        wide_rows = dot(stack, jnp.concatenate(two, axis=1))
        for c in (2 * pair, 2 * pair + 1):
            lanes = slice((c % 2) * LANES, (c % 2 + 1) * LANES)
            wl = slice((c % groups) * LANES, (c % groups + 1) * LANES)
            for own in range(2):
                base = 2 * own * modes_x
                wr = w_ref[c // groups, base : base + modes_x, wl].astype(F32)
                wi = w_ref[c // groups, base + modes_x : base + 2 * modes_x, wl].astype(F32)
                for k in range(0, 2 * tiles // 3) if own == 0 else range(2 * tiles // 3, tiles):
                    xr = wide_rows[2 * k * modes_x : (2 * k + 1) * modes_x, lanes]
                    xi = wide_rows[(2 * k + 1) * modes_x : (2 * k + 2) * modes_x, lanes]
                    if adjoint:
                        r, i = xr * wr + xi * wi, xi * wr - xr * wi
                    else:
                        r, i = xr * wr - xi * wi, xr * wi + xi * wr
                    real[k] = r if real[k] is None else real[k] + r
                    imag[k] = i if imag[k] is None else imag[k] + i
    return jnp.concatenate([jnp.concatenate(real, axis=1), jnp.concatenate(imag, axis=1)], axis=0).astype(BF16)


def mode_step(pencil, spread_w, forward, inverse, chans, adjoint):
    modes_x = forward.shape[0] // 2

    def kernel(p_ref, w_hbm, f_hbm, i_hbm, spec_ref, out_hbm, w_ref, f_ref, i_ref, out_ref, sem, out_sem):
        copies = start_all([(f_hbm, f_ref), (w_hbm, w_ref), (i_hbm, i_ref)], sem)
        copies[0].wait()
        spec = dot(f_ref[...], p_ref[...]).astype(BF16)
        spec_ref[...] = spec
        copies[1].wait()
        copies[2].wait()
        mixed = weigh(spec, w_ref, chans, modes_x, adjoint)
        out_ref[...] = dot(i_ref[...], mixed).astype(BF16)
        copy = pltpu.make_async_copy(out_ref, out_hbm, out_sem)
        copy.start()
        copy.wait()

    return pl.pallas_call(
        kernel,
        in_specs=[vmem()] + [hbm()] * 3,
        out_specs=(vmem(), hbm()),
        out_shape=(
            jax.ShapeDtypeStruct((2 * modes_x, pencil.shape[1]), BF16),
            pltpu.HBM(pencil.shape, BF16),
        ),
        scratch_shapes=[
            pltpu.VMEM(spread_w.shape, BF16),
            pltpu.VMEM(forward.shape, BF16),
            pltpu.VMEM(inverse.shape, BF16),
            pltpu.VMEM(pencil.shape, BF16),
            pltpu.SemaphoreType.DMA((3,)),
            pltpu.SemaphoreType.DMA,
        ],
        compiler_params=params(),
        cost_estimate=cost(2 * 48 * 6 * 128 * 4096, spread_w.size * 4),
        name="adjoint_step" if adjoint else "mode_step",
    )(pencil, *in_hbm(spread_w, forward, inverse))


def pointwise(field, cotangent, pencil, table_t, table, block_weight, bias_row, chips, half):
    rows, length, width = field.shape
    chunk = 64

    def kernel(
        u_hbm, c_hbm, p_ref, tt_hbm, t_hbm, w_hbm, b_hbm, out_hbm, dpre_hbm, send_hbm,
        u_ref, c_ref, tt_ref, t_ref, w_ref, b_ref, out_ref, dpre_ref, send_ref, bscr, dscr, sem, out_sem,
    ):
        copies = start_all([(tt_hbm, tt_ref), (w_hbm, w_ref), (b_hbm, b_ref), (t_hbm, t_ref)], sem)
        for x in range(rows):
            pltpu.make_async_copy(u_hbm.at[x], u_ref.at[x], sem.at[5 + x]).start()
            pltpu.make_async_copy(c_hbm.at[x], c_ref.at[x], sem.at[5 + rows + x]).start()
        for copy in copies:
            copy.wait()
        cut_lanes(bscr, p_ref)
        root = math.sqrt(2.0 / math.pi)

        def one_row(x):
            pltpu.make_async_copy(u_hbm.at[x], u_ref.at[x], sem.at[5 + x]).wait()
            pltpu.make_async_copy(c_hbm.at[x], c_ref.at[x], sem.at[5 + rows + x]).wait()
            bias = b_ref[0:1, :]
            coeff = gather_rows(bscr, x, chips, half)
            for k in range(length // chunk):
                where = pl.ds(k * chunk, chunk)
                u = u_ref[x, where, :]
                spec = dot(tt_ref[where, :], coeff)
                for h in range(2):
                    lanes = slice(h * half, (h + 1) * half)
                    pre = spec[:, lanes] + dot(u[:, lanes], w_ref[...]) + bias[:, lanes]
                    inner = pre * (root + (root * 0.044715) * (pre * pre))
                    th = jnp.tanh(inner)
                    cdf = 0.5 * th + 0.5
                    out_ref[x, where, lanes] = (pre * cdf).astype(BF16)
                    slope = 6.0 * inner - (4.0 * root) * pre
                    grad = cdf + (cdf - cdf * cdf) * slope
                    dpre_ref[x, where, lanes] = (c_ref[x, where, lanes].astype(F32) * grad).astype(BF16)
            pltpu.make_async_copy(out_ref.at[x], out_hbm.at[x], out_sem.at[x]).start()
            pltpu.make_async_copy(dpre_ref.at[x], dpre_hbm.at[x], out_sem.at[rows + x]).start()
            scatter_rows(dscr, dot(t_ref[...], dpre_ref[x]), x, chips, half)

        pl.loop(0, rows)(one_row)
        join_lanes(send_ref, dscr)
        pltpu.make_async_copy(send_ref, send_hbm, out_sem.at[2 * rows]).start()
        for x in range(rows):
            pltpu.make_async_copy(out_ref.at[x], out_hbm.at[x], out_sem.at[x]).wait()
            pltpu.make_async_copy(dpre_ref.at[x], dpre_hbm.at[x], out_sem.at[rows + x]).wait()
        pltpu.make_async_copy(send_ref, send_hbm, out_sem.at[2 * rows]).wait()

    return pl.pallas_call(
        kernel,
        in_specs=[hbm(), hbm(), vmem()] + [hbm()] * 4,
        out_specs=(hbm(), hbm(), hbm()),
        out_shape=(
            pltpu.HBM(field.shape, BF16),
            pltpu.HBM(field.shape, BF16),
            pltpu.HBM(pencil.shape, BF16),
        ),
        scratch_shapes=[
            pltpu.VMEM(field.shape, BF16),
            pltpu.VMEM(field.shape, BF16),
            pltpu.VMEM(table_t.shape, BF16),
            pltpu.VMEM(table.shape, BF16),
            pltpu.VMEM(block_weight.shape, BF16),
            pltpu.VMEM(bias_row.shape, F32),
            pltpu.VMEM(field.shape, BF16),
            pltpu.VMEM(field.shape, BF16),
            pltpu.VMEM(pencil.shape, BF16),
            pltpu.VMEM(cut_shape(pencil.shape), F32),
            pltpu.VMEM(cut_shape(pencil.shape), F32),
            pltpu.SemaphoreType.DMA((5 + 2 * rows,)),
            pltpu.SemaphoreType.DMA((2 * rows + 1,)),
        ],
        compiler_params=params(),
        cost_estimate=cost(field.size * 1000, field.size * 8),
        name="pointwise",
    )(*in_hbm(field, cotangent), pencil, *in_hbm(table_t, table, block_weight, bias_row))


def local_sums(field, dpre, chans, half):
    rows, length, width = field.shape
    slices = half // chans

    def kernel(u_hbm, d_hbm, out_ref, u_ref, d_ref, sem):
        copies = start_all(
            [(u_hbm.at[x], u_ref.at[x]) for x in range(rows)] + [(d_hbm.at[x], d_ref.at[x]) for x in range(rows)], sem
        )
        both = bias = None
        ones = jnp.ones((16, length), BF16)
        for x in range(rows):
            copies[x].wait()
            copies[rows + x].wait()
            for h in range(2):
                lanes = slice(h * half, (h + 1) * half)
                part = lax.dot_general(
                    u_ref[x, :, lanes], d_ref[x, :, lanes], (((0,), (0,)), ((), ())), preferred_element_type=F32
                )
                both = part if both is None else both + part
            part = dot(ones, d_ref[x])[0:8]
            bias = part if bias is None else bias + part
        group = lax.broadcasted_iota(jnp.int32, (chans, half), 1) // chans
        total = jnp.zeros((chans, half), F32)
        for p in range(slices):
            total = jnp.where(group == p, both[p * chans : (p + 1) * chans], total)
        total = sum(total[:, k * LANES : (k + 1) * LANES] for k in range(half // LANES))
        bias = sum(bias[:, k * LANES : (k + 1) * LANES] for k in range(width // LANES))
        shift = LANES // 2
        while shift >= chans:
            total = total + pltpu.roll(total, shift, 1)
            bias = bias + pltpu.roll(bias, shift, 1)
            shift //= 2
        group8 = lax.broadcasted_iota(jnp.int32, (8, LANES), 1) // chans
        folded = jnp.zeros((8, LANES), F32)
        for k in range(chans // 8):
            folded = jnp.where(group8 == k, total[8 * k : 8 * k + 8], folded)
        value = jnp.concatenate([folded, bias], axis=0)
        high = value.astype(BF16).astype(F32)
        mid = (value - high).astype(BF16).astype(F32)
        low = value - high - mid
        left = jnp.concatenate([high, mid[0:8]], axis=0)
        right = jnp.concatenate([mid[8:16], low], axis=0)
        out_ref[...] = jnp.concatenate([left, right], axis=1).astype(BF16)

    return pl.pallas_call(
        kernel,
        in_specs=[hbm(), hbm()],
        out_specs=vmem(),
        out_shape=jax.ShapeDtypeStruct((24, 2 * LANES), BF16),
        scratch_shapes=[
            pltpu.VMEM(field.shape, BF16),
            pltpu.VMEM(field.shape, BF16),
            pltpu.SemaphoreType.DMA((2 * rows,)),
        ],
        compiler_params=params(),
        cost_estimate=cost(field.size * 1000, field.size * 4),
        name="local_sums",
    )(*in_hbm(field, dpre))


def weight_sums(me, spectrum, grads, chans):
    modes_x = spectrum.shape[0] // 2
    tiles = spectrum.shape[1] // LANES
    groups = LANES // chans
    step = 2 * LANES
    full = chans * chans
    parts = full // step

    def kernel(me_ref, u_ref, d_ref, own_ref, keep_ref, send_ref):
        def stack(ref):
            return jnp.concatenate([ref[:, k * LANES : (k + 1) * LANES] for k in range(tiles)], axis=0)

        first = me_ref[0] % 2 == 0
        left = stack(u_ref)
        repeat = jnp.concatenate(
            [lane_equals(LANES, LANES, lambda l: l % chans, chans * g) for g in range(groups)], axis=1
        )
        right = dot(stack(d_ref), repeat)
        for a in range(parts):
            sums = {}
            for g in range(groups):
                pick = lane_equals(LANES, step, lambda l: l // chans, g * chans + a * (step // chans))
                spread_u = dot(left, pick)
                for k in range(tiles):
                    kind = 0 if k < 2 * tiles // 3 else 1
                    re = slice(2 * k * modes_x, (2 * k + 1) * modes_x)
                    im = slice((2 * k + 1) * modes_x, (2 * k + 2) * modes_x)
                    for z in range(2):
                        lanes = slice(z * LANES, (z + 1) * LANES)
                        ur, ui = spread_u[re, lanes], spread_u[im, lanes]
                        dr = right[re, g * LANES : (g + 1) * LANES]
                        di = right[im, g * LANES : (g + 1) * LANES]
                        for t, term in ((0, ur * dr + ui * di), (1, ur * di - ui * dr)):
                            key = (kind, t, z)
                            sums[key] = term if key not in sums else sums[key] + term
            for t in range(2):
                own = jnp.concatenate([sums[0, t, 0], sums[0, t, 1]], axis=1)
                own_ref[:, t * full + a * step : t * full + (a + 1) * step] = own.astype(BF16)
                shared = jnp.concatenate([sums[1, t, 0], sums[1, t, 1]], axis=1)
                at = t * (full // 2) + (a % (parts // 2)) * step
                low = a < parts // 2

                @pl.when(first if low else jnp.logical_not(first))
                def _():
                    keep_ref[:, at : at + step] = shared

                @pl.when(jnp.logical_not(first) if low else first)
                def _():
                    send_ref[:, at : at + step] = shared

    half_shape = jax.ShapeDtypeStruct((modes_x, full), F32)
    return pl.pallas_call(
        kernel,
        in_specs=[smem(), vmem(), vmem()],
        out_shape=(jax.ShapeDtypeStruct((modes_x, 2 * full), BF16), half_shape, half_shape),
        compiler_params=params(),
        cost_estimate=cost(2 * 288 * 128 * 4096, 4 * 1024 * 1024),
        name="weight_sums",
    )(me, spectrum, grads)


def make_shard(own, keep, other, stats):
    rows, full2 = own.shape
    full = keep.shape[1]
    width = full2 + full + stats.shape[1]

    def kernel(o_ref, k_ref, r_ref, s_ref, out_ref):
        out_ref[:, 0:full2] = o_ref[...]
        out_ref[:, full2 : full2 + full] = (k_ref[...] + r_ref[...]).astype(BF16)
        out_ref[:, full2 + full :] = s_ref[...]

    return pl.pallas_call(
        kernel,
        out_shape=jax.ShapeDtypeStruct((rows, width), BF16),
        compiler_params=params(),
        name="make_shard",
    )(own, keep, other, stats)


def ring_chip(spot, chips):
    return jnp.where(spot < chips // 2, 2 * spot, 2 * (chips - 1 - spot) + 1)


def ring_spot(chip, chips):
    return jnp.where(chip % 2 == 0, chip // 2, chips - 1 - chip // 2)


def assemble(me, shards_all, turns, modes_y, chans, chips):
    rows = shards_all[0].shape[0]
    full = chans * chans
    count = len(shards_all)
    step = 2 * LANES
    blocks = 2 * full // LANES

    def kernel(me_ref, *refs):
        ins, (g_ref, l_ref, b_ref, scr, stat, out, sem) = refs[:count], refs[count:]
        spot = ring_spot(me_ref[0] // 2, chips)
        places = []
        for back, swapped in turns:
            chip = ring_chip((spot + chips - back) % chips, chips)
            core = me_ref[0] % 2
            places.append((chip, 1 - core if swapped else core))
        copies = []
        for k in range(blocks):
            for n in range(count):
                chip, core = places[n]
                own = pl.ds(chip + 2 * chips * core, rows, stride=modes_y)
                scr[k, own, :] = ins[n][:, k * LANES : (k + 1) * LANES].astype(F32)
            part = k % (blocks // 2)
            from_core = part // (blocks // 4)
            at = 2 * full + (k // (blocks // 2)) * (full // 2) + (part % (blocks // 4)) * LANES
            for n in range(count):
                if turns[n][1]:
                    continue
                chip, core = places[n]
                mate = turns.index((turns[n][0], True))
                here = ins[n][:, at : at + LANES].astype(F32)
                there = ins[mate][:, at : at + LANES].astype(F32)
                where = pl.ds(chip + chips, rows, stride=modes_y)
                scr[k, where, :] = jnp.where(core == from_core, here, there)
            lanes = slice(k * LANES, (k + 1) * LANES)
            for j in range(rows):
                out[j, :, lanes] = scr[k, j * modes_y : (j + 1) * modes_y, :].astype(BF16)
            if k % 4 == 3:
                lanes = pl.ds((k - 3) * LANES, 4 * LANES)
                copies.append(pltpu.make_async_copy(out.at[:, :, lanes], g_ref.at[:, :, lanes], sem.at[k // 4]))
                copies[-1].start()
        for n in range(count):
            chip, core = places[n]
            left = ins[n][:, 3 * full : 3 * full + LANES].astype(F32)
            right = ins[n][:, 3 * full + LANES :].astype(F32)
            middle = jnp.concatenate([left[16:24], right[0:8]], axis=0)
            stat[2 * chip + core] = left[0:16] + middle + right[8:24]
        total = stat[0]
        for n in range(1, count):
            total = total + stat[n]
        for k in range(chans // 8):
            piece = total[0:8] if k == 0 else pltpu.roll(total[0:8], LANES - k * chans, 1)
            l_ref[8 * k : 8 * k + 8, :] = piece[:, 0:chans]
        b_ref[...] = total[8:9, 0:chans]
        for copy in copies:
            copy.wait()

    vmem = pl.BlockSpec(memory_space=pltpu.VMEM)
    shape = (rows, modes_y, 2 * full)
    return pl.pallas_call(
        kernel,
        in_specs=[pl.BlockSpec(memory_space=pltpu.SMEM)] + [vmem] * count,
        out_specs=(pl.BlockSpec(memory_space=pl.ANY), vmem, vmem),
        out_shape=(
            jax.ShapeDtypeStruct(shape, BF16),
            jax.ShapeDtypeStruct((chans, chans), F32),
            jax.ShapeDtypeStruct((1, chans), F32),
        ),
        scratch_shapes=[
            pltpu.VMEM((blocks, rows * modes_y, LANES), F32),
            pltpu.VMEM((count, 16, LANES), F32),
            pltpu.VMEM(shape, BF16),
            pltpu.SemaphoreType.DMA((blocks // 4,)),
        ],
        compiler_params=params(),
        cost_estimate=cost(1000000, 8 * 1024 * 1024),
        name="assemble",
    )(me, *shards_all)


def back_to_field(dpre, pencil, table_t, block_weight, chips, half):
    rows, length, width = dpre.shape
    chunk = 128

    def kernel(d_hbm, p_ref, tt_hbm, w_hbm, out_hbm, d_ref, tt_ref, w_ref, out_ref, bscr, sem, out_sem):
        copies = start_all(
            [(tt_hbm, tt_ref), (w_hbm, w_ref)] + [(d_hbm.at[x], d_ref.at[x]) for x in range(rows)], sem
        )
        for copy in copies[0:2]:
            copy.wait()
        cut_lanes(bscr, p_ref)
        out_copies = []
        for x in range(rows):
            copies[2 + x].wait()
            coeff = gather_rows(bscr, x, chips, half)
            for k in range(length // chunk):
                where = pl.ds(k * chunk, chunk)
                d = d_ref[x, where, :]
                spec = dot(tt_ref[where, :], coeff)
                for h in range(2):
                    lanes = slice(h * half, (h + 1) * half)
                    out_ref[x, where, lanes] = (spec[:, lanes] + dot(d[:, lanes], w_ref[...])).astype(BF16)
            out_copies.append(pltpu.make_async_copy(out_ref.at[x], out_hbm.at[x], out_sem.at[x]))
            out_copies[-1].start()
        for copy in out_copies:
            copy.wait()

    return pl.pallas_call(
        kernel,
        in_specs=[hbm(), vmem(), hbm(), hbm()],
        out_specs=hbm(),
        out_shape=pltpu.HBM(dpre.shape, BF16),
        scratch_shapes=[
            pltpu.VMEM(dpre.shape, BF16),
            pltpu.VMEM(table_t.shape, BF16),
            pltpu.VMEM(block_weight.shape, BF16),
            pltpu.VMEM(dpre.shape, BF16),
            pltpu.VMEM(cut_shape(pencil.shape), F32),
            pltpu.SemaphoreType.DMA((2 + rows,)),
            pltpu.SemaphoreType.DMA((rows,)),
        ],
        compiler_params=params(),
        cost_estimate=cost(dpre.size * 500, dpre.size * 4),
        name="back_to_field",
    )(*in_hbm(dpre), pencil, *in_hbm(table_t, block_weight))


def exchange(pencil):
    return lax.all_to_all(pencil, "xy", split_axis=0, concat_axis=0, tiled=True)


class Ring:
    def __init__(self, shard, chips):
        order = [ring_chip_int(i, chips) for i in range(chips)]
        self.chips = chips
        self.hops = {
            way: [(2 * order[i] + c, 2 * order[(i + way) % chips] + c) for i in range(chips) for c in range(2)]
            for way in (1, -1)
        }
        self.swap = [(i, i ^ 1) for i in range(2 * chips)]
        self.step = 0
        self.ahead = self.back = shard
        self.parts, self.turns = [], []
        self.keep(shard, 0)

    def keep(self, piece, turn):
        self.parts.append(piece)
        self.turns.append((turn, False))
        self.parts.append(lax.ppermute(piece, "xy", self.swap))
        self.turns.append((turn, True))

    def hop(self):
        self.step += 1
        self.ahead = lax.ppermute(self.ahead, "xy", self.hops[1])
        if self.step < self.chips // 2:
            self.back = lax.ppermute(self.back, "xy", self.hops[-1])

    def settle(self):
        self.keep(self.ahead, self.step)
        if self.step < self.chips // 2:
            self.keep(self.back, self.chips - self.step)

    def tie(self, other):
        self.ahead, self.back, other = lax.optimization_barrier((self.ahead, self.back, other))
        return other

    def hold(self, other):
        self.ahead, other = lax.optimization_barrier((self.ahead, other))
        return other


def ring_chip_int(spot, chips):
    return 2 * spot if spot < chips // 2 else 2 * (chips - 1 - spot) + 1


def fast_shards(field, spectral_weight, local_weight, bias, cotangent):
    rows, length_y, width = field.shape
    chans = local_weight.shape[0]
    planes = width // chans
    modes_x, modes_y = spectral_weight.shape[:2]
    devices = lax.axis_size("xy")
    chips = devices // 2
    half = width // 2
    me = lax.axis_index("xy")
    table_y = np_ytable(modes_y, length_y, False)
    table_yw = np_ytable(modes_y, length_y, True)
    table_y_t, table_yw_t = (np.ascontiguousarray(t.T) for t in (table_y, table_yw))
    forward, inverse = np_xtables(modes_x, rows * devices)
    me_id = me.astype(jnp.int32)[None]

    send = rows_to_modes(field, table_y, chips, half)
    pencil = exchange(send)
    plain, turned, block, block_t, bias_row = prepare(
        me_id, spectral_weight, local_weight, bias[None, :], chips, half
    )
    spectrum, send = mode_step(pencil, plain, forward, inverse, chans, False)
    pencil = exchange(send)
    output_field, dpre, send = pointwise(
        field, cotangent, pencil, table_yw_t, table_yw, block, bias_row, chips, half
    )
    pencil = exchange(send)
    stats = local_sums(field, dpre, chans, half)
    pencil, stats = lax.optimization_barrier((pencil, stats))
    grads, send = mode_step(pencil, turned, forward, inverse, chans, True)
    pencil = exchange(send)
    own, keep, give = weight_sums(me_id, spectrum, grads, chans)
    got = lax.ppermute(give, "xy", [(i, i ^ 1) for i in range(devices)])
    shard = make_shard(own, keep, got, stats)

    ring = Ring(shard, chips)
    ring.hop()
    pencil = ring.tie(pencil)
    ring.settle()
    ring.hop()
    field_grad = back_to_field(dpre, pencil, table_y_t, block_t, chips, half)
    field_grad = ring.tie(field_grad)
    ring.settle()
    ring.hop()
    ring.settle()
    ring.hop()
    ring.settle()
    parts, turns = ring.parts, ring.turns
    spectral_grad, local_grad, bias_grad = assemble(me_id, parts, turns, modes_y, chans, chips)
    return output_field, field_grad, spectral_grad, local_grad, bias_grad.reshape(chans)


def fits(field, spectral_weight, local_weight, devices):
    rows, length_y, width = field.shape
    chans = local_weight.shape[0]
    modes_x, modes_y = spectral_weight.shape[:2]
    return (
        rows == 4
        and chans == 32
        and width == 512
        and length_y % 128 == 0
        and modes_x == 24
        and devices == 16
        and 2 * modes_y == 3 * devices
    )


def shards(field, spectral_weight, local_weight, bias, cotangent):
    if fits(field, spectral_weight, local_weight, lax.axis_size("xy")):
        return fast_shards(field, spectral_weight, local_weight, bias, cotangent)
    return general_shards(field, spectral_weight, local_weight, bias, cotangent)


def solution(mesh):
    return jax.shard_map(
        shards,
        mesh=mesh,
        in_specs=(P(("groups", "xy"), None, None), P(), P(), P(), P(("groups", "xy"), None, None)),
        out_specs=(
            P(("groups", "xy"), None, None),
            P(("groups", "xy"), None, None),
            P("groups", None, None),
            P("groups", None),
            P("groups"),
        ),
        check_vma=False,
    )
```

```python
import math

import jax
import jax.numpy as jnp
import ml_dtypes
import numpy as np
from jax import lax
from jax.experimental import pallas as pl
from jax.experimental.pallas import tpu as pltpu
from jax.sharding import PartitionSpec as P


def ytable(count, length, weighted):
    modes = jnp.arange(count, dtype=jnp.int32)
    places = jnp.arange(length, dtype=jnp.int32)
    phase = 2.0 * math.pi * (modes[:, None] * places[None, :] % length).astype(jnp.float32) / length
    factor = (
        jnp.where(modes == 0, 1.0, 2.0).astype(jnp.float32)
        if weighted
        else jnp.ones((count,), jnp.float32)
    )
    scale = factor[:, None] / math.sqrt(length)
    return jnp.stack([scale * jnp.cos(phase), -scale * jnp.sin(phase)]).astype(jnp.bfloat16)


def xtable(count, length, places):
    index = jnp.arange(count, dtype=jnp.int32)
    modes = jnp.where(index < count // 2, index, length - count + index)
    phase = 2.0 * math.pi * (modes[:, None] * places[None, :] % length).astype(jnp.float32) / length
    return (jnp.stack([jnp.cos(phase), jnp.sin(phase)]) / math.sqrt(length)).astype(jnp.bfloat16)


def mult(form, left, right):
    return jnp.einsum(form, left, right, preferred_element_type=jnp.float32)


def to_slab(flat, table, planes):
    rows = flat.shape[0]
    count = table.shape[1]
    chans = flat.shape[2] // planes
    coeff = mult("smy,xyq->xsmq", table, flat).astype(jnp.bfloat16)
    coeff = coeff.reshape(rows, 2, count, planes, chans).transpose(0, 2, 3, 1, 4)
    return coeff.reshape(rows, count * planes, 2 * chans)


def from_slab(slab, table, planes):
    rows = slab.shape[0]
    count = table.shape[1]
    chans = slab.shape[2] // 2
    spread = slab.reshape(rows, count, planes, 2, chans)
    return mult("smy,xmpsc->xypc", table, spread).reshape(rows, table.shape[2], planes * chans)


def forward_x(table, pencil):
    proj = mult("ajx,xnsc->ajnsc", table, pencil)
    real_part = proj[0, :, :, 0] + proj[1, :, :, 1]
    imag_part = proj[0, :, :, 1] - proj[1, :, :, 0]
    return jnp.stack([real_part, imag_part], axis=2).astype(jnp.bfloat16)


def inverse_x(table, modes):
    proj = mult("ajx,jnsc->axnsc", table, modes)
    real_part = proj[0, :, :, 0] - proj[1, :, :, 1]
    imag_part = proj[0, :, :, 1] + proj[1, :, :, 0]
    return jnp.stack([real_part, imag_part], axis=2).astype(jnp.bfloat16)


def mix_modes(spectrum, weights):
    real_part = mult("jnc,jnco->jno", spectrum[:, :, 0], weights[:, :, 0]) - mult(
        "jnc,jnco->jno", spectrum[:, :, 1], weights[:, :, 1]
    )
    imag_part = mult("jnc,jnco->jno", spectrum[:, :, 0], weights[:, :, 1]) + mult(
        "jnc,jnco->jno", spectrum[:, :, 1], weights[:, :, 0]
    )
    return jnp.stack([real_part, imag_part], axis=2).astype(jnp.bfloat16)


def adjoint_mix(grads, weights):
    real_part = mult("jnco,jno->jnc", weights[:, :, 0], grads[:, :, 0]) + mult(
        "jnco,jno->jnc", weights[:, :, 1], grads[:, :, 1]
    )
    imag_part = mult("jnco,jno->jnc", weights[:, :, 0], grads[:, :, 1]) - mult(
        "jnco,jno->jnc", weights[:, :, 1], grads[:, :, 0]
    )
    return jnp.stack([real_part, imag_part], axis=2).astype(jnp.bfloat16)


def pair_grad(spectrum, grads):
    real_part = mult("jmpc,jmpo->jmco", spectrum[:, :, :, 0], grads[:, :, :, 0]) + mult(
        "jmpc,jmpo->jmco", spectrum[:, :, :, 1], grads[:, :, :, 1]
    )
    imag_part = mult("jmpc,jmpo->jmco", spectrum[:, :, :, 0], grads[:, :, :, 1]) - mult(
        "jmpc,jmpo->jmco", spectrum[:, :, :, 1], grads[:, :, :, 0]
    )
    return jnp.stack([real_part, imag_part], axis=2)


def to_modes(slab, table_full):
    count = table_full.shape[1]
    pencil = lax.all_to_all(slab, "xy", split_axis=1, concat_axis=0, tiled=True)
    chans = pencil.shape[2] // 2
    items = pencil.shape[1]
    spread = pencil.reshape(pencil.shape[0], items, 2, chans)
    return forward_x(table_full, spread).reshape(count, items, 2 * chans)


def to_space(modes, table_full):
    count, pairs_dev, twice, chans = modes.shape
    pencil = inverse_x(table_full, modes)
    moved = lax.all_to_all(
        pencil.reshape(pencil.shape[0], pairs_dev, 2 * chans),
        "xy",
        split_axis=0,
        concat_axis=1,
        tiled=True,
    )
    return moved


def general_shards(field, spectral_weight, local_weight, bias, cotangent):
    rows, length_y, width_all = field.shape
    chans = local_weight.shape[0]
    planes = width_all // chans
    modes_x, modes_y = (spectral_weight.shape[0], spectral_weight.shape[1])
    devices = lax.axis_size("xy")
    length_x = rows * devices
    pairs_dev = modes_y * planes // devices
    offset = lax.axis_index("xy")
    table_y = ytable(modes_y, length_y, False)
    table_yw = ytable(modes_y, length_y, True)
    table_x = xtable(modes_x, length_x, jnp.arange(length_x, dtype=jnp.int32))
    weight_all = spectral_weight.reshape(modes_x, modes_y, 2, chans, chans)
    ky_index = (offset * pairs_dev + jnp.arange(pairs_dev, dtype=jnp.int32)) // planes
    weight_pairs = jnp.take(weight_all, ky_index, axis=1)
    spectrum = to_modes(to_slab(field, table_y, planes), table_x).reshape(
        modes_x, pairs_dev, 2, chans
    )
    mixed = mix_modes(spectrum, weight_pairs)
    spatial = from_slab(to_space(mixed, table_x), table_yw, planes)
    field4 = field.reshape(rows, length_y, planes, chans)
    local_term = mult("xypc,co->xypo", field4, local_weight)
    preact = spatial.reshape(rows, length_y, planes, chans) + local_term + bias
    output_field = jax.nn.gelu(preact).astype(jnp.bfloat16).reshape(rows, length_y, width_all)
    unused, pullback = jax.vjp(jax.nn.gelu, preact)
    grad_pre = pullback(cotangent.reshape(rows, length_y, planes, chans).astype(jnp.float32))[
        0
    ].astype(jnp.bfloat16)
    bias_part = jnp.sum(grad_pre.astype(jnp.float32), axis=(0, 1, 2))
    weight_part = mult("xypc,xypo->co", field4, grad_pre)
    back_local = mult("xypo,co->xypc", grad_pre, local_weight)
    grad_slab = to_slab(grad_pre.reshape(rows, length_y, width_all), table_yw, planes)
    grad_modes = to_modes(grad_slab, table_x).reshape(modes_x, pairs_dev, 2, chans)
    grad_spec = adjoint_mix(grad_modes, weight_pairs)
    back_spec = from_slab(to_space(grad_spec, table_x), table_y, planes)
    field_grad = (back_spec + back_local.reshape(rows, length_y, width_all)).astype(jnp.bfloat16)
    per_pair = pair_grad(
        spectrum.reshape(modes_x, pairs_dev, 1, 2, chans),
        grad_modes.reshape(modes_x, pairs_dev, 1, 2, chans),
    )
    onehot = (ky_index[:, None] == jnp.arange(modes_y, dtype=jnp.int32)[None, :]).astype(
        jnp.float32
    )
    partial_grad = jnp.einsum("jnsco,nm->jmsco", per_pair, onehot, precision=lax.Precision.HIGHEST)
    total, local_grad, bias_grad = lax.psum((partial_grad, weight_part, bias_part), "xy")
    spectral_grad = total.reshape(modes_x, modes_y, 2 * chans * chans).astype(jnp.bfloat16)
    return (output_field, field_grad, spectral_grad, local_grad, bias_grad)


F32 = jnp.float32
BF16 = jnp.bfloat16
LANES = 128
VMEM_LIMIT = 24 * 1024 * 1024


def dot(left, right):
    return jnp.dot(left, right, preferred_element_type=F32)


def params(**kwargs):
    return pltpu.CompilerParams(vmem_limit_bytes=VMEM_LIMIT, **kwargs)


def cost(flops, bytes_accessed):
    return pl.CostEstimate(flops=flops, bytes_accessed=bytes_accessed, transcendentals=0)


def np_ytable(count, length, weighted):
    modes = np.arange(count)
    places = np.arange(length)
    phase = np.float32(2.0 * math.pi) * (modes[:, None] * places[None, :] % length).astype(np.float32) / np.float32(length)
    factor = np.where(modes == 0, 1.0, 2.0).astype(np.float32) if weighted else np.ones((count,), np.float32)
    scale = (factor / np.float32(math.sqrt(length)))[:, None]
    both = np.stack([scale * np.cos(phase), -scale * np.sin(phase)]).astype(ml_dtypes.bfloat16)
    return both.reshape(2 * count, length)


def np_xtables(count, length):
    index = np.arange(count)
    modes = np.where(index < count // 2, index, length - count + index)
    places = np.arange(length)
    phase = np.float32(2.0 * math.pi) * (modes[:, None] * places[None, :] % length).astype(np.float32) / np.float32(length)
    norm = np.float32(math.sqrt(length))
    cosines = np.cos(phase) / norm
    sines = np.sin(phase) / norm
    forward = np.stack([np.stack([cosines, sines], -1), np.stack([-sines, cosines], -1)])
    forward = forward.reshape(2 * count, 2 * length).astype(ml_dtypes.bfloat16)
    return forward, np.ascontiguousarray(forward.T)


def lane_equals(rows, lanes, divide, offset):
    row = lax.broadcasted_iota(jnp.int32, (rows, lanes), 0)
    lane = lax.broadcasted_iota(jnp.int32, (rows, lanes), 1)
    return jnp.where(row - divide(lane) == offset, 1.0, 0.0).astype(BF16)


def start_all(pairs, sem):
    copies = [pltpu.make_async_copy(src, dst, sem.at[n]) for n, (src, dst) in enumerate(pairs)]
    for copy in copies:
        copy.start()
    return copies


def hbm():
    return pl.BlockSpec(memory_space=pltpu.HBM)


def in_hbm(*arrays):
    return [pltpu.with_memory_space_constraint(a, pltpu.HBM) for a in arrays]


def vmem():
    return pl.BlockSpec(memory_space=pltpu.VMEM)


def smem():
    return pl.BlockSpec(memory_space=pltpu.SMEM)


def scatter_rows(dst, sums, place, chips, half):
    tiles = half // LANES
    for s in range(2):
        for core in range(2):
            where = pl.ds(core * 8 + 2 * place + s, chips, stride=16)
            own = (3 * s + 2 * core) * chips
            shared = (3 * s + 1) * chips
            for k in range(2 * tiles):
                dst[k, where, :] = sums[own : own + chips, k * LANES : (k + 1) * LANES]
            for k in range(tiles):
                at = (core * tiles + k) * LANES
                dst[2 * tiles + k, where, :] = sums[shared : shared + chips, at : at + LANES]


def gather_rows(src, place, chips, half):
    tiles = half // LANES
    out = []
    for s in range(2):
        one = pl.ds(2 * place + s, chips, stride=16)
        two = pl.ds(8 + 2 * place + s, chips, stride=16)
        own = range(2 * tiles)
        shared = range(2 * tiles, 3 * tiles)
        out.append(jnp.concatenate([src[k, one, :] for k in own], axis=1))
        out.append(jnp.concatenate([src[k, w, :] for w in (one, two) for k in shared], axis=1))
        out.append(jnp.concatenate([src[k, two, :] for k in own], axis=1))
    return jnp.concatenate(out, axis=0).astype(BF16)


def cut_lanes(dst, src):
    for k in range(dst.shape[0]):
        dst[k] = src[:, k * LANES : (k + 1) * LANES].astype(F32)


def join_lanes(dst, src):
    for k in range(src.shape[0]):
        dst[:, k * LANES : (k + 1) * LANES] = src[k].astype(BF16)


def cut_shape(shape):
    return (shape[1] // LANES, shape[0], LANES)


def rows_to_modes(field, table, chips, half):
    rows, length, width = field.shape
    shape = (chips * 16, 3 * half)

    def kernel(u_hbm, t_hbm, out_hbm, u_ref, t_ref, scr, out_ref, sem, out_sem):
        copies = start_all([(t_hbm, t_ref)] + [(u_hbm.at[x], u_ref.at[x]) for x in range(rows)], sem)
        copies[0].wait()
        for x in range(rows):
            copies[1 + x].wait()
            scatter_rows(scr, dot(t_ref[...], u_ref[x]), x, chips, half)
        join_lanes(out_ref, scr)
        copy = pltpu.make_async_copy(out_ref, out_hbm, out_sem)
        copy.start()
        copy.wait()

    return pl.pallas_call(
        kernel,
        in_specs=[hbm(), hbm()],
        out_specs=hbm(),
        out_shape=pltpu.HBM(shape, BF16),
        scratch_shapes=[
            pltpu.VMEM(field.shape, BF16),
            pltpu.VMEM(table.shape, BF16),
            pltpu.VMEM(cut_shape(shape), F32),
            pltpu.VMEM(shape, BF16),
            pltpu.SemaphoreType.DMA((1 + rows,)),
            pltpu.SemaphoreType.DMA,
        ],
        compiler_params=params(),
        cost_estimate=cost(2 * table.size * rows * width, field.size * 2),
        name="rows_to_modes",
    )(*in_hbm(field, table))


def prepare(me, weights, local_weight, bias, chips, half):
    modes_x, modes_y, full2 = weights.shape
    chans = local_weight.shape[0]
    tiles = full2 // LANES
    rows = 4 * modes_x
    groups = full2 // 2 // LANES
    batch = 6

    def kernel(
        me_ref, w_hbm, l_ref, b_ref, plain_hbm, turned_hbm, block_hbm, block_t_hbm, bias_hbm,
        w_ref, scr, pick, one, two, plain_ref, turned_ref, block_ref, block_t_ref, bias_ref, sem, out_sem,
    ):
        cuts = [pl.ds(j, batch) for j in range(0, modes_x, batch)]
        copies = start_all([(w_hbm.at[cut], w_ref.at[cut]) for cut in cuts], sem)

        spread = lane_equals(chans, half, lambda l: l % chans, 0)
        row = lax.broadcasted_iota(jnp.int32, (half, half), 0) // chans
        lane = lax.broadcasted_iota(jnp.int32, (half, half), 1) // chans
        local = l_ref[...]
        for ref, dims in ((block_ref, 1), (block_t_ref, 0)):
            wide = lax.dot_general(local, spread, (((dims,), (0,)), ((), ())), preferred_element_type=F32)
            wide = jnp.concatenate([wide] * (half // chans), axis=0)
            ref[...] = jnp.where(row == lane, wide, 0.0).astype(BF16)
        value = jnp.concatenate([b_ref[...]] * 8, axis=0)
        high = value.astype(BF16)
        mid = (value - high.astype(F32)).astype(BF16)
        low = (value - high.astype(F32) - mid.astype(F32)).astype(BF16)
        wide = dot(high, spread) + dot(mid, spread) + dot(low, spread)
        bias_ref[...] = jnp.concatenate([wide, wide], axis=1)
        out_copies = start_all(
            [(block_ref, block_hbm), (block_t_ref, block_t_hbm), (bias_ref, bias_hbm)], out_sem
        )

        for n, first in enumerate(range(0, modes_x, batch)):
            copies[n].wait()
            for j in range(first, first + batch):
                for k in range(tiles):
                    scr[k, j * modes_y : (j + 1) * modes_y, :] = w_ref[j, :, k * LANES : (k + 1) * LANES].astype(F32)
        chip, core = me_ref[0] // 2, me_ref[0] % 2
        for w, mode in enumerate((chip + 2 * chips * core, chip + chips)):
            for k in range(tiles):
                s, g = divmod(k, groups)
                base = (2 * w + s) * modes_x
                pick[g, base : base + modes_x, :] = scr[k, pl.ds(mode, modes_x, stride=modes_y), :]
        per = LANES // chans
        repeat = jnp.concatenate(
            [lane_equals(LANES, LANES, lambda l: l % chans, chans * g) for g in range(per)], axis=1
        )
        pad = jnp.zeros((LANES - rows, LANES), F32)
        for g in range(groups):
            plain_ref[g] = dot(pick[g].astype(BF16), repeat).astype(BF16)
            one[g * LANES : (g + 1) * LANES, :] = jnp.transpose(jnp.concatenate([pick[g], pad]))
        out_copies.append(pltpu.make_async_copy(plain_ref, plain_hbm, out_sem.at[3]))
        out_copies[-1].start()
        for b in range(chans):
            two[b * chans : (b + 1) * chans, :] = one[pl.ds(b, chans, stride=chans), :]
        for g in range(groups):
            part = jnp.transpose(two[g * LANES : (g + 1) * LANES, :])[0:rows]
            turned_ref[g] = dot(part.astype(BF16), repeat).astype(BF16)
        out_copies.append(pltpu.make_async_copy(turned_ref, turned_hbm, out_sem.at[4]))
        out_copies[-1].start()
        for copy in out_copies:
            copy.wait()

    shape = (groups, rows, LANES * LANES // chans)
    wide = pltpu.HBM(shape, BF16)
    block = pltpu.HBM((half, half), BF16)
    return pl.pallas_call(
        kernel,
        in_specs=[smem(), hbm(), vmem(), vmem()],
        out_specs=(hbm(),) * 5,
        out_shape=(wide, wide, block, block, pltpu.HBM((8, 2 * half), F32)),
        scratch_shapes=[
            pltpu.VMEM(weights.shape, BF16),
            pltpu.VMEM((tiles, modes_x * modes_y, LANES), F32),
            pltpu.VMEM((groups, rows, LANES), F32),
            pltpu.VMEM((full2 // 2, LANES), F32),
            pltpu.VMEM((full2 // 2, LANES), F32),
            pltpu.VMEM(shape, BF16),
            pltpu.VMEM(shape, BF16),
            pltpu.VMEM((half, half), BF16),
            pltpu.VMEM((half, half), BF16),
            pltpu.VMEM((8, 2 * half), F32),
            pltpu.SemaphoreType.DMA((modes_x // batch,)),
            pltpu.SemaphoreType.DMA((5,)),
        ],
        compiler_params=params(),
        cost_estimate=cost(1000000, 4 * 1024 * 1024),
        name="prepare",
    )(me, *in_hbm(weights), local_weight, bias)


def weigh(spec, w_ref, chans, modes_x, adjoint):
    tiles = spec.shape[1] // LANES
    groups = LANES // chans
    stack = jnp.concatenate([spec[:, k * LANES : (k + 1) * LANES] for k in range(tiles)], axis=0)
    real = [None] * tiles
    imag = [None] * tiles
    for pair in range(chans // 2):
        two = [lane_equals(LANES, LANES, lambda l: l // chans * chans, c) for c in (2 * pair, 2 * pair + 1)]
        wide_rows = dot(stack, jnp.concatenate(two, axis=1))
        for c in (2 * pair, 2 * pair + 1):
            lanes = slice((c % 2) * LANES, (c % 2 + 1) * LANES)
            wl = slice((c % groups) * LANES, (c % groups + 1) * LANES)
            for own in range(2):
                base = 2 * own * modes_x
                wr = w_ref[c // groups, base : base + modes_x, wl].astype(F32)
                wi = w_ref[c // groups, base + modes_x : base + 2 * modes_x, wl].astype(F32)
                for k in range(0, 2 * tiles // 3) if own == 0 else range(2 * tiles // 3, tiles):
                    xr = wide_rows[2 * k * modes_x : (2 * k + 1) * modes_x, lanes]
                    xi = wide_rows[(2 * k + 1) * modes_x : (2 * k + 2) * modes_x, lanes]
                    if adjoint:
                        r, i = xr * wr + xi * wi, xi * wr - xr * wi
                    else:
                        r, i = xr * wr - xi * wi, xr * wi + xi * wr
                    real[k] = r if real[k] is None else real[k] + r
                    imag[k] = i if imag[k] is None else imag[k] + i
    return jnp.concatenate([jnp.concatenate(real, axis=1), jnp.concatenate(imag, axis=1)], axis=0).astype(BF16)


def mode_step(pencil, spread_w, forward, inverse, chans):
    modes_x = forward.shape[0] // 2

    def kernel(p_ref, w_hbm, f_hbm, i_hbm, spec_ref, out_hbm, w_ref, f_ref, i_ref, out_ref, sem, out_sem):
        copies = start_all([(f_hbm, f_ref), (w_hbm, w_ref), (i_hbm, i_ref)], sem)
        copies[0].wait()
        spec = dot(f_ref[...], p_ref[...]).astype(BF16)
        spec_ref[...] = spec
        copies[1].wait()
        copies[2].wait()
        mixed = weigh(spec, w_ref, chans, modes_x, False)
        out_ref[...] = dot(i_ref[...], mixed).astype(BF16)
        copy = pltpu.make_async_copy(out_ref, out_hbm, out_sem)
        copy.start()
        copy.wait()

    return pl.pallas_call(
        kernel,
        in_specs=[vmem()] + [hbm()] * 3,
        out_specs=(vmem(), hbm()),
        out_shape=(
            jax.ShapeDtypeStruct((2 * modes_x, pencil.shape[1]), BF16),
            pltpu.HBM(pencil.shape, BF16),
        ),
        scratch_shapes=[
            pltpu.VMEM(spread_w.shape, BF16),
            pltpu.VMEM(forward.shape, BF16),
            pltpu.VMEM(inverse.shape, BF16),
            pltpu.VMEM(pencil.shape, BF16),
            pltpu.SemaphoreType.DMA((3,)),
            pltpu.SemaphoreType.DMA,
        ],
        compiler_params=params(),
        cost_estimate=cost(2 * 48 * 6 * 128 * 4096, spread_w.size * 4),
        name="mode_step",
    )(pencil, *in_hbm(spread_w, forward, inverse))


def adjoint_step(grads, spread_w, inverse, chans):
    modes_x = grads.shape[0] // 2
    shape = (inverse.shape[0], grads.shape[1])

    def kernel(g_ref, w_hbm, i_hbm, out_hbm, w_ref, i_ref, out_ref, sem, out_sem):
        for copy in start_all([(w_hbm, w_ref), (i_hbm, i_ref)], sem):
            copy.wait()
        mixed = weigh(g_ref[...], w_ref, chans, modes_x, True)
        out_ref[...] = dot(i_ref[...], mixed).astype(BF16)
        copy = pltpu.make_async_copy(out_ref, out_hbm, out_sem)
        copy.start()
        copy.wait()

    return pl.pallas_call(
        kernel,
        in_specs=[vmem(), hbm(), hbm()],
        out_specs=hbm(),
        out_shape=pltpu.HBM(shape, BF16),
        scratch_shapes=[
            pltpu.VMEM(spread_w.shape, BF16),
            pltpu.VMEM(inverse.shape, BF16),
            pltpu.VMEM(shape, BF16),
            pltpu.SemaphoreType.DMA((2,)),
            pltpu.SemaphoreType.DMA,
        ],
        compiler_params=params(),
        cost_estimate=cost(2 * 48 * 6 * 128 * 4096, spread_w.size * 4),
        name="adjoint_step",
    )(grads, *in_hbm(spread_w, inverse))


def pointwise(field, cotangent, pencil, table_t, table, block_weight, bias_row, chips, half):
    rows, length, width = field.shape
    chunk, sub = 128, 16
    modes = table.shape[0]
    depth = table_t.shape[1]

    def kernel(
        u_hbm, c_hbm, p_ref, tt_hbm, t_hbm, w_hbm, b_hbm, out_hbm, dpre_hbm, send_hbm,
        u_ref, c_ref, tt_ref, t_ref, w_ref, b_ref, out_ref, dpre_ref, send_ref, bscr, dscr, sem, out_sem,
    ):
        copies = start_all([(tt_hbm, tt_ref), (w_hbm, w_ref), (b_hbm, b_ref), (t_hbm, t_ref)], sem)
        for x in range(rows):
            pltpu.make_async_copy(u_hbm.at[x], u_ref.at[x], sem.at[4 + x]).start()
            pltpu.make_async_copy(c_hbm.at[x], c_ref.at[x], sem.at[4 + rows + x]).start()
        for copy in copies:
            copy.wait()
        cut_lanes(bscr, p_ref)
        root = math.sqrt(2.0 / math.pi)
        bias = b_ref[0:1, :]
        high = bias.astype(BF16)
        mid = (bias - high.astype(F32)).astype(BF16)
        low = (bias - high.astype(F32) - mid.astype(F32)).astype(BF16)
        parts = [t.astype(F32) for t in (high, mid, low)]
        bias = jnp.concatenate(parts + [jnp.zeros((depth - modes - 3, width), F32)], axis=0)
        bias = (0.5 * bias).astype(BF16)
        weight = (0.5 * w_ref[...].astype(F32)).astype(BF16)

        def one_row(x):
            pltpu.make_async_copy(u_hbm.at[x], u_ref.at[x], sem.at[4 + x]).wait()
            pltpu.make_async_copy(c_hbm.at[x], c_ref.at[x], sem.at[4 + rows + x]).wait()
            coeff = (0.5 * gather_rows(bscr, x, chips, half).astype(F32)).astype(BF16)
            coeff = jnp.concatenate([coeff, bias], axis=0)
            for k in range(length // chunk):
                where = pl.ds(k * chunk, chunk)
                for h in range(2):
                    lanes = slice(h * half, (h + 1) * half)
                    left = jnp.concatenate([u_ref[x, where, lanes], tt_ref[where, :]], axis=1)
                    right = jnp.concatenate([weight, coeff[:, lanes]], axis=0)
                    halved = dot(left, right)
                    for at in range(0, chunk, sub):
                        place = pl.ds(k * chunk + at, sub)
                        p = halved[at : at + sub]
                        inner = p * (2.0 * root + (8.0 * root * 0.044715) * (p * p))
                        th = jnp.tanh(inner)
                        twice = 1.0 + th
                        out_ref[x, place, lanes] = (p * twice).astype(BF16)
                        slope = 1.5 * inner - (2.0 * root) * p
                        grad = twice * (0.5 + (1.0 - th) * slope)
                        dpre_ref[x, place, lanes] = (c_ref[x, place, lanes].astype(F32) * grad).astype(BF16)
            pltpu.make_async_copy(out_ref.at[x], out_hbm.at[x], out_sem.at[x]).start()
            pltpu.make_async_copy(dpre_ref.at[x], dpre_hbm.at[x], out_sem.at[rows + x]).start()
            scatter_rows(dscr, dot(t_ref[...], dpre_ref[x]), x, chips, half)

        for x in range(rows):
            one_row(x)
        join_lanes(send_ref, dscr)
        pltpu.make_async_copy(send_ref, send_hbm, out_sem.at[2 * rows]).start()
        for x in range(rows):
            pltpu.make_async_copy(out_ref.at[x], out_hbm.at[x], out_sem.at[x]).wait()
            pltpu.make_async_copy(dpre_ref.at[x], dpre_hbm.at[x], out_sem.at[rows + x]).wait()
        pltpu.make_async_copy(send_ref, send_hbm, out_sem.at[2 * rows]).wait()

    return pl.pallas_call(
        kernel,
        in_specs=[hbm(), hbm(), vmem()] + [hbm()] * 4,
        out_specs=(hbm(), hbm(), hbm()),
        out_shape=(
            pltpu.HBM(field.shape, BF16),
            pltpu.HBM(field.shape, BF16),
            pltpu.HBM(pencil.shape, BF16),
        ),
        scratch_shapes=[
            pltpu.VMEM(field.shape, BF16),
            pltpu.VMEM(field.shape, BF16),
            pltpu.VMEM(table_t.shape, BF16),
            pltpu.VMEM(table.shape, BF16),
            pltpu.VMEM(block_weight.shape, BF16),
            pltpu.VMEM(bias_row.shape, F32),
            pltpu.VMEM(field.shape, BF16),
            pltpu.VMEM(field.shape, BF16),
            pltpu.VMEM(pencil.shape, BF16),
            pltpu.VMEM(cut_shape(pencil.shape), F32),
            pltpu.VMEM(cut_shape(pencil.shape), F32),
            pltpu.SemaphoreType.DMA((4 + 2 * rows,)),
            pltpu.SemaphoreType.DMA((2 * rows + 1,)),
        ],
        compiler_params=params(),
        cost_estimate=cost(field.size * 1000, field.size * 8),
        name="pointwise",
    )(*in_hbm(field, cotangent), pencil, *in_hbm(table_t, table, block_weight, bias_row))


def local_sums(field, dpre, chans, half):
    rows, length, width = field.shape
    slices = half // chans

    def kernel(u_hbm, d_hbm, out_ref, u_ref, d_ref, sem):
        copies = start_all(
            [(u_hbm.at[x], u_ref.at[x]) for x in range(rows)] + [(d_hbm.at[x], d_ref.at[x]) for x in range(rows)], sem
        )
        both = bias = None
        ones = jnp.ones((16, length), BF16)
        for x in range(rows):
            copies[x].wait()
            copies[rows + x].wait()
            for h in range(2):
                lanes = slice(h * half, (h + 1) * half)
                part = lax.dot_general(
                    u_ref[x, :, lanes], d_ref[x, :, lanes], (((0,), (0,)), ((), ())), preferred_element_type=F32
                )
                both = part if both is None else both + part
            part = dot(ones, d_ref[x])[0:8]
            bias = part if bias is None else bias + part
        group = lax.broadcasted_iota(jnp.int32, (chans, half), 1) // chans
        total = jnp.zeros((chans, half), F32)
        for p in range(slices):
            total = jnp.where(group == p, both[p * chans : (p + 1) * chans], total)
        total = sum(total[:, k * LANES : (k + 1) * LANES] for k in range(half // LANES))
        bias = sum(bias[:, k * LANES : (k + 1) * LANES] for k in range(width // LANES))
        shift = LANES // 2
        while shift >= chans:
            total = total + pltpu.roll(total, shift, 1)
            bias = bias + pltpu.roll(bias, shift, 1)
            shift //= 2
        group8 = lax.broadcasted_iota(jnp.int32, (8, LANES), 1) // chans
        folded = jnp.zeros((8, LANES), F32)
        for k in range(chans // 8):
            folded = jnp.where(group8 == k, total[8 * k : 8 * k + 8], folded)
        value = jnp.concatenate([folded, bias], axis=0)
        high = value.astype(BF16).astype(F32)
        mid = (value - high).astype(BF16).astype(F32)
        low = value - high - mid
        left = jnp.concatenate([high, mid[0:8]], axis=0)
        right = jnp.concatenate([mid[8:16], low], axis=0)
        out_ref[...] = jnp.concatenate([left, right], axis=1).astype(BF16)

    return pl.pallas_call(
        kernel,
        in_specs=[hbm(), hbm()],
        out_specs=vmem(),
        out_shape=jax.ShapeDtypeStruct((24, 2 * LANES), BF16),
        scratch_shapes=[
            pltpu.VMEM(field.shape, BF16),
            pltpu.VMEM(field.shape, BF16),
            pltpu.SemaphoreType.DMA((2 * rows,)),
        ],
        compiler_params=params(),
        cost_estimate=cost(field.size * 1000, field.size * 4),
        name="local_sums",
    )(*in_hbm(field, dpre))


def weight_sums(spectrum, pencil, forward, chans):
    modes_x = spectrum.shape[0] // 2
    tiles = spectrum.shape[1] // LANES
    groups = LANES // chans
    step = 2 * LANES
    full = chans * chans
    parts = full // step

    def kernel(u_ref, p_ref, f_hbm, d_ref, own_ref, shared_ref, f_ref, sem):
        copy = start_all([(f_hbm, f_ref)], sem)[0]

        def stack(ref):
            return jnp.concatenate([ref[:, k * LANES : (k + 1) * LANES] for k in range(tiles)], axis=0)

        left = stack(u_ref)
        copy.wait()
        d_ref[...] = dot(f_ref[...], p_ref[...]).astype(BF16)
        repeat = jnp.concatenate(
            [lane_equals(LANES, LANES, lambda l: l % chans, chans * g) for g in range(groups)], axis=1
        )
        right = dot(stack(d_ref), repeat)
        for a in range(parts):
            sums = {}
            for g in range(groups):
                pick = lane_equals(LANES, step, lambda l: l // chans, g * chans + a * (step // chans))
                spread_u = dot(left, pick)
                for k in range(tiles):
                    kind = 0 if k < 2 * tiles // 3 else 1
                    re = slice(2 * k * modes_x, (2 * k + 1) * modes_x)
                    im = slice((2 * k + 1) * modes_x, (2 * k + 2) * modes_x)
                    for z in range(2):
                        lanes = slice(z * LANES, (z + 1) * LANES)
                        ur, ui = spread_u[re, lanes], spread_u[im, lanes]
                        dr = right[re, g * LANES : (g + 1) * LANES]
                        di = right[im, g * LANES : (g + 1) * LANES]
                        for t, term in ((0, ur * dr + ui * di), (1, ur * di - ui * dr)):
                            key = (kind, t, z)
                            sums[key] = term if key not in sums else sums[key] + term
            for t in range(2):
                lanes = slice(t * full + a * step, t * full + (a + 1) * step)
                own_ref[:, lanes] = jnp.concatenate([sums[0, t, 0], sums[0, t, 1]], axis=1).astype(BF16)
                shared_ref[:, lanes] = jnp.concatenate([sums[1, t, 0], sums[1, t, 1]], axis=1)

    return pl.pallas_call(
        kernel,
        in_specs=[vmem(), vmem(), hbm()],
        out_shape=(
            jax.ShapeDtypeStruct(spectrum.shape, BF16),
            jax.ShapeDtypeStruct((modes_x, 2 * full), BF16),
            jax.ShapeDtypeStruct((modes_x, 2 * full), F32),
        ),
        scratch_shapes=[pltpu.VMEM(forward.shape, BF16), pltpu.SemaphoreType.DMA((1,))],
        compiler_params=params(),
        cost_estimate=cost(2 * 288 * 128 * 4096, 4 * 1024 * 1024),
        name="weight_sums",
    )(spectrum, pencil, *in_hbm(forward))


def make_shard(me, own, shared, other, stats):
    rows, full2 = own.shape
    full = full2 // 2
    half = full // 2
    width = full2 + full + stats.shape[1]

    def kernel(me_ref, o_ref, s_ref, r_ref, st_ref, out_ref):
        first = me_ref[0] % 2 == 0
        out_ref[:, 0:full2] = o_ref[...]
        for t in range(2):
            low = slice(t * full, t * full + half)
            high = slice(t * full + half, (t + 1) * full)
            mine = jnp.where(first, s_ref[:, low], s_ref[:, high])
            theirs = jnp.where(first, r_ref[:, low], r_ref[:, high])
            out_ref[:, full2 + t * half : full2 + (t + 1) * half] = (mine + theirs).astype(BF16)
        out_ref[:, full2 + full :] = st_ref[...]

    return pl.pallas_call(
        kernel,
        in_specs=[smem()] + [vmem()] * 4,
        out_shape=jax.ShapeDtypeStruct((rows, width), BF16),
        compiler_params=params(),
        cost_estimate=cost(100000, 1000000),
        name="make_shard",
    )(me, own, shared, other, stats)


def ring_chip(spot, chips):
    return jnp.where(spot < chips // 2, 2 * spot, 2 * (chips - 1 - spot) + 1)


def ring_spot(chip, chips):
    return jnp.where(chip % 2 == 0, chip // 2, chips - 1 - chip // 2)


def read_sums(ref, full):
    left = ref[:, 3 * full : 3 * full + LANES].astype(F32)
    right = ref[:, 3 * full + LANES : 3 * full + 2 * LANES].astype(F32)
    middle = jnp.concatenate([left[16:24], right[0:8]], axis=0)
    return left[0:16] + middle + right[8:24]


def early_sums(shards_all, chans):
    count = len(shards_all)
    shape = (count, 16, LANES)

    def kernel(*refs):
        ins, (out_hbm, out_ref, sem) = refs[:count], refs[count:]
        for n in range(count):
            out_ref[n] = read_sums(ins[n], chans * chans)
        copy = pltpu.make_async_copy(out_ref, out_hbm, sem)
        copy.start()
        copy.wait()

    return pl.pallas_call(
        kernel,
        in_specs=[vmem()] * count,
        out_specs=hbm(),
        out_shape=pltpu.HBM(shape, F32),
        scratch_shapes=[pltpu.VMEM(shape, F32), pltpu.SemaphoreType.DMA],
        compiler_params=params(),
        cost_estimate=cost(3 * 10**10, 4 * 1024 * 1024),
        name="early_sums",
    )(*shards_all)


def assemble(me, early, shards_all, turns, modes_y, chans, chips):
    rows = shards_all[0].shape[0]
    full = chans * chans
    tiles = 2 * full // LANES
    part = full // 2 // LANES
    count = len(shards_all)

    def kernel(me_ref, e_hbm, *refs):
        ins, (g_ref, l_ref, b_ref, scr, stat, out, e_ref, sem) = refs[:count], refs[count:]
        fetch = pltpu.make_async_copy(e_hbm, e_ref, sem.at[tiles // 4])
        fetch.start()
        spot = ring_spot(me_ref[0] // 2, chips)
        places = []
        for back, swapped in turns:
            chip = ring_chip((spot + chips - back) % chips, chips)
            core = me_ref[0] % 2
            places.append((chip, 1 - core if swapped else core))
        copies = []
        for k in range(tiles):
            keeper = k % (2 * part) // part
            at = tiles + k // (2 * part) * part + k % part
            for n, (chip, core) in enumerate(places):
                own = pl.ds(chip + 2 * chips * core, rows, stride=modes_y)
                scr[k, own, :] = ins[n][:, k * LANES : (k + 1) * LANES].astype(F32)
                if turns[n][1]:
                    continue
                mate = turns.index((turns[n][0], True))
                lanes = slice(at * LANES, (at + 1) * LANES)
                shared = pl.ds(chip + chips, rows, stride=modes_y)
                scr[k, shared, :] = jnp.where(core == keeper, ins[n][:, lanes], ins[mate][:, lanes]).astype(F32)
            lanes = slice(k * LANES, (k + 1) * LANES)
            for j in range(rows):
                out[j, :, lanes] = scr[k, j * modes_y : (j + 1) * modes_y, :].astype(BF16)
            if k % 4 == 3:
                lanes = pl.ds((k - 3) * LANES, 4 * LANES)
                copies.append(pltpu.make_async_copy(out.at[:, :, lanes], g_ref.at[:, :, lanes], sem.at[k // 4]))
                copies[-1].start()
        fetch.wait()
        for n, (chip, core) in enumerate(places):
            stat[2 * chip + core] = e_ref[n] if n < early.shape[0] else read_sums(ins[n], full)
        total = stat[0]
        for n in range(1, count):
            total = total + stat[n]
        for k in range(chans // 8):
            piece = total[0:8] if k == 0 else pltpu.roll(total[0:8], LANES - k * chans, 1)
            l_ref[8 * k : 8 * k + 8, :] = piece[:, 0:chans]
        b_ref[...] = total[8:9, 0:chans]
        for copy in copies:
            copy.wait()

    shape = (rows, modes_y, 2 * full)
    return pl.pallas_call(
        kernel,
        in_specs=[smem(), hbm()] + [vmem()] * count,
        out_specs=(hbm(), vmem(), vmem()),
        out_shape=(
            pltpu.HBM(shape, BF16),
            jax.ShapeDtypeStruct((chans, chans), F32),
            jax.ShapeDtypeStruct((1, chans), F32),
        ),
        scratch_shapes=[
            pltpu.VMEM((tiles, rows * modes_y, LANES), F32),
            pltpu.VMEM((count, 16, LANES), F32),
            pltpu.VMEM(shape, BF16),
            pltpu.VMEM(early.shape, F32),
            pltpu.SemaphoreType.DMA((tiles // 4 + 1,)),
        ],
        compiler_params=params(),
        cost_estimate=cost(1000000, 8 * 1024 * 1024),
        name="assemble",
    )(me, *in_hbm(early), *shards_all)


def back_to_field(dpre, pencil, table_t, block_weight, chips, half):
    rows, length, width = dpre.shape
    chunk = 128

    def kernel(d_hbm, p_ref, tt_hbm, w_hbm, out_hbm, d_ref, tt_ref, w_ref, out_ref, bscr, sem, out_sem):
        copies = start_all(
            [(tt_hbm, tt_ref), (w_hbm, w_ref)] + [(d_hbm.at[x], d_ref.at[x]) for x in range(rows)], sem
        )
        for copy in copies[0:2]:
            copy.wait()
        cut_lanes(bscr, p_ref)
        out_copies = []
        for x in range(rows):
            copies[2 + x].wait()
            coeff = gather_rows(bscr, x, chips, half)
            for k in range(length // chunk):
                where = pl.ds(k * chunk, chunk)
                d = d_ref[x, where, :]
                spec = dot(tt_ref[where, :], coeff)
                for h in range(2):
                    lanes = slice(h * half, (h + 1) * half)
                    out_ref[x, where, lanes] = (spec[:, lanes] + dot(d[:, lanes], w_ref[...])).astype(BF16)
            out_copies.append(pltpu.make_async_copy(out_ref.at[x], out_hbm.at[x], out_sem.at[x]))
            out_copies[-1].start()
        for copy in out_copies:
            copy.wait()

    return pl.pallas_call(
        kernel,
        in_specs=[hbm(), vmem(), hbm(), hbm()],
        out_specs=hbm(),
        out_shape=pltpu.HBM(dpre.shape, BF16),
        scratch_shapes=[
            pltpu.VMEM(dpre.shape, BF16),
            pltpu.VMEM(table_t.shape, BF16),
            pltpu.VMEM(block_weight.shape, BF16),
            pltpu.VMEM(dpre.shape, BF16),
            pltpu.VMEM(cut_shape(pencil.shape), F32),
            pltpu.SemaphoreType.DMA((2 + rows,)),
            pltpu.SemaphoreType.DMA((rows,)),
        ],
        compiler_params=params(),
        cost_estimate=cost(dpre.size * 500, dpre.size * 4),
        name="back_to_field",
    )(*in_hbm(dpre), pencil, *in_hbm(table_t, block_weight))


def exchange(pencil):
    return lax.all_to_all(pencil, "xy", split_axis=0, concat_axis=0, tiled=True)


class Ring:
    def __init__(self, shard, chips):
        order = [ring_chip_int(i, chips) for i in range(chips)]
        self.chips = chips
        self.hops = {
            way: [(2 * order[i] + c, 2 * order[(i + way) % chips] + c) for i in range(chips) for c in range(2)]
            for way in (1, -1)
        }
        self.swap = [(i, i ^ 1) for i in range(2 * chips)]
        self.step = 0
        self.ahead = self.back = shard
        self.parts, self.turns = [], []
        self.keep(shard, 0)

    def keep(self, piece, turn):
        self.parts.append(piece)
        self.turns.append((turn, False))
        self.parts.append(lax.ppermute(piece, "xy", self.swap))
        self.turns.append((turn, True))

    def hop(self):
        self.step += 1
        self.ahead = lax.ppermute(self.ahead, "xy", self.hops[1])
        if self.step < self.chips // 2:
            self.back = lax.ppermute(self.back, "xy", self.hops[-1])

    def settle(self):
        self.keep(self.ahead, self.step)
        if self.step < self.chips // 2:
            self.keep(self.back, self.chips - self.step)

    def tie(self, other):
        self.ahead, self.back, other = lax.optimization_barrier((self.ahead, self.back, other))
        return other

    def hold(self, other):
        self.ahead, other = lax.optimization_barrier((self.ahead, other))
        return other


def ring_chip_int(spot, chips):
    return 2 * spot if spot < chips // 2 else 2 * (chips - 1 - spot) + 1


def fast_shards(field, spectral_weight, local_weight, bias, cotangent):
    rows, length_y, width = field.shape
    chans = local_weight.shape[0]
    planes = width // chans
    modes_x, modes_y = spectral_weight.shape[:2]
    devices = lax.axis_size("xy")
    chips = devices // 2
    half = width // 2
    me = lax.axis_index("xy")
    table_y = np_ytable(modes_y, length_y, False)
    table_yw = np_ytable(modes_y, length_y, True)
    table_y_t, table_yw_t = (np.ascontiguousarray(t.T) for t in (table_y, table_yw))
    ones = np.ones((length_y, 3), table_yw_t.dtype)
    zeros = np.zeros((length_y, -(table_yw_t.shape[1] + 3) % 16), table_yw_t.dtype)
    table_yw_t = np.concatenate([table_yw_t, ones, zeros], axis=1)
    forward, inverse = np_xtables(modes_x, rows * devices)
    me_id = me.astype(jnp.int32)[None]

    send = rows_to_modes(field, table_y, chips, half)
    pencil = exchange(send)
    plain, turned, block, block_t, bias_row = prepare(
        me_id, spectral_weight, local_weight, bias[None, :], chips, half
    )
    spectrum, send = mode_step(pencil, plain, forward, inverse, chans)
    pencil = exchange(send)
    output_field, dpre, send = pointwise(
        field, cotangent, pencil, table_yw_t, table_yw, block, bias_row, chips, half
    )
    pencil = exchange(send)
    stats = local_sums(field, dpre, chans, half)
    pencil, stats = lax.optimization_barrier((pencil, stats))
    grads, own, shared = weight_sums(spectrum, pencil, forward, chans)
    other = lax.ppermute(shared, "xy", [(i, i ^ 1) for i in range(devices)])
    shard = make_shard(me_id, own, shared, other, stats)

    ring = Ring(shard, chips)
    grads = ring.tie(grads)
    ring.hop()
    send = adjoint_step(grads, turned, inverse, chans)
    send = ring.tie(send)
    ring.settle()
    early = list(ring.parts)
    ring.hop()
    pencil = exchange(send)
    ring.settle()
    sums = early_sums(early, chans)
    sums = ring.tie(sums)
    ring.hop()
    pencil, sums = lax.optimization_barrier((pencil, sums))
    ring.settle()
    ring.hop()
    field_grad = back_to_field(dpre, pencil, table_y_t, block_t, chips, half)
    field_grad = ring.hold(field_grad)
    ring.settle()
    spectral_grad, local_grad, bias_grad = assemble(
        me_id, sums, ring.parts, ring.turns, modes_y, chans, chips
    )
    return output_field, field_grad, spectral_grad, local_grad, bias_grad.reshape(chans)


def fits(field, spectral_weight, local_weight, devices):
    rows, length_y, width = field.shape
    chans = local_weight.shape[0]
    modes_x, modes_y = spectral_weight.shape[:2]
    return (
        rows == 4
        and chans == 32
        and width == 512
        and length_y % 128 == 0
        and modes_x == 24
        and devices == 16
        and 2 * modes_y == 3 * devices
    )


def shards(field, spectral_weight, local_weight, bias, cotangent):
    if fits(field, spectral_weight, local_weight, lax.axis_size("xy")):
        return fast_shards(field, spectral_weight, local_weight, bias, cotangent)
    return general_shards(field, spectral_weight, local_weight, bias, cotangent)


def solution(mesh):
    return jax.shard_map(
        shards,
        mesh=mesh,
        in_specs=(P(("groups", "xy"), None, None), P(), P(), P(), P(("groups", "xy"), None, None)),
        out_specs=(
            P(("groups", "xy"), None, None),
            P(("groups", "xy"), None, None),
            P("groups", None, None),
            P("groups", None),
            P("groups"),
        ),
        check_vma=False,
    )
```

```python
import math

import jax
import jax.numpy as jnp
import ml_dtypes
import numpy as np
from jax import lax
from jax.experimental import pallas as pl
from jax.experimental.pallas import tpu as pltpu
from jax.sharding import PartitionSpec as P


def ytable(count, length, weighted):
    modes = jnp.arange(count, dtype=jnp.int32)
    places = jnp.arange(length, dtype=jnp.int32)
    phase = 2.0 * math.pi * (modes[:, None] * places[None, :] % length).astype(jnp.float32) / length
    factor = (
        jnp.where(modes == 0, 1.0, 2.0).astype(jnp.float32)
        if weighted
        else jnp.ones((count,), jnp.float32)
    )
    scale = factor[:, None] / math.sqrt(length)
    return jnp.stack([scale * jnp.cos(phase), -scale * jnp.sin(phase)]).astype(jnp.bfloat16)


def xtable(count, length, places):
    index = jnp.arange(count, dtype=jnp.int32)
    modes = jnp.where(index < count // 2, index, length - count + index)
    phase = 2.0 * math.pi * (modes[:, None] * places[None, :] % length).astype(jnp.float32) / length
    return (jnp.stack([jnp.cos(phase), jnp.sin(phase)]) / math.sqrt(length)).astype(jnp.bfloat16)


def mult(form, left, right):
    return jnp.einsum(form, left, right, preferred_element_type=jnp.float32)


def to_slab(flat, table, planes):
    rows = flat.shape[0]
    count = table.shape[1]
    chans = flat.shape[2] // planes
    coeff = mult("smy,xyq->xsmq", table, flat).astype(jnp.bfloat16)
    coeff = coeff.reshape(rows, 2, count, planes, chans).transpose(0, 2, 3, 1, 4)
    return coeff.reshape(rows, count * planes, 2 * chans)


def from_slab(slab, table, planes):
    rows = slab.shape[0]
    count = table.shape[1]
    chans = slab.shape[2] // 2
    spread = slab.reshape(rows, count, planes, 2, chans)
    return mult("smy,xmpsc->xypc", table, spread).reshape(rows, table.shape[2], planes * chans)


def forward_x(table, pencil):
    proj = mult("ajx,xnsc->ajnsc", table, pencil)
    real_part = proj[0, :, :, 0] + proj[1, :, :, 1]
    imag_part = proj[0, :, :, 1] - proj[1, :, :, 0]
    return jnp.stack([real_part, imag_part], axis=2).astype(jnp.bfloat16)


def inverse_x(table, modes):
    proj = mult("ajx,jnsc->axnsc", table, modes)
    real_part = proj[0, :, :, 0] - proj[1, :, :, 1]
    imag_part = proj[0, :, :, 1] + proj[1, :, :, 0]
    return jnp.stack([real_part, imag_part], axis=2).astype(jnp.bfloat16)


def mix_modes(spectrum, weights):
    real_part = mult("jnc,jnco->jno", spectrum[:, :, 0], weights[:, :, 0]) - mult(
        "jnc,jnco->jno", spectrum[:, :, 1], weights[:, :, 1]
    )
    imag_part = mult("jnc,jnco->jno", spectrum[:, :, 0], weights[:, :, 1]) + mult(
        "jnc,jnco->jno", spectrum[:, :, 1], weights[:, :, 0]
    )
    return jnp.stack([real_part, imag_part], axis=2).astype(jnp.bfloat16)


def adjoint_mix(grads, weights):
    real_part = mult("jnco,jno->jnc", weights[:, :, 0], grads[:, :, 0]) + mult(
        "jnco,jno->jnc", weights[:, :, 1], grads[:, :, 1]
    )
    imag_part = mult("jnco,jno->jnc", weights[:, :, 0], grads[:, :, 1]) - mult(
        "jnco,jno->jnc", weights[:, :, 1], grads[:, :, 0]
    )
    return jnp.stack([real_part, imag_part], axis=2).astype(jnp.bfloat16)


def pair_grad(spectrum, grads):
    real_part = mult("jmpc,jmpo->jmco", spectrum[:, :, :, 0], grads[:, :, :, 0]) + mult(
        "jmpc,jmpo->jmco", spectrum[:, :, :, 1], grads[:, :, :, 1]
    )
    imag_part = mult("jmpc,jmpo->jmco", spectrum[:, :, :, 0], grads[:, :, :, 1]) - mult(
        "jmpc,jmpo->jmco", spectrum[:, :, :, 1], grads[:, :, :, 0]
    )
    return jnp.stack([real_part, imag_part], axis=2)


def to_modes(slab, table_full):
    count = table_full.shape[1]
    pencil = lax.all_to_all(slab, "xy", split_axis=1, concat_axis=0, tiled=True)
    chans = pencil.shape[2] // 2
    items = pencil.shape[1]
    spread = pencil.reshape(pencil.shape[0], items, 2, chans)
    return forward_x(table_full, spread).reshape(count, items, 2 * chans)


def to_space(modes, table_full):
    count, pairs_dev, twice, chans = modes.shape
    pencil = inverse_x(table_full, modes)
    moved = lax.all_to_all(
        pencil.reshape(pencil.shape[0], pairs_dev, 2 * chans),
        "xy",
        split_axis=0,
        concat_axis=1,
        tiled=True,
    )
    return moved


def general_shards(field, spectral_weight, local_weight, bias, cotangent):
    rows, length_y, width_all = field.shape
    chans = local_weight.shape[0]
    planes = width_all // chans
    modes_x, modes_y = (spectral_weight.shape[0], spectral_weight.shape[1])
    devices = lax.axis_size("xy")
    length_x = rows * devices
    pairs_dev = modes_y * planes // devices
    offset = lax.axis_index("xy")
    table_y = ytable(modes_y, length_y, False)
    table_yw = ytable(modes_y, length_y, True)
    table_x = xtable(modes_x, length_x, jnp.arange(length_x, dtype=jnp.int32))
    weight_all = spectral_weight.reshape(modes_x, modes_y, 2, chans, chans)
    ky_index = (offset * pairs_dev + jnp.arange(pairs_dev, dtype=jnp.int32)) // planes
    weight_pairs = jnp.take(weight_all, ky_index, axis=1)
    spectrum = to_modes(to_slab(field, table_y, planes), table_x).reshape(
        modes_x, pairs_dev, 2, chans
    )
    mixed = mix_modes(spectrum, weight_pairs)
    spatial = from_slab(to_space(mixed, table_x), table_yw, planes)
    field4 = field.reshape(rows, length_y, planes, chans)
    local_term = mult("xypc,co->xypo", field4, local_weight)
    preact = spatial.reshape(rows, length_y, planes, chans) + local_term + bias
    output_field = jax.nn.gelu(preact).astype(jnp.bfloat16).reshape(rows, length_y, width_all)
    unused, pullback = jax.vjp(jax.nn.gelu, preact)
    grad_pre = pullback(cotangent.reshape(rows, length_y, planes, chans).astype(jnp.float32))[
        0
    ].astype(jnp.bfloat16)
    bias_part = jnp.sum(grad_pre.astype(jnp.float32), axis=(0, 1, 2))
    weight_part = mult("xypc,xypo->co", field4, grad_pre)
    back_local = mult("xypo,co->xypc", grad_pre, local_weight)
    grad_slab = to_slab(grad_pre.reshape(rows, length_y, width_all), table_yw, planes)
    grad_modes = to_modes(grad_slab, table_x).reshape(modes_x, pairs_dev, 2, chans)
    grad_spec = adjoint_mix(grad_modes, weight_pairs)
    back_spec = from_slab(to_space(grad_spec, table_x), table_y, planes)
    field_grad = (back_spec + back_local.reshape(rows, length_y, width_all)).astype(jnp.bfloat16)
    per_pair = pair_grad(
        spectrum.reshape(modes_x, pairs_dev, 1, 2, chans),
        grad_modes.reshape(modes_x, pairs_dev, 1, 2, chans),
    )
    onehot = (ky_index[:, None] == jnp.arange(modes_y, dtype=jnp.int32)[None, :]).astype(
        jnp.float32
    )
    partial_grad = jnp.einsum("jnsco,nm->jmsco", per_pair, onehot, precision=lax.Precision.HIGHEST)
    total, local_grad, bias_grad = lax.psum((partial_grad, weight_part, bias_part), "xy")
    spectral_grad = total.reshape(modes_x, modes_y, 2 * chans * chans).astype(jnp.bfloat16)
    return (output_field, field_grad, spectral_grad, local_grad, bias_grad)


F32 = jnp.float32
BF16 = jnp.bfloat16
LANES = 128
VMEM_LIMIT = 24 * 1024 * 1024


def dot(left, right):
    return jnp.dot(left, right, preferred_element_type=F32)


def params(**kwargs):
    return pltpu.CompilerParams(vmem_limit_bytes=VMEM_LIMIT, **kwargs)


def cost(flops, bytes_accessed):
    return pl.CostEstimate(flops=flops, bytes_accessed=bytes_accessed, transcendentals=0)


def np_ytable(count, length, weighted):
    modes = np.arange(count)
    places = np.arange(length)
    phase = np.float32(2.0 * math.pi) * (modes[:, None] * places[None, :] % length).astype(np.float32) / np.float32(length)
    factor = np.where(modes == 0, 1.0, 2.0).astype(np.float32) if weighted else np.ones((count,), np.float32)
    scale = (factor / np.float32(math.sqrt(length)))[:, None]
    both = np.stack([scale * np.cos(phase), -scale * np.sin(phase)]).astype(ml_dtypes.bfloat16)
    return both.reshape(2 * count, length)


def np_xtables(count, length):
    index = np.arange(count)
    modes = np.where(index < count // 2, index, length - count + index)
    places = np.arange(length)
    phase = np.float32(2.0 * math.pi) * (modes[:, None] * places[None, :] % length).astype(np.float32) / np.float32(length)
    norm = np.float32(math.sqrt(length))
    cosines = np.cos(phase) / norm
    sines = np.sin(phase) / norm
    forward = np.stack([np.stack([cosines, sines], -1), np.stack([-sines, cosines], -1)])
    forward = forward.reshape(2 * count, 2 * length).astype(ml_dtypes.bfloat16)
    return forward, np.ascontiguousarray(forward.T)


def lane_equals(rows, lanes, divide, offset):
    row = lax.broadcasted_iota(jnp.int32, (rows, lanes), 0)
    lane = lax.broadcasted_iota(jnp.int32, (rows, lanes), 1)
    return jnp.where(row - divide(lane) == offset, 1.0, 0.0).astype(BF16)


def start_all(pairs, sem):
    copies = [pltpu.make_async_copy(src, dst, sem.at[n]) for n, (src, dst) in enumerate(pairs)]
    for copy in copies:
        copy.start()
    return copies


def hbm():
    return pl.BlockSpec(memory_space=pltpu.HBM)


def in_hbm(*arrays):
    return [pltpu.with_memory_space_constraint(a, pltpu.HBM) for a in arrays]


def vmem():
    return pl.BlockSpec(memory_space=pltpu.VMEM)


def smem():
    return pl.BlockSpec(memory_space=pltpu.SMEM)


def scatter_rows(dst, sums, place, chips, half):
    tiles = half // LANES
    for s in range(2):
        for core in range(2):
            where = pl.ds(core * 8 + 2 * place + s, chips, stride=16)
            own = (3 * s + 2 * core) * chips
            shared = (3 * s + 1) * chips
            for k in range(2 * tiles):
                dst[k, where, :] = sums[own : own + chips, k * LANES : (k + 1) * LANES]
            for k in range(tiles):
                at = (core * tiles + k) * LANES
                dst[2 * tiles + k, where, :] = sums[shared : shared + chips, at : at + LANES]


def gather_rows(src, place, chips, half):
    tiles = half // LANES
    out = []
    for s in range(2):
        one = pl.ds(2 * place + s, chips, stride=16)
        two = pl.ds(8 + 2 * place + s, chips, stride=16)
        own = range(2 * tiles)
        shared = range(2 * tiles, 3 * tiles)
        out.append(jnp.concatenate([src[k, one, :] for k in own], axis=1))
        out.append(jnp.concatenate([src[k, w, :] for w in (one, two) for k in shared], axis=1))
        out.append(jnp.concatenate([src[k, two, :] for k in own], axis=1))
    return jnp.concatenate(out, axis=0).astype(BF16)


def cut_lanes(dst, src):
    for k in range(dst.shape[0]):
        dst[k] = src[:, k * LANES : (k + 1) * LANES].astype(F32)


def join_lanes(dst, src):
    for k in range(src.shape[0]):
        dst[:, k * LANES : (k + 1) * LANES] = src[k].astype(BF16)


def cut_shape(shape):
    return (shape[1] // LANES, shape[0], LANES)


def rows_to_modes(field, table, chips, half):
    rows, length, width = field.shape
    shape = (chips * 16, 3 * half)

    def kernel(u_hbm, t_hbm, out_hbm, u_ref, t_ref, scr, out_ref, sem, out_sem):
        copies = start_all([(t_hbm, t_ref)] + [(u_hbm.at[x], u_ref.at[x]) for x in range(rows)], sem)
        copies[0].wait()
        for x in range(rows):
            copies[1 + x].wait()
            scatter_rows(scr, dot(t_ref[...], u_ref[x]), x, chips, half)
        join_lanes(out_ref, scr)
        copy = pltpu.make_async_copy(out_ref, out_hbm, out_sem)
        copy.start()
        copy.wait()

    return pl.pallas_call(
        kernel,
        in_specs=[hbm(), hbm()],
        out_specs=hbm(),
        out_shape=pltpu.HBM(shape, BF16),
        scratch_shapes=[
            pltpu.VMEM(field.shape, BF16),
            pltpu.VMEM(table.shape, BF16),
            pltpu.VMEM(cut_shape(shape), F32),
            pltpu.VMEM(shape, BF16),
            pltpu.SemaphoreType.DMA((1 + rows,)),
            pltpu.SemaphoreType.DMA,
        ],
        compiler_params=params(),
        cost_estimate=cost(2 * table.size * rows * width, field.size * 2),
        name="rows_to_modes",
    )(*in_hbm(field, table))


def prepare(me, weights, local_weight, bias, tables, chips, half):
    modes_x, modes_y, full2 = weights.shape
    chans = local_weight.shape[0]
    tiles = full2 // LANES
    rows = 4 * modes_x
    groups = full2 // 2 // LANES
    batch = 6

    count = len(tables)

    def kernel(me_ref, w_hbm, l_ref, b_ref, *refs):
        tables_hbm, (plain_ref, turned_ref, block_ref, block_t_ref, bias_ref) = refs[:count], refs[count : count + 5]
        tables_ref, (w_ref, scr, pick, one, two, sem, table_sem) = refs[count + 5 : 2 * count + 5], refs[2 * count + 5 :]
        table_copies = start_all(list(zip(tables_hbm, tables_ref)), table_sem)
        cuts = [pl.ds(j, batch) for j in range(0, modes_x, batch)]
        copies = start_all([(w_hbm.at[cut], w_ref.at[cut]) for cut in cuts], sem)

        spread = lane_equals(chans, half, lambda l: l % chans, 0)
        row = lax.broadcasted_iota(jnp.int32, (half, half), 0) // chans
        lane = lax.broadcasted_iota(jnp.int32, (half, half), 1) // chans
        local = l_ref[...]
        for ref, dims in ((block_ref, 1), (block_t_ref, 0)):
            wide = lax.dot_general(local, spread, (((dims,), (0,)), ((), ())), preferred_element_type=F32)
            wide = jnp.concatenate([wide] * (half // chans), axis=0)
            ref[...] = jnp.where(row == lane, wide, 0.0).astype(BF16)
        value = jnp.concatenate([b_ref[...]] * 8, axis=0)
        high = value.astype(BF16)
        mid = (value - high.astype(F32)).astype(BF16)
        low = (value - high.astype(F32) - mid.astype(F32)).astype(BF16)
        wide = dot(high, spread) + dot(mid, spread) + dot(low, spread)
        bias_ref[...] = jnp.concatenate([wide, wide], axis=1)

        for n, first in enumerate(range(0, modes_x, batch)):
            copies[n].wait()
            for j in range(first, first + batch):
                for k in range(tiles):
                    scr[k, j * modes_y : (j + 1) * modes_y, :] = w_ref[j, :, k * LANES : (k + 1) * LANES].astype(F32)
        chip, core = me_ref[0] // 2, me_ref[0] % 2
        for w, mode in enumerate((chip + 2 * chips * core, chip + chips)):
            for k in range(tiles):
                s, g = divmod(k, groups)
                base = (2 * w + s) * modes_x
                pick[g, base : base + modes_x, :] = scr[k, pl.ds(mode, modes_x, stride=modes_y), :]
        per = LANES // chans
        repeat = jnp.concatenate(
            [lane_equals(LANES, LANES, lambda l: l % chans, chans * g) for g in range(per)], axis=1
        )
        pad = jnp.zeros((LANES - rows, LANES), F32)
        for g in range(groups):
            plain_ref[g] = dot(pick[g].astype(BF16), repeat).astype(BF16)
            one[g * LANES : (g + 1) * LANES, :] = jnp.transpose(jnp.concatenate([pick[g], pad]))
        for b in range(chans):
            two[b * chans : (b + 1) * chans, :] = one[pl.ds(b, chans, stride=chans), :]
        for g in range(groups):
            part = jnp.transpose(two[g * LANES : (g + 1) * LANES, :])[0:rows]
            turned_ref[g] = dot(part.astype(BF16), repeat).astype(BF16)
        for copy in table_copies:
            copy.wait()

    shape = (groups, rows, LANES * LANES // chans)
    wide = jax.ShapeDtypeStruct(shape, BF16)
    block = jax.ShapeDtypeStruct((half, half), BF16)
    held = tuple(jax.ShapeDtypeStruct(t.shape, t.dtype) for t in tables)
    return pl.pallas_call(
        kernel,
        in_specs=[smem(), hbm(), vmem(), vmem()] + [hbm()] * count,
        out_specs=(vmem(),) * (5 + count),
        out_shape=(wide, wide, block, block, jax.ShapeDtypeStruct((8, 2 * half), F32)) + held,
        scratch_shapes=[
            pltpu.VMEM(weights.shape, BF16),
            pltpu.VMEM((tiles, modes_x * modes_y, LANES), F32),
            pltpu.VMEM((groups, rows, LANES), F32),
            pltpu.VMEM((full2 // 2, LANES), F32),
            pltpu.VMEM((full2 // 2, LANES), F32),
            pltpu.SemaphoreType.DMA((modes_x // batch,)),
            pltpu.SemaphoreType.DMA((count,)),
        ],
        compiler_params=params(),
        cost_estimate=cost(1000000, 4 * 1024 * 1024),
        name="prepare",
    )(me, *in_hbm(weights), local_weight, bias, *in_hbm(*tables))


def weigh(spec, w_ref, chans, modes_x, adjoint):
    tiles = spec.shape[1] // LANES
    groups = LANES // chans
    stack = jnp.concatenate([spec[:, k * LANES : (k + 1) * LANES] for k in range(tiles)], axis=0)
    real = [None] * tiles
    imag = [None] * tiles
    for pair in range(chans // 2):
        two = [lane_equals(LANES, LANES, lambda l: l // chans * chans, c) for c in (2 * pair, 2 * pair + 1)]
        wide_rows = dot(stack, jnp.concatenate(two, axis=1))
        for c in (2 * pair, 2 * pair + 1):
            lanes = slice((c % 2) * LANES, (c % 2 + 1) * LANES)
            wl = slice((c % groups) * LANES, (c % groups + 1) * LANES)
            for own in range(2):
                base = 2 * own * modes_x
                wr = w_ref[c // groups, base : base + modes_x, wl].astype(F32)
                wi = w_ref[c // groups, base + modes_x : base + 2 * modes_x, wl].astype(F32)
                for k in range(0, 2 * tiles // 3) if own == 0 else range(2 * tiles // 3, tiles):
                    xr = wide_rows[2 * k * modes_x : (2 * k + 1) * modes_x, lanes]
                    xi = wide_rows[(2 * k + 1) * modes_x : (2 * k + 2) * modes_x, lanes]
                    if adjoint:
                        r, i = xr * wr + xi * wi, xi * wr - xr * wi
                    else:
                        r, i = xr * wr - xi * wi, xr * wi + xi * wr
                    real[k] = r if real[k] is None else real[k] + r
                    imag[k] = i if imag[k] is None else imag[k] + i
    return jnp.concatenate([jnp.concatenate(real, axis=1), jnp.concatenate(imag, axis=1)], axis=0).astype(BF16)


def mode_step(pencil, spread_w, forward, inverse, field, cotangent, chans):
    modes_x = forward.shape[0] // 2

    def kernel(p_ref, w_ref, f_ref, i_ref, u_hbm, c_hbm, spec_ref, out_ref, u_ref, c_ref, sem):
        copies = start_all([(u_hbm.at[0], u_ref), (c_hbm.at[0], c_ref)], sem)
        spec = dot(f_ref[...], p_ref[...]).astype(BF16)
        spec_ref[...] = spec
        mixed = weigh(spec, w_ref, chans, modes_x, False)
        out_ref[...] = dot(i_ref[...], mixed).astype(BF16)
        for copy in copies:
            copy.wait()

    return pl.pallas_call(
        kernel,
        in_specs=[vmem()] * 4 + [hbm()] * 2,
        out_specs=(vmem(),) * 4,
        out_shape=(
            jax.ShapeDtypeStruct((2 * modes_x, pencil.shape[1]), BF16),
            jax.ShapeDtypeStruct(pencil.shape, BF16),
            jax.ShapeDtypeStruct(field.shape[1:], BF16),
            jax.ShapeDtypeStruct(field.shape[1:], BF16),
        ),
        scratch_shapes=[pltpu.SemaphoreType.DMA((2,))],
        compiler_params=params(),
        cost_estimate=cost(2 * 48 * 6 * 128 * 4096, spread_w.size * 4),
        name="mode_step",
    )(pencil, spread_w, forward, inverse, *in_hbm(field, cotangent))


def adjoint_step(grads, spread_w, inverse, chans):
    modes_x = grads.shape[0] // 2
    shape = (inverse.shape[0], grads.shape[1])

    def kernel(g_ref, w_ref, i_ref, out_hbm, out_ref, out_sem):
        mixed = weigh(g_ref[...], w_ref, chans, modes_x, True)
        out_ref[...] = dot(i_ref[...], mixed).astype(BF16)
        copy = pltpu.make_async_copy(out_ref, out_hbm, out_sem)
        copy.start()
        copy.wait()

    return pl.pallas_call(
        kernel,
        in_specs=[vmem()] * 3,
        out_specs=hbm(),
        out_shape=pltpu.HBM(shape, BF16),
        scratch_shapes=[pltpu.VMEM(shape, BF16), pltpu.SemaphoreType.DMA],
        compiler_params=params(),
        cost_estimate=cost(2 * 48 * 6 * 128 * 4096, spread_w.size * 4),
        name="adjoint_step",
    )(grads, spread_w, inverse)


def pointwise(field, cotangent, first_rows, pencil, table_t, table, block_weight, bias_row, chips, half):
    rows, length, width = field.shape
    chunk, sub = 128, 16
    modes = table.shape[0]
    depth = table_t.shape[1]

    def kernel(
        u_hbm, c_hbm, u_first, c_first, p_ref, tt_ref, t_ref, w_ref, b_ref, out_hbm, dpre_hbm, send_hbm,
        u_rest, c_rest, out_ref, dpre_ref, send_ref, bscr, dscr, sem, out_sem,
    ):
        copies = []
        for x in range(1, rows):
            pairs = [(u_hbm.at[x], u_rest.at[x - 1]), (c_hbm.at[x], c_rest.at[x - 1])]
            copies.append(start_all(pairs, sem.at[x - 1]))
        cut_lanes(bscr, p_ref)
        root = math.sqrt(2.0 / math.pi)
        bias = b_ref[0:1, :]
        high = bias.astype(BF16)
        mid = (bias - high.astype(F32)).astype(BF16)
        low = (bias - high.astype(F32) - mid.astype(F32)).astype(BF16)
        parts = [t.astype(F32) for t in (high, mid, low)]
        bias = jnp.concatenate(parts + [jnp.zeros((depth - modes - 3, width), F32)], axis=0)
        bias = (0.5 * bias).astype(BF16)
        weight = (0.5 * w_ref[...].astype(F32)).astype(BF16)

        def one_row(x):
            if x > 0:
                for copy in copies[x - 1]:
                    copy.wait()
            u_ref = u_rest.at[x - 1] if x > 0 else u_first
            c_ref = c_rest.at[x - 1] if x > 0 else c_first
            coeff = (0.5 * gather_rows(bscr, x, chips, half).astype(F32)).astype(BF16)
            coeff = jnp.concatenate([coeff, bias], axis=0)
            for k in range(length // chunk):
                where = pl.ds(k * chunk, chunk)
                for h in range(2):
                    lanes = slice(h * half, (h + 1) * half)
                    left = jnp.concatenate([u_ref[where, lanes], tt_ref[where, :]], axis=1)
                    right = jnp.concatenate([weight, coeff[:, lanes]], axis=0)
                    halved = dot(left, right)
                    for at in range(0, chunk, sub):
                        place = pl.ds(k * chunk + at, sub)
                        p = halved[at : at + sub]
                        inner = p * (2.0 * root + (8.0 * root * 0.044715) * (p * p))
                        th = jnp.tanh(inner)
                        twice = 1.0 + th
                        out_ref[x, place, lanes] = (p * twice).astype(BF16)
                        slope = 1.5 * inner - (2.0 * root) * p
                        grad = twice * (0.5 + (1.0 - th) * slope)
                        dpre_ref[x, place, lanes] = (c_ref[place, lanes].astype(F32) * grad).astype(BF16)
            pltpu.make_async_copy(out_ref.at[x], out_hbm.at[x], out_sem.at[x]).start()
            pltpu.make_async_copy(dpre_ref.at[x], dpre_hbm.at[x], out_sem.at[rows + x]).start()
            scatter_rows(dscr, dot(t_ref[...], dpre_ref[x]), x, chips, half)

        for x in range(rows):
            one_row(x)
        join_lanes(send_ref, dscr)
        pltpu.make_async_copy(send_ref, send_hbm, out_sem.at[2 * rows]).start()
        for x in range(rows):
            pltpu.make_async_copy(out_ref.at[x], out_hbm.at[x], out_sem.at[x]).wait()
            pltpu.make_async_copy(dpre_ref.at[x], dpre_hbm.at[x], out_sem.at[rows + x]).wait()
        pltpu.make_async_copy(send_ref, send_hbm, out_sem.at[2 * rows]).wait()

    return pl.pallas_call(
        kernel,
        in_specs=[hbm(), hbm()] + [vmem()] * 7,
        out_specs=(hbm(), hbm(), hbm()),
        out_shape=(
            pltpu.HBM(field.shape, BF16),
            pltpu.HBM(field.shape, BF16),
            pltpu.HBM(pencil.shape, BF16),
        ),
        scratch_shapes=[
            pltpu.VMEM((rows - 1, length, width), BF16),
            pltpu.VMEM((rows - 1, length, width), BF16),
            pltpu.VMEM(field.shape, BF16),
            pltpu.VMEM(field.shape, BF16),
            pltpu.VMEM(pencil.shape, BF16),
            pltpu.VMEM(cut_shape(pencil.shape), F32),
            pltpu.VMEM(cut_shape(pencil.shape), F32),
            pltpu.SemaphoreType.DMA((rows - 1, 2)),
            pltpu.SemaphoreType.DMA((2 * rows + 1,)),
        ],
        compiler_params=params(),
        cost_estimate=cost(field.size * 1000, field.size * 8),
        name="pointwise",
    )(*in_hbm(field, cotangent), *first_rows, pencil, table_t, table, block_weight, bias_row)


def local_sums(field, dpre, chans, half):
    rows, length, width = field.shape
    slices = half // chans

    def kernel(u_hbm, d_hbm, out_ref, u_ref, d_ref, sem):
        copies = start_all(
            [(u_hbm.at[x], u_ref.at[x]) for x in range(rows)] + [(d_hbm.at[x], d_ref.at[x]) for x in range(rows)], sem
        )
        both = bias = None
        ones = jnp.ones((16, length), BF16)
        for x in range(rows):
            copies[x].wait()
            copies[rows + x].wait()
            for h in range(2):
                lanes = slice(h * half, (h + 1) * half)
                part = lax.dot_general(
                    u_ref[x, :, lanes], d_ref[x, :, lanes], (((0,), (0,)), ((), ())), preferred_element_type=F32
                )
                both = part if both is None else both + part
            part = dot(ones, d_ref[x])[0:8]
            bias = part if bias is None else bias + part
        group = lax.broadcasted_iota(jnp.int32, (chans, half), 1) // chans
        total = jnp.zeros((chans, half), F32)
        for p in range(slices):
            total = jnp.where(group == p, both[p * chans : (p + 1) * chans], total)
        total = sum(total[:, k * LANES : (k + 1) * LANES] for k in range(half // LANES))
        bias = sum(bias[:, k * LANES : (k + 1) * LANES] for k in range(width // LANES))
        shift = LANES // 2
        while shift >= chans:
            total = total + pltpu.roll(total, shift, 1)
            bias = bias + pltpu.roll(bias, shift, 1)
            shift //= 2
        group8 = lax.broadcasted_iota(jnp.int32, (8, LANES), 1) // chans
        folded = jnp.zeros((8, LANES), F32)
        for k in range(chans // 8):
            folded = jnp.where(group8 == k, total[8 * k : 8 * k + 8], folded)
        value = jnp.concatenate([folded, bias], axis=0)
        high = value.astype(BF16).astype(F32)
        mid = (value - high).astype(BF16).astype(F32)
        low = value - high - mid
        left = jnp.concatenate([high, mid[0:8]], axis=0)
        right = jnp.concatenate([mid[8:16], low], axis=0)
        out_ref[...] = jnp.concatenate([left, right], axis=1).astype(BF16)

    return pl.pallas_call(
        kernel,
        in_specs=[hbm(), hbm()],
        out_specs=vmem(),
        out_shape=jax.ShapeDtypeStruct((24, 2 * LANES), BF16),
        scratch_shapes=[
            pltpu.VMEM(field.shape, BF16),
            pltpu.VMEM(field.shape, BF16),
            pltpu.SemaphoreType.DMA((2 * rows,)),
        ],
        compiler_params=params(),
        cost_estimate=cost(field.size * 1000, field.size * 4),
        name="local_sums",
    )(*in_hbm(field, dpre))


def weight_sums(spectrum, pencil, forward, chans):
    modes_x = spectrum.shape[0] // 2
    tiles = spectrum.shape[1] // LANES
    groups = LANES // chans
    step = 2 * LANES
    full = chans * chans
    parts = full // step

    def kernel(u_ref, p_ref, f_ref, d_ref, own_ref, shared_ref):
        def stack(ref):
            return jnp.concatenate([ref[:, k * LANES : (k + 1) * LANES] for k in range(tiles)], axis=0)

        left = stack(u_ref)
        d_ref[...] = dot(f_ref[...], p_ref[...]).astype(BF16)
        repeat = jnp.concatenate(
            [lane_equals(LANES, LANES, lambda l: l % chans, chans * g) for g in range(groups)], axis=1
        )
        right = dot(stack(d_ref), repeat)
        for a in range(parts):
            sums = {}
            for g in range(groups):
                pick = lane_equals(LANES, step, lambda l: l // chans, g * chans + a * (step // chans))
                spread_u = dot(left, pick)
                for k in range(tiles):
                    kind = 0 if k < 2 * tiles // 3 else 1
                    re = slice(2 * k * modes_x, (2 * k + 1) * modes_x)
                    im = slice((2 * k + 1) * modes_x, (2 * k + 2) * modes_x)
                    for z in range(2):
                        lanes = slice(z * LANES, (z + 1) * LANES)
                        ur, ui = spread_u[re, lanes], spread_u[im, lanes]
                        dr = right[re, g * LANES : (g + 1) * LANES]
                        di = right[im, g * LANES : (g + 1) * LANES]
                        for t, term in ((0, ur * dr + ui * di), (1, ur * di - ui * dr)):
                            key = (kind, t, z)
                            sums[key] = term if key not in sums else sums[key] + term
            for t in range(2):
                lanes = slice(t * full + a * step, t * full + (a + 1) * step)
                own_ref[:, lanes] = jnp.concatenate([sums[0, t, 0], sums[0, t, 1]], axis=1).astype(BF16)
                shared_ref[:, lanes] = jnp.concatenate([sums[1, t, 0], sums[1, t, 1]], axis=1)

    return pl.pallas_call(
        kernel,
        in_specs=[vmem()] * 3,
        out_shape=(
            jax.ShapeDtypeStruct(spectrum.shape, BF16),
            jax.ShapeDtypeStruct((modes_x, 2 * full), BF16),
            jax.ShapeDtypeStruct((modes_x, 2 * full), F32),
        ),
        compiler_params=params(),
        cost_estimate=cost(2 * 288 * 128 * 4096, 4 * 1024 * 1024),
        name="weight_sums",
    )(spectrum, pencil, forward)


def make_shard(me, own, shared, other, stats):
    rows, full2 = own.shape
    full = full2 // 2
    half = full // 2
    width = full2 + full + stats.shape[1]

    def kernel(me_ref, o_ref, s_ref, r_ref, st_ref, out_ref):
        first = me_ref[0] % 2 == 0
        out_ref[:, 0:full2] = o_ref[...]
        for t in range(2):
            low = slice(t * full, t * full + half)
            high = slice(t * full + half, (t + 1) * full)
            mine = jnp.where(first, s_ref[:, low], s_ref[:, high])
            theirs = jnp.where(first, r_ref[:, low], r_ref[:, high])
            out_ref[:, full2 + t * half : full2 + (t + 1) * half] = (mine + theirs).astype(BF16)
        out_ref[:, full2 + full :] = st_ref[...]

    return pl.pallas_call(
        kernel,
        in_specs=[smem()] + [vmem()] * 4,
        out_shape=jax.ShapeDtypeStruct((rows, width), BF16),
        compiler_params=params(),
        cost_estimate=cost(100000, 1000000),
        name="make_shard",
    )(me, own, shared, other, stats)


def ring_chip(spot, chips):
    return jnp.where(spot < chips // 2, 2 * spot, 2 * (chips - 1 - spot) + 1)


def ring_spot(chip, chips):
    return jnp.where(chip % 2 == 0, chip // 2, chips - 1 - chip // 2)


def read_sums(ref, full):
    left = ref[:, 3 * full : 3 * full + LANES].astype(F32)
    right = ref[:, 3 * full + LANES : 3 * full + 2 * LANES].astype(F32)
    middle = jnp.concatenate([left[16:24], right[0:8]], axis=0)
    return left[0:16] + middle + right[8:24]


def early_sums(shards_all, chans):
    count = len(shards_all)
    shape = (count, 16, LANES)

    def kernel(*refs):
        ins, (out_hbm, out_ref, sem) = refs[:count], refs[count:]
        for n in range(count):
            out_ref[n] = read_sums(ins[n], chans * chans)
        copy = pltpu.make_async_copy(out_ref, out_hbm, sem)
        copy.start()
        copy.wait()

    return pl.pallas_call(
        kernel,
        in_specs=[vmem()] * count,
        out_specs=hbm(),
        out_shape=pltpu.HBM(shape, F32),
        scratch_shapes=[pltpu.VMEM(shape, F32), pltpu.SemaphoreType.DMA],
        compiler_params=params(),
        cost_estimate=cost(3 * 10**10, 4 * 1024 * 1024),
        name="early_sums",
    )(*shards_all)


def shard_places(me, turns, chips):
    spot = ring_spot(me // 2, chips)
    core = me % 2
    return [
        (ring_chip((spot + chips - back) % chips, chips), 1 - core if swapped else core) for back, swapped in turns
    ]


def place_tile(scr, refs, places, turns, k, modes_y, tiles):
    rows = scr.shape[1] // modes_y
    part = tiles // 4
    chips = modes_y // 3
    keeper = k % (2 * part) // part
    at = tiles + k // (2 * part) * part + k % part
    for n, (chip, core) in enumerate(places):
        own = pl.ds(chip + 2 * chips * core, rows, stride=modes_y)
        scr[k, own, :] = refs[n][:, k * LANES : (k + 1) * LANES].astype(F32)
        if turns[n][1]:
            continue
        mate = turns.index((turns[n][0], True))
        lanes = slice(at * LANES, (at + 1) * LANES)
        shared = pl.ds(chip + chips, rows, stride=modes_y)
        scr[k, shared, :] = jnp.where(core == keeper, refs[n][:, lanes], refs[mate][:, lanes]).astype(F32)


def assemble_first(me, shards_all, known, turns, modes_y, chans, chips):
    rows = shards_all[0].shape[0]
    count = len(shards_all)
    tiles = 2 * chans * chans // LANES

    def kernel(me_ref, *refs):
        places = shard_places(me_ref[0], turns, chips)
        for k in range(tiles):
            place_tile(refs[count], refs[:count], places, turns, k, modes_y, tiles)
        for n in range(known, count):
            refs[count + 1][n - known] = read_sums(refs[n], chans * chans)

    return pl.pallas_call(
        kernel,
        in_specs=[smem()] + [vmem()] * count,
        out_specs=(vmem(), vmem()),
        out_shape=(
            jax.ShapeDtypeStruct((tiles, rows * modes_y, LANES), F32),
            jax.ShapeDtypeStruct((count - known, 16, LANES), F32),
        ),
        compiler_params=params(),
        cost_estimate=cost(1000000, 4 * 1024 * 1024),
        name="assemble_first",
    )(me, *shards_all)


def assemble(me, scr, early, more, shards_all, turns, modes_y, chans, chips):
    rows = shards_all[0].shape[0]
    full = chans * chans
    tiles = 2 * full // LANES
    count = len(shards_all)
    total_count = len(turns)
    before = total_count - count
    known = early.shape[0]

    def kernel(me_ref, scr_in, e_hbm, m_ref, *refs):
        ins, (scr, g_ref, l_ref, b_ref, stat, out, e_ref, sem) = refs[:count], refs[count:]
        fetch = pltpu.make_async_copy(e_hbm, e_ref, sem.at[tiles // 4])
        fetch.start()
        places = shard_places(me_ref[0], turns, chips)
        copies = []
        for k in range(tiles):
            place_tile(scr, ins, places[before:], turns[before:], k, modes_y, tiles)
            lanes = slice(k * LANES, (k + 1) * LANES)
            for j in range(rows):
                out[j, :, lanes] = scr[k, j * modes_y : (j + 1) * modes_y, :].astype(BF16)
            if k % 4 == 3:
                lanes = pl.ds((k - 3) * LANES, 4 * LANES)
                copies.append(pltpu.make_async_copy(out.at[:, :, lanes], g_ref.at[:, :, lanes], sem.at[k // 4]))
                copies[-1].start()
        fetch.wait()
        for n, (chip, core) in enumerate(places):
            if n < known:
                stat[2 * chip + core] = e_ref[n]
            elif n < before:
                stat[2 * chip + core] = m_ref[n - known]
            else:
                stat[2 * chip + core] = read_sums(ins[n - before], full)
        total = stat[0]
        for n in range(1, total_count):
            total = total + stat[n]
        for k in range(chans // 8):
            piece = total[0:8] if k == 0 else pltpu.roll(total[0:8], LANES - k * chans, 1)
            l_ref[8 * k : 8 * k + 8, :] = piece[:, 0:chans]
        b_ref[...] = total[8:9, 0:chans]
        for copy in copies:
            copy.wait()

    shape = (rows, modes_y, 2 * full)
    return pl.pallas_call(
        kernel,
        in_specs=[smem(), vmem(), hbm(), vmem()] + [vmem()] * count,
        out_specs=(vmem(), hbm(), vmem(), vmem()),
        out_shape=(
            jax.ShapeDtypeStruct(scr.shape, F32),
            pltpu.HBM(shape, BF16),
            jax.ShapeDtypeStruct((chans, chans), F32),
            jax.ShapeDtypeStruct((1, chans), F32),
        ),
        input_output_aliases={1: 0},
        scratch_shapes=[
            pltpu.VMEM((total_count, 16, LANES), F32),
            pltpu.VMEM(shape, BF16),
            pltpu.VMEM(early.shape, F32),
            pltpu.SemaphoreType.DMA((tiles // 4 + 1,)),
        ],
        compiler_params=params(),
        cost_estimate=cost(1000000, 8 * 1024 * 1024),
        name="assemble",
    )(me, scr, *in_hbm(early), more, *shards_all)[1:]


def back_to_field(dpre, pencil, table_t, block_weight, chips, half):
    rows, length, width = dpre.shape
    chunk = 128

    def kernel(d_hbm, p_ref, tt_ref, w_ref, out_hbm, d_ref, out_ref, bscr, sem, out_sem):
        copies = start_all([(d_hbm.at[x], d_ref.at[x]) for x in range(rows)], sem)
        cut_lanes(bscr, p_ref)
        out_copies = []
        for x in range(rows):
            copies[x].wait()
            coeff = gather_rows(bscr, x, chips, half)
            for k in range(length // chunk):
                where = pl.ds(k * chunk, chunk)
                d = d_ref[x, where, :]
                spec = dot(tt_ref[where, :], coeff)
                for h in range(2):
                    lanes = slice(h * half, (h + 1) * half)
                    out_ref[x, where, lanes] = (spec[:, lanes] + dot(d[:, lanes], w_ref[...])).astype(BF16)
            out_copies.append(pltpu.make_async_copy(out_ref.at[x], out_hbm.at[x], out_sem.at[x]))
            out_copies[-1].start()
        for copy in out_copies:
            copy.wait()

    return pl.pallas_call(
        kernel,
        in_specs=[hbm()] + [vmem()] * 3,
        out_specs=hbm(),
        out_shape=pltpu.HBM(dpre.shape, BF16),
        scratch_shapes=[
            pltpu.VMEM(dpre.shape, BF16),
            pltpu.VMEM(dpre.shape, BF16),
            pltpu.VMEM(cut_shape(pencil.shape), F32),
            pltpu.SemaphoreType.DMA((rows,)),
            pltpu.SemaphoreType.DMA((rows,)),
        ],
        compiler_params=params(),
        cost_estimate=cost(dpre.size * 500, dpre.size * 4),
        name="back_to_field",
    )(*in_hbm(dpre), pencil, table_t, block_weight)


def exchange(pencil):
    return lax.all_to_all(pencil, "xy", split_axis=0, concat_axis=0, tiled=True)


class Ring:
    def __init__(self, shard, chips):
        order = [ring_chip_int(i, chips) for i in range(chips)]
        self.chips = chips
        self.hops = {
            way: [(2 * order[i] + c, 2 * order[(i + way) % chips] + c) for i in range(chips) for c in range(2)]
            for way in (1, -1)
        }
        self.swap = [(i, i ^ 1) for i in range(2 * chips)]
        self.step = 0
        self.ahead = self.back = shard
        self.parts, self.turns = [], []
        self.keep(shard, 0)

    def keep(self, piece, turn):
        self.parts.append(piece)
        self.turns.append((turn, False))
        self.parts.append(lax.ppermute(piece, "xy", self.swap))
        self.turns.append((turn, True))

    def hop(self):
        self.step += 1
        self.ahead = lax.ppermute(self.ahead, "xy", self.hops[1])
        if self.step < self.chips // 2:
            self.back = lax.ppermute(self.back, "xy", self.hops[-1])

    def settle(self):
        self.keep(self.ahead, self.step)
        if self.step < self.chips // 2:
            self.keep(self.back, self.chips - self.step)

    def tie(self, other):
        self.ahead, self.back, other = lax.optimization_barrier((self.ahead, self.back, other))
        return other

    def hold(self, other):
        self.ahead, other = lax.optimization_barrier((self.ahead, other))
        return other


def ring_chip_int(spot, chips):
    return 2 * spot if spot < chips // 2 else 2 * (chips - 1 - spot) + 1


def fast_shards(field, spectral_weight, local_weight, bias, cotangent):
    rows, length_y, width = field.shape
    chans = local_weight.shape[0]
    planes = width // chans
    modes_x, modes_y = spectral_weight.shape[:2]
    devices = lax.axis_size("xy")
    chips = devices // 2
    half = width // 2
    me = lax.axis_index("xy")
    table_y = np_ytable(modes_y, length_y, False)
    table_yw = np_ytable(modes_y, length_y, True)
    table_y_t, table_yw_t = (np.ascontiguousarray(t.T) for t in (table_y, table_yw))
    ones = np.ones((length_y, 3), table_yw_t.dtype)
    zeros = np.zeros((length_y, -(table_yw_t.shape[1] + 3) % 16), table_yw_t.dtype)
    table_yw_t = np.concatenate([table_yw_t, ones, zeros], axis=1)
    forward, inverse = np_xtables(modes_x, rows * devices)
    me_id = me.astype(jnp.int32)[None]

    send = rows_to_modes(field, table_y, chips, half)
    pencil = exchange(send)
    tables = [jnp.asarray(t) for t in (forward, inverse, table_yw_t, table_yw, table_y_t)]
    plain, turned, block, block_t, bias_row, *tables = prepare(
        me_id, spectral_weight, local_weight, bias[None, :], tables, chips, half
    )
    forward, inverse, table_yw_t, table_yw, table_y_t = tables
    spectrum, send, *first_rows = mode_step(pencil, plain, forward, inverse, field, cotangent, chans)
    pencil = exchange(send)
    output_field, dpre, send = pointwise(
        field, cotangent, first_rows, pencil, table_yw_t, table_yw, block, bias_row, chips, half
    )
    pencil = exchange(send)
    stats = local_sums(field, dpre, chans, half)
    pencil, stats = lax.optimization_barrier((pencil, stats))
    grads, own, shared = weight_sums(spectrum, pencil, forward, chans)
    other = lax.ppermute(shared, "xy", [(i, i ^ 1) for i in range(devices)])
    shard = make_shard(me_id, own, shared, other, stats)

    ring = Ring(shard, chips)
    grads = ring.tie(grads)
    ring.hop()
    send = adjoint_step(grads, turned, inverse, chans)
    send = ring.tie(send)
    ring.settle()
    first = list(ring.parts)
    ring.hop()
    pencil = exchange(send)
    ring.settle()
    early, turns = list(ring.parts), list(ring.turns)
    sums = early_sums(first, chans)
    sums = ring.tie(sums)
    ring.hop()
    pencil, sums = lax.optimization_barrier((pencil, sums))
    ring.settle()
    ring.hop()
    field_grad = back_to_field(dpre, pencil, table_y_t, block_t, chips, half)
    early[0], field_grad = lax.optimization_barrier((early[0], field_grad))
    scr, more = assemble_first(me_id, early, len(first), turns, modes_y, chans, chips)
    scr = ring.hold(scr)
    ring.settle()
    late = ring.parts[len(early) :]
    spectral_grad, local_grad, bias_grad = assemble(
        me_id, scr, sums, more, late, ring.turns, modes_y, chans, chips
    )
    return output_field, field_grad, spectral_grad, local_grad, bias_grad.reshape(chans)


def fits(field, spectral_weight, local_weight, devices):
    rows, length_y, width = field.shape
    chans = local_weight.shape[0]
    modes_x, modes_y = spectral_weight.shape[:2]
    return (
        rows == 4
        and chans == 32
        and width == 512
        and length_y % 128 == 0
        and modes_x == 24
        and devices == 16
        and 2 * modes_y == 3 * devices
    )


def shards(field, spectral_weight, local_weight, bias, cotangent):
    if fits(field, spectral_weight, local_weight, lax.axis_size("xy")):
        return fast_shards(field, spectral_weight, local_weight, bias, cotangent)
    return general_shards(field, spectral_weight, local_weight, bias, cotangent)


def solution(mesh):
    return jax.shard_map(
        shards,
        mesh=mesh,
        in_specs=(P(("groups", "xy"), None, None), P(), P(), P(), P(("groups", "xy"), None, None)),
        out_specs=(
            P(("groups", "xy"), None, None),
            P(("groups", "xy"), None, None),
            P("groups", None, None),
            P("groups", None),
            P("groups"),
        ),
        check_vma=False,
    )
```

```python
import math

import jax
import jax.numpy as jnp
import ml_dtypes
import numpy as np
from jax import lax
from jax.experimental import pallas as pl
from jax.experimental.pallas import tpu as pltpu
from jax.sharding import PartitionSpec as P


def ytable(count, length, weighted):
    modes = jnp.arange(count, dtype=jnp.int32)
    places = jnp.arange(length, dtype=jnp.int32)
    phase = 2.0 * math.pi * (modes[:, None] * places[None, :] % length).astype(jnp.float32) / length
    factor = (
        jnp.where(modes == 0, 1.0, 2.0).astype(jnp.float32)
        if weighted
        else jnp.ones((count,), jnp.float32)
    )
    scale = factor[:, None] / math.sqrt(length)
    return jnp.stack([scale * jnp.cos(phase), -scale * jnp.sin(phase)]).astype(jnp.bfloat16)


def xtable(count, length, places):
    index = jnp.arange(count, dtype=jnp.int32)
    modes = jnp.where(index < count // 2, index, length - count + index)
    phase = 2.0 * math.pi * (modes[:, None] * places[None, :] % length).astype(jnp.float32) / length
    return (jnp.stack([jnp.cos(phase), jnp.sin(phase)]) / math.sqrt(length)).astype(jnp.bfloat16)


def mult(form, left, right):
    return jnp.einsum(form, left, right, preferred_element_type=jnp.float32)


def to_slab(flat, table, planes):
    rows = flat.shape[0]
    count = table.shape[1]
    chans = flat.shape[2] // planes
    coeff = mult("smy,xyq->xsmq", table, flat).astype(jnp.bfloat16)
    coeff = coeff.reshape(rows, 2, count, planes, chans).transpose(0, 2, 3, 1, 4)
    return coeff.reshape(rows, count * planes, 2 * chans)


def from_slab(slab, table, planes):
    rows = slab.shape[0]
    count = table.shape[1]
    chans = slab.shape[2] // 2
    spread = slab.reshape(rows, count, planes, 2, chans)
    return mult("smy,xmpsc->xypc", table, spread).reshape(rows, table.shape[2], planes * chans)


def forward_x(table, pencil):
    proj = mult("ajx,xnsc->ajnsc", table, pencil)
    real_part = proj[0, :, :, 0] + proj[1, :, :, 1]
    imag_part = proj[0, :, :, 1] - proj[1, :, :, 0]
    return jnp.stack([real_part, imag_part], axis=2).astype(jnp.bfloat16)


def inverse_x(table, modes):
    proj = mult("ajx,jnsc->axnsc", table, modes)
    real_part = proj[0, :, :, 0] - proj[1, :, :, 1]
    imag_part = proj[0, :, :, 1] + proj[1, :, :, 0]
    return jnp.stack([real_part, imag_part], axis=2).astype(jnp.bfloat16)


def mix_modes(spectrum, weights):
    real_part = mult("jnc,jnco->jno", spectrum[:, :, 0], weights[:, :, 0]) - mult(
        "jnc,jnco->jno", spectrum[:, :, 1], weights[:, :, 1]
    )
    imag_part = mult("jnc,jnco->jno", spectrum[:, :, 0], weights[:, :, 1]) + mult(
        "jnc,jnco->jno", spectrum[:, :, 1], weights[:, :, 0]
    )
    return jnp.stack([real_part, imag_part], axis=2).astype(jnp.bfloat16)


def adjoint_mix(grads, weights):
    real_part = mult("jnco,jno->jnc", weights[:, :, 0], grads[:, :, 0]) + mult(
        "jnco,jno->jnc", weights[:, :, 1], grads[:, :, 1]
    )
    imag_part = mult("jnco,jno->jnc", weights[:, :, 0], grads[:, :, 1]) - mult(
        "jnco,jno->jnc", weights[:, :, 1], grads[:, :, 0]
    )
    return jnp.stack([real_part, imag_part], axis=2).astype(jnp.bfloat16)


def pair_grad(spectrum, grads):
    real_part = mult("jmpc,jmpo->jmco", spectrum[:, :, :, 0], grads[:, :, :, 0]) + mult(
        "jmpc,jmpo->jmco", spectrum[:, :, :, 1], grads[:, :, :, 1]
    )
    imag_part = mult("jmpc,jmpo->jmco", spectrum[:, :, :, 0], grads[:, :, :, 1]) - mult(
        "jmpc,jmpo->jmco", spectrum[:, :, :, 1], grads[:, :, :, 0]
    )
    return jnp.stack([real_part, imag_part], axis=2)


def to_modes(slab, table_full):
    count = table_full.shape[1]
    pencil = lax.all_to_all(slab, "xy", split_axis=1, concat_axis=0, tiled=True)
    chans = pencil.shape[2] // 2
    items = pencil.shape[1]
    spread = pencil.reshape(pencil.shape[0], items, 2, chans)
    return forward_x(table_full, spread).reshape(count, items, 2 * chans)


def to_space(modes, table_full):
    count, pairs_dev, twice, chans = modes.shape
    pencil = inverse_x(table_full, modes)
    moved = lax.all_to_all(
        pencil.reshape(pencil.shape[0], pairs_dev, 2 * chans),
        "xy",
        split_axis=0,
        concat_axis=1,
        tiled=True,
    )
    return moved


def general_shards(field, spectral_weight, local_weight, bias, cotangent):
    rows, length_y, width_all = field.shape
    chans = local_weight.shape[0]
    planes = width_all // chans
    modes_x, modes_y = (spectral_weight.shape[0], spectral_weight.shape[1])
    devices = lax.axis_size("xy")
    length_x = rows * devices
    pairs_dev = modes_y * planes // devices
    offset = lax.axis_index("xy")
    table_y = ytable(modes_y, length_y, False)
    table_yw = ytable(modes_y, length_y, True)
    table_x = xtable(modes_x, length_x, jnp.arange(length_x, dtype=jnp.int32))
    weight_all = spectral_weight.reshape(modes_x, modes_y, 2, chans, chans)
    ky_index = (offset * pairs_dev + jnp.arange(pairs_dev, dtype=jnp.int32)) // planes
    weight_pairs = jnp.take(weight_all, ky_index, axis=1)
    spectrum = to_modes(to_slab(field, table_y, planes), table_x).reshape(
        modes_x, pairs_dev, 2, chans
    )
    mixed = mix_modes(spectrum, weight_pairs)
    spatial = from_slab(to_space(mixed, table_x), table_yw, planes)
    field4 = field.reshape(rows, length_y, planes, chans)
    local_term = mult("xypc,co->xypo", field4, local_weight)
    preact = spatial.reshape(rows, length_y, planes, chans) + local_term + bias
    output_field = jax.nn.gelu(preact).astype(jnp.bfloat16).reshape(rows, length_y, width_all)
    unused, pullback = jax.vjp(jax.nn.gelu, preact)
    grad_pre = pullback(cotangent.reshape(rows, length_y, planes, chans).astype(jnp.float32))[
        0
    ].astype(jnp.bfloat16)
    bias_part = jnp.sum(grad_pre.astype(jnp.float32), axis=(0, 1, 2))
    weight_part = mult("xypc,xypo->co", field4, grad_pre)
    back_local = mult("xypo,co->xypc", grad_pre, local_weight)
    grad_slab = to_slab(grad_pre.reshape(rows, length_y, width_all), table_yw, planes)
    grad_modes = to_modes(grad_slab, table_x).reshape(modes_x, pairs_dev, 2, chans)
    grad_spec = adjoint_mix(grad_modes, weight_pairs)
    back_spec = from_slab(to_space(grad_spec, table_x), table_y, planes)
    field_grad = (back_spec + back_local.reshape(rows, length_y, width_all)).astype(jnp.bfloat16)
    per_pair = pair_grad(
        spectrum.reshape(modes_x, pairs_dev, 1, 2, chans),
        grad_modes.reshape(modes_x, pairs_dev, 1, 2, chans),
    )
    onehot = (ky_index[:, None] == jnp.arange(modes_y, dtype=jnp.int32)[None, :]).astype(
        jnp.float32
    )
    partial_grad = jnp.einsum("jnsco,nm->jmsco", per_pair, onehot, precision=lax.Precision.HIGHEST)
    total, local_grad, bias_grad = lax.psum((partial_grad, weight_part, bias_part), "xy")
    spectral_grad = total.reshape(modes_x, modes_y, 2 * chans * chans).astype(jnp.bfloat16)
    return (output_field, field_grad, spectral_grad, local_grad, bias_grad)


F32 = jnp.float32
BF16 = jnp.bfloat16
LANES = 128
VMEM_LIMIT = 24 * 1024 * 1024


def dot(left, right):
    return jnp.dot(left, right, preferred_element_type=F32)


def params(**kwargs):
    return pltpu.CompilerParams(vmem_limit_bytes=VMEM_LIMIT, **kwargs)


def cost(flops, bytes_accessed):
    return pl.CostEstimate(flops=flops, bytes_accessed=bytes_accessed, transcendentals=0)


def np_ytable(count, length, weighted):
    modes = np.arange(count)
    places = np.arange(length)
    phase = np.float32(2.0 * math.pi) * (modes[:, None] * places[None, :] % length).astype(np.float32) / np.float32(length)
    factor = np.where(modes == 0, 1.0, 2.0).astype(np.float32) if weighted else np.ones((count,), np.float32)
    scale = (factor / np.float32(math.sqrt(length)))[:, None]
    both = np.stack([scale * np.cos(phase), -scale * np.sin(phase)]).astype(ml_dtypes.bfloat16)
    return both.reshape(2 * count, length)


def np_xtables(count, length):
    index = np.arange(count)
    modes = np.where(index < count // 2, index, length - count + index)
    places = np.arange(length)
    phase = np.float32(2.0 * math.pi) * (modes[:, None] * places[None, :] % length).astype(np.float32) / np.float32(length)
    norm = np.float32(math.sqrt(length))
    cosines = np.cos(phase) / norm
    sines = np.sin(phase) / norm
    forward = np.stack([np.stack([cosines, sines], -1), np.stack([-sines, cosines], -1)])
    forward = forward.reshape(2 * count, 2 * length).astype(ml_dtypes.bfloat16)
    return forward, np.ascontiguousarray(forward.T)


def lane_equals(rows, lanes, divide, offset):
    row = lax.broadcasted_iota(jnp.int32, (rows, lanes), 0)
    lane = lax.broadcasted_iota(jnp.int32, (rows, lanes), 1)
    return jnp.where(row - divide(lane) == offset, 1.0, 0.0).astype(BF16)


def start_all(pairs, sem):
    copies = [pltpu.make_async_copy(src, dst, sem.at[n]) for n, (src, dst) in enumerate(pairs)]
    for copy in copies:
        copy.start()
    return copies


def hbm():
    return pl.BlockSpec(memory_space=pltpu.HBM)


def in_hbm(*arrays):
    return [pltpu.with_memory_space_constraint(a, pltpu.HBM) for a in arrays]


def vmem():
    return pl.BlockSpec(memory_space=pltpu.VMEM)


def smem():
    return pl.BlockSpec(memory_space=pltpu.SMEM)


def scatter_rows(dst, sums, place, chips, half):
    tiles = half // LANES
    for s in range(2):
        for core in range(2):
            where = pl.ds(core * 8 + 2 * place + s, chips, stride=16)
            own = (3 * s + 2 * core) * chips
            shared = (3 * s + 1) * chips
            for k in range(2 * tiles):
                dst[k, where, :] = sums[own : own + chips, k * LANES : (k + 1) * LANES]
            for k in range(tiles):
                at = (core * tiles + k) * LANES
                dst[2 * tiles + k, where, :] = sums[shared : shared + chips, at : at + LANES]


def gather_rows(src, place, chips, half):
    tiles = half // LANES
    out = []
    for s in range(2):
        one = pl.ds(2 * place + s, chips, stride=16)
        two = pl.ds(8 + 2 * place + s, chips, stride=16)
        own = range(2 * tiles)
        shared = range(2 * tiles, 3 * tiles)
        out.append(jnp.concatenate([src[k, one, :] for k in own], axis=1))
        out.append(jnp.concatenate([src[k, w, :] for w in (one, two) for k in shared], axis=1))
        out.append(jnp.concatenate([src[k, two, :] for k in own], axis=1))
    return jnp.concatenate(out, axis=0).astype(BF16)


def cut_lanes(dst, src):
    for k in range(dst.shape[0]):
        dst[k] = src[:, k * LANES : (k + 1) * LANES].astype(F32)


def join_lanes(dst, src):
    for k in range(src.shape[0]):
        dst[:, k * LANES : (k + 1) * LANES] = src[k].astype(BF16)


def cut_shape(shape):
    return (shape[1] // LANES, shape[0], LANES)


def rows_to_modes(field, table, chips, half):
    rows, length, width = field.shape
    shape = (chips * 16, 3 * half)

    def kernel(u_hbm, t_hbm, out_hbm, u_ref, t_ref, scr, out_ref, sem, out_sem):
        copies = start_all([(t_hbm, t_ref)] + [(u_hbm.at[x], u_ref.at[x]) for x in range(rows)], sem)
        copies[0].wait()
        for x in range(rows):
            copies[1 + x].wait()
            scatter_rows(scr, dot(t_ref[...], u_ref[x]), x, chips, half)
        join_lanes(out_ref, scr)
        copy = pltpu.make_async_copy(out_ref, out_hbm, out_sem)
        copy.start()
        copy.wait()

    return pl.pallas_call(
        kernel,
        in_specs=[hbm(), hbm()],
        out_specs=hbm(),
        out_shape=pltpu.HBM(shape, BF16),
        scratch_shapes=[
            pltpu.VMEM(field.shape, BF16),
            pltpu.VMEM(table.shape, BF16),
            pltpu.VMEM(cut_shape(shape), F32),
            pltpu.VMEM(shape, BF16),
            pltpu.SemaphoreType.DMA((1 + rows,)),
            pltpu.SemaphoreType.DMA,
        ],
        compiler_params=params(),
        cost_estimate=cost(2 * table.size * rows * width, field.size * 2),
        name="rows_to_modes",
    )(*in_hbm(field, table))


def prepare(me, weights, local_weight, bias, tables, chips, half):
    modes_x, modes_y, full2 = weights.shape
    chans = local_weight.shape[0]
    tiles = full2 // LANES
    rows = 4 * modes_x
    groups = full2 // 2 // LANES
    batch = 6

    count = len(tables)

    def kernel(me_ref, w_hbm, l_ref, b_ref, *refs):
        tables_hbm, (plain_ref, turned_ref, block_ref, block_t_ref, bias_ref) = refs[:count], refs[count : count + 5]
        tables_ref, (w_ref, scr, pick, one, two, sem, table_sem) = refs[count + 5 : 2 * count + 5], refs[2 * count + 5 :]
        table_copies = start_all(list(zip(tables_hbm, tables_ref)), table_sem)
        cuts = [pl.ds(j, batch) for j in range(0, modes_x, batch)]
        copies = start_all([(w_hbm.at[cut], w_ref.at[cut]) for cut in cuts], sem)

        spread = lane_equals(chans, half, lambda l: l % chans, 0)
        row = lax.broadcasted_iota(jnp.int32, (half, half), 0) // chans
        lane = lax.broadcasted_iota(jnp.int32, (half, half), 1) // chans
        local = l_ref[...]
        for ref, dims in ((block_ref, 1), (block_t_ref, 0)):
            wide = lax.dot_general(local, spread, (((dims,), (0,)), ((), ())), preferred_element_type=F32)
            wide = jnp.concatenate([wide] * (half // chans), axis=0)
            ref[...] = jnp.where(row == lane, wide, 0.0).astype(BF16)
        value = jnp.concatenate([b_ref[...]] * 8, axis=0)
        high = value.astype(BF16)
        mid = (value - high.astype(F32)).astype(BF16)
        low = (value - high.astype(F32) - mid.astype(F32)).astype(BF16)
        wide = dot(high, spread) + dot(mid, spread) + dot(low, spread)
        bias_ref[...] = jnp.concatenate([wide, wide], axis=1)

        for n, first in enumerate(range(0, modes_x, batch)):
            copies[n].wait()
            for j in range(first, first + batch):
                for k in range(tiles):
                    scr[k, j * modes_y : (j + 1) * modes_y, :] = w_ref[j, :, k * LANES : (k + 1) * LANES].astype(F32)
        chip, core = me_ref[0] // 2, me_ref[0] % 2
        for w, mode in enumerate((chip + 2 * chips * core, chip + chips)):
            for k in range(tiles):
                s, g = divmod(k, groups)
                base = (2 * w + s) * modes_x
                pick[g, base : base + modes_x, :] = scr[k, pl.ds(mode, modes_x, stride=modes_y), :]
        per = LANES // chans
        repeat = jnp.concatenate(
            [lane_equals(LANES, LANES, lambda l: l % chans, chans * g) for g in range(per)], axis=1
        )
        pad = jnp.zeros((LANES - rows, LANES), F32)
        for g in range(groups):
            plain_ref[g] = dot(pick[g].astype(BF16), repeat).astype(BF16)
            one[g * LANES : (g + 1) * LANES, :] = jnp.transpose(jnp.concatenate([pick[g], pad]))
        for b in range(chans):
            two[b * chans : (b + 1) * chans, :] = one[pl.ds(b, chans, stride=chans), :]
        for g in range(groups):
            part = jnp.transpose(two[g * LANES : (g + 1) * LANES, :])[0:rows]
            turned_ref[g] = dot(part.astype(BF16), repeat).astype(BF16)
        for copy in table_copies:
            copy.wait()

    shape = (groups, rows, LANES * LANES // chans)
    wide = jax.ShapeDtypeStruct(shape, BF16)
    block = jax.ShapeDtypeStruct((half, half), BF16)
    held = tuple(jax.ShapeDtypeStruct(t.shape, t.dtype) for t in tables)
    return pl.pallas_call(
        kernel,
        in_specs=[smem(), hbm(), vmem(), vmem()] + [hbm()] * count,
        out_specs=(vmem(),) * (5 + count),
        out_shape=(wide, wide, block, block, jax.ShapeDtypeStruct((8, 2 * half), F32)) + held,
        scratch_shapes=[
            pltpu.VMEM(weights.shape, BF16),
            pltpu.VMEM((tiles, modes_x * modes_y, LANES), F32),
            pltpu.VMEM((groups, rows, LANES), F32),
            pltpu.VMEM((full2 // 2, LANES), F32),
            pltpu.VMEM((full2 // 2, LANES), F32),
            pltpu.SemaphoreType.DMA((modes_x // batch,)),
            pltpu.SemaphoreType.DMA((count,)),
        ],
        compiler_params=params(),
        cost_estimate=cost(1000000, 4 * 1024 * 1024),
        name="prepare",
    )(me, *in_hbm(weights), local_weight, bias, *in_hbm(*tables))


def weigh(spec, w_ref, chans, modes_x, adjoint):
    tiles = spec.shape[1] // LANES
    groups = LANES // chans
    stack = jnp.concatenate([spec[:, k * LANES : (k + 1) * LANES] for k in range(tiles)], axis=0)
    real = [None] * tiles
    imag = [None] * tiles
    for pair in range(chans // 2):
        two = [lane_equals(LANES, LANES, lambda l: l // chans * chans, c) for c in (2 * pair, 2 * pair + 1)]
        wide_rows = dot(stack, jnp.concatenate(two, axis=1))
        for c in (2 * pair, 2 * pair + 1):
            lanes = slice((c % 2) * LANES, (c % 2 + 1) * LANES)
            wl = slice((c % groups) * LANES, (c % groups + 1) * LANES)
            for own in range(2):
                base = 2 * own * modes_x
                wr = w_ref[c // groups, base : base + modes_x, wl].astype(F32)
                wi = w_ref[c // groups, base + modes_x : base + 2 * modes_x, wl].astype(F32)
                for k in range(0, 2 * tiles // 3) if own == 0 else range(2 * tiles // 3, tiles):
                    xr = wide_rows[2 * k * modes_x : (2 * k + 1) * modes_x, lanes]
                    xi = wide_rows[(2 * k + 1) * modes_x : (2 * k + 2) * modes_x, lanes]
                    if adjoint:
                        r, i = xr * wr + xi * wi, xi * wr - xr * wi
                    else:
                        r, i = xr * wr - xi * wi, xr * wi + xi * wr
                    real[k] = r if real[k] is None else real[k] + r
                    imag[k] = i if imag[k] is None else imag[k] + i
    return jnp.concatenate([jnp.concatenate(real, axis=1), jnp.concatenate(imag, axis=1)], axis=0).astype(BF16)


def mode_step(pencil, spread_w, forward, inverse, field, cotangent, chans):
    modes_x = forward.shape[0] // 2

    def kernel(p_ref, w_ref, f_ref, i_ref, u_hbm, c_hbm, spec_ref, out_ref, u_ref, c_ref, sem):
        copies = start_all([(u_hbm.at[0], u_ref), (c_hbm.at[0], c_ref)], sem)
        spec = dot(f_ref[...], p_ref[...]).astype(BF16)
        spec_ref[...] = spec
        mixed = weigh(spec, w_ref, chans, modes_x, False)
        out_ref[...] = dot(i_ref[...], mixed).astype(BF16)
        for copy in copies:
            copy.wait()

    return pl.pallas_call(
        kernel,
        in_specs=[vmem()] * 4 + [hbm()] * 2,
        out_specs=(vmem(),) * 4,
        out_shape=(
            jax.ShapeDtypeStruct((2 * modes_x, pencil.shape[1]), BF16),
            jax.ShapeDtypeStruct(pencil.shape, BF16),
            jax.ShapeDtypeStruct(field.shape[1:], BF16),
            jax.ShapeDtypeStruct(field.shape[1:], BF16),
        ),
        scratch_shapes=[pltpu.SemaphoreType.DMA((2,))],
        compiler_params=params(),
        cost_estimate=cost(2 * 48 * 6 * 128 * 4096, spread_w.size * 4),
        name="mode_step",
    )(pencil, spread_w, forward, inverse, *in_hbm(field, cotangent))


def adjoint_step(grads, spread_w, inverse, chans):
    modes_x = grads.shape[0] // 2
    shape = (inverse.shape[0], grads.shape[1])

    def kernel(g_ref, w_ref, i_ref, out_hbm, out_ref, out_sem):
        mixed = weigh(g_ref[...], w_ref, chans, modes_x, True)
        out_ref[...] = dot(i_ref[...], mixed).astype(BF16)
        copy = pltpu.make_async_copy(out_ref, out_hbm, out_sem)
        copy.start()
        copy.wait()

    return pl.pallas_call(
        kernel,
        in_specs=[vmem()] * 3,
        out_specs=hbm(),
        out_shape=pltpu.HBM(shape, BF16),
        scratch_shapes=[pltpu.VMEM(shape, BF16), pltpu.SemaphoreType.DMA],
        compiler_params=params(),
        cost_estimate=cost(2 * 48 * 6 * 128 * 4096, spread_w.size * 4),
        name="adjoint_step",
    )(grads, spread_w, inverse)


def pointwise(field, cotangent, first_rows, pencil, table_t, table, block_weight, bias_row, chips, half):
    rows, length, width = field.shape
    chunk, sub = 128, 16
    modes = table.shape[0]
    depth = table_t.shape[1]

    def kernel(
        u_hbm, c_hbm, u_first, c_first, p_ref, tt_ref, t_ref, w_ref, b_ref, out_hbm, dpre_hbm, send_hbm,
        u_rest, c_rest, out_ref, dpre_ref, send_ref, bscr, dscr, sem, out_sem,
    ):
        copies = []
        for x in range(1, rows):
            pairs = [(u_hbm.at[x], u_rest.at[x - 1]), (c_hbm.at[x], c_rest.at[x - 1])]
            copies.append(start_all(pairs, sem.at[x - 1]))
        cut_lanes(bscr, p_ref)
        root = math.sqrt(2.0 / math.pi)
        bias = b_ref[0:1, :]
        high = bias.astype(BF16)
        mid = (bias - high.astype(F32)).astype(BF16)
        low = (bias - high.astype(F32) - mid.astype(F32)).astype(BF16)
        parts = [t.astype(F32) for t in (high, mid, low)]
        bias = jnp.concatenate(parts + [jnp.zeros((depth - modes - 3, width), F32)], axis=0)
        bias = (0.5 * bias).astype(BF16)
        weight = (0.5 * w_ref[...].astype(F32)).astype(BF16)

        def one_row(x):
            if x > 0:
                for copy in copies[x - 1]:
                    copy.wait()
            u_ref = u_rest.at[x - 1] if x > 0 else u_first
            c_ref = c_rest.at[x - 1] if x > 0 else c_first
            coeff = (0.5 * gather_rows(bscr, x, chips, half).astype(F32)).astype(BF16)
            coeff = jnp.concatenate([coeff, bias], axis=0)
            for k in range(length // chunk):
                where = pl.ds(k * chunk, chunk)
                for h in range(2):
                    lanes = slice(h * half, (h + 1) * half)
                    left = jnp.concatenate([u_ref[where, lanes], tt_ref[where, :]], axis=1)
                    right = jnp.concatenate([weight, coeff[:, lanes]], axis=0)
                    halved = dot(left, right)
                    for at in range(0, chunk, sub):
                        place = pl.ds(k * chunk + at, sub)
                        p = halved[at : at + sub]
                        inner = p * (2.0 * root + (8.0 * root * 0.044715) * (p * p))
                        th = jnp.tanh(inner)
                        twice = 1.0 + th
                        out_ref[x, place, lanes] = (p * twice).astype(BF16)
                        slope = 1.5 * inner - (2.0 * root) * p
                        grad = twice * (0.5 + (1.0 - th) * slope)
                        dpre_ref[x, place, lanes] = (c_ref[place, lanes].astype(F32) * grad).astype(BF16)
            pltpu.make_async_copy(out_ref.at[x], out_hbm.at[x], out_sem.at[x]).start()
            pltpu.make_async_copy(dpre_ref.at[x], dpre_hbm.at[x], out_sem.at[rows + x]).start()
            scatter_rows(dscr, dot(t_ref[...], dpre_ref[x]), x, chips, half)

        for x in range(rows):
            one_row(x)
        join_lanes(send_ref, dscr)
        pltpu.make_async_copy(send_ref, send_hbm, out_sem.at[2 * rows]).start()
        for x in range(rows):
            pltpu.make_async_copy(out_ref.at[x], out_hbm.at[x], out_sem.at[x]).wait()
            pltpu.make_async_copy(dpre_ref.at[x], dpre_hbm.at[x], out_sem.at[rows + x]).wait()
        pltpu.make_async_copy(send_ref, send_hbm, out_sem.at[2 * rows]).wait()

    return pl.pallas_call(
        kernel,
        in_specs=[hbm(), hbm()] + [vmem()] * 7,
        out_specs=(hbm(), hbm(), hbm()),
        out_shape=(
            pltpu.HBM(field.shape, BF16),
            pltpu.HBM(field.shape, BF16),
            pltpu.HBM(pencil.shape, BF16),
        ),
        scratch_shapes=[
            pltpu.VMEM((rows - 1, length, width), BF16),
            pltpu.VMEM((rows - 1, length, width), BF16),
            pltpu.VMEM(field.shape, BF16),
            pltpu.VMEM(field.shape, BF16),
            pltpu.VMEM(pencil.shape, BF16),
            pltpu.VMEM(cut_shape(pencil.shape), F32),
            pltpu.VMEM(cut_shape(pencil.shape), F32),
            pltpu.SemaphoreType.DMA((rows - 1, 2)),
            pltpu.SemaphoreType.DMA((2 * rows + 1,)),
        ],
        compiler_params=params(),
        cost_estimate=cost(field.size * 1000, field.size * 8),
        name="pointwise",
    )(*in_hbm(field, cotangent), *first_rows, pencil, table_t, table, block_weight, bias_row)


def local_sums(field, dpre, chans, half):
    rows, length, width = field.shape
    slices = half // chans

    def kernel(u_hbm, d_hbm, out_ref, u_ref, d_ref, sem):
        copies = start_all(
            [(u_hbm.at[x], u_ref.at[x]) for x in range(rows)] + [(d_hbm.at[x], d_ref.at[x]) for x in range(rows)], sem
        )
        both = bias = None
        ones = jnp.ones((16, length), BF16)
        for x in range(rows):
            copies[x].wait()
            copies[rows + x].wait()
            for h in range(2):
                lanes = slice(h * half, (h + 1) * half)
                part = lax.dot_general(
                    u_ref[x, :, lanes], d_ref[x, :, lanes], (((0,), (0,)), ((), ())), preferred_element_type=F32
                )
                both = part if both is None else both + part
            part = dot(ones, d_ref[x])[0:8]
            bias = part if bias is None else bias + part
        group = lax.broadcasted_iota(jnp.int32, (chans, half), 1) // chans
        total = jnp.zeros((chans, half), F32)
        for p in range(slices):
            total = jnp.where(group == p, both[p * chans : (p + 1) * chans], total)
        total = sum(total[:, k * LANES : (k + 1) * LANES] for k in range(half // LANES))
        bias = sum(bias[:, k * LANES : (k + 1) * LANES] for k in range(width // LANES))
        shift = LANES // 2
        while shift >= chans:
            total = total + pltpu.roll(total, shift, 1)
            bias = bias + pltpu.roll(bias, shift, 1)
            shift //= 2
        group8 = lax.broadcasted_iota(jnp.int32, (8, LANES), 1) // chans
        folded = jnp.zeros((8, LANES), F32)
        for k in range(chans // 8):
            folded = jnp.where(group8 == k, total[8 * k : 8 * k + 8], folded)
        high = folded.astype(BF16).astype(F32)
        rest = (folded - high).astype(BF16).astype(F32)
        bias_high = bias.astype(BF16).astype(F32)
        bias_mid = (bias - bias_high).astype(BF16).astype(F32)
        bias_low = bias - bias_high - bias_mid
        row = lax.broadcasted_iota(jnp.int32, (8, LANES), 0)
        terms = jnp.where(row == 0, bias_high, jnp.where(row == 1, bias_mid, jnp.where(row == 2, bias_low, 0.0)))
        out_ref[...] = jnp.concatenate([high, rest, terms], axis=0).astype(BF16)

    return pl.pallas_call(
        kernel,
        in_specs=[hbm(), hbm()],
        out_specs=vmem(),
        out_shape=jax.ShapeDtypeStruct((24, LANES), BF16),
        scratch_shapes=[
            pltpu.VMEM(field.shape, BF16),
            pltpu.VMEM(field.shape, BF16),
            pltpu.SemaphoreType.DMA((2 * rows,)),
        ],
        compiler_params=params(),
        cost_estimate=cost(field.size * 1000, field.size * 4),
        name="local_sums",
    )(*in_hbm(field, dpre))


def weight_sums(spectrum, pencil, forward, chans):
    modes_x = spectrum.shape[0] // 2
    tiles = spectrum.shape[1] // LANES
    groups = LANES // chans
    step = 2 * LANES
    full = chans * chans
    parts = full // step

    def kernel(u_ref, p_ref, f_ref, d_ref, own_ref, shared_ref):
        def stack(ref):
            return jnp.concatenate([ref[:, k * LANES : (k + 1) * LANES] for k in range(tiles)], axis=0)

        left = stack(u_ref)
        d_ref[...] = dot(f_ref[...], p_ref[...]).astype(BF16)
        repeat = jnp.concatenate(
            [lane_equals(LANES, LANES, lambda l: l % chans, chans * g) for g in range(groups)], axis=1
        )
        right = dot(stack(d_ref), repeat)
        for a in range(parts):
            sums = {}
            for g in range(groups):
                pick = lane_equals(LANES, step, lambda l: l // chans, g * chans + a * (step // chans))
                spread_u = dot(left, pick)
                for k in range(tiles):
                    kind = 0 if k < 2 * tiles // 3 else 1
                    re = slice(2 * k * modes_x, (2 * k + 1) * modes_x)
                    im = slice((2 * k + 1) * modes_x, (2 * k + 2) * modes_x)
                    for z in range(2):
                        lanes = slice(z * LANES, (z + 1) * LANES)
                        ur, ui = spread_u[re, lanes], spread_u[im, lanes]
                        dr = right[re, g * LANES : (g + 1) * LANES]
                        di = right[im, g * LANES : (g + 1) * LANES]
                        for t, term in ((0, ur * dr + ui * di), (1, ur * di - ui * dr)):
                            key = (kind, t, z)
                            sums[key] = term if key not in sums else sums[key] + term
            for t in range(2):
                lanes = slice(t * full + a * step, t * full + (a + 1) * step)
                own_ref[:, lanes] = jnp.concatenate([sums[0, t, 0], sums[0, t, 1]], axis=1).astype(BF16)
                shared_ref[:, lanes] = jnp.concatenate([sums[1, t, 0], sums[1, t, 1]], axis=1)

    return pl.pallas_call(
        kernel,
        in_specs=[vmem()] * 3,
        out_shape=(
            jax.ShapeDtypeStruct(spectrum.shape, BF16),
            jax.ShapeDtypeStruct((modes_x, 2 * full), BF16),
            jax.ShapeDtypeStruct((modes_x, 2 * full), F32),
        ),
        compiler_params=params(),
        cost_estimate=cost(2 * 288 * 128 * 4096, 4 * 1024 * 1024),
        name="weight_sums",
    )(spectrum, pencil, forward)


def make_shard(me, own, shared, other, stats):
    rows, full2 = own.shape
    full = full2 // 2
    half = full // 2
    width = full2 + full + stats.shape[1]

    def kernel(me_ref, o_ref, s_ref, r_ref, st_ref, out_ref):
        first = me_ref[0] % 2 == 0
        out_ref[:, 0:full2] = o_ref[...]
        for t in range(2):
            low = slice(t * full, t * full + half)
            high = slice(t * full + half, (t + 1) * full)
            mine = jnp.where(first, s_ref[:, low], s_ref[:, high])
            theirs = jnp.where(first, r_ref[:, low], r_ref[:, high])
            out_ref[:, full2 + t * half : full2 + (t + 1) * half] = (mine + theirs).astype(BF16)
        out_ref[:, full2 + full :] = st_ref[...]

    return pl.pallas_call(
        kernel,
        in_specs=[smem()] + [vmem()] * 4,
        out_shape=jax.ShapeDtypeStruct((rows, width), BF16),
        compiler_params=params(),
        cost_estimate=cost(100000, 1000000),
        name="make_shard",
    )(me, own, shared, other, stats)


def ring_chip(spot, chips):
    return jnp.where(spot < chips // 2, 2 * spot, 2 * (chips - 1 - spot) + 1)


def ring_spot(chip, chips):
    return jnp.where(chip % 2 == 0, chip // 2, chips - 1 - chip // 2)


def read_sums(ref, full):
    sums = ref[:, 3 * full : 3 * full + LANES].astype(F32)
    return jnp.concatenate([sums[0:8] + sums[8:16], sums[16:24]], axis=0)


def early_sums(shards_all, chans):
    count = len(shards_all)

    def kernel(*refs):
        for n in range(count):
            refs[count][n] = read_sums(refs[n], chans * chans)

    return pl.pallas_call(
        kernel,
        in_specs=[vmem()] * count,
        out_specs=vmem(),
        out_shape=jax.ShapeDtypeStruct((count, 16, LANES), F32),
        compiler_params=params(),
        cost_estimate=cost(3 * 10**10, 4 * 1024 * 1024),
        name="early_sums",
    )(*shards_all)


def shard_places(me, turns, chips):
    spot = ring_spot(me // 2, chips)
    core = me % 2
    return [
        (ring_chip((spot + chips - back) % chips, chips), 1 - core if swapped else core) for back, swapped in turns
    ]


def place_tile(scr, refs, places, turns, k, modes_y, tiles):
    rows = scr.shape[1] // modes_y
    part = tiles // 4
    chips = modes_y // 3
    keeper = k % (2 * part) // part
    at = tiles + k // (2 * part) * part + k % part
    for n, (chip, core) in enumerate(places):
        own = pl.ds(chip + 2 * chips * core, rows, stride=modes_y)
        scr[k, own, :] = refs[n][:, k * LANES : (k + 1) * LANES].astype(F32)
        if turns[n][1]:
            continue
        mate = turns.index((turns[n][0], True))
        lanes = slice(at * LANES, (at + 1) * LANES)
        shared = pl.ds(chip + chips, rows, stride=modes_y)
        scr[k, shared, :] = jnp.where(core == keeper, refs[n][:, lanes], refs[mate][:, lanes]).astype(F32)


def assemble_first(me, shards_all, known, turns, modes_y, chans, chips):
    rows = shards_all[0].shape[0]
    count = len(shards_all)
    tiles = 2 * chans * chans // LANES

    def kernel(me_ref, *refs):
        places = shard_places(me_ref[0], turns, chips)
        for k in range(tiles):
            place_tile(refs[count], refs[:count], places, turns, k, modes_y, tiles)
        for n in range(known, count):
            refs[count + 1][n - known] = read_sums(refs[n], chans * chans)

    return pl.pallas_call(
        kernel,
        in_specs=[smem()] + [vmem()] * count,
        out_specs=(vmem(), vmem()),
        out_shape=(
            jax.ShapeDtypeStruct((tiles, rows * modes_y, LANES), F32),
            jax.ShapeDtypeStruct((count - known, 16, LANES), F32),
        ),
        compiler_params=params(),
        cost_estimate=cost(1000000, 4 * 1024 * 1024),
        name="assemble_first",
    )(me, *shards_all)


def assemble(me, scr, early, more, shards_all, turns, modes_y, chans, chips):
    rows = shards_all[0].shape[0]
    full = chans * chans
    tiles = 2 * full // LANES
    count = len(shards_all)
    total_count = len(turns)
    before = total_count - count
    known = early.shape[0]

    def kernel(me_ref, scr_in, e_ref, m_ref, *refs):
        ins, (scr, g_ref, l_ref, b_ref, stat, out, sem) = refs[:count], refs[count:]
        places = shard_places(me_ref[0], turns, chips)
        copies = []
        for k in range(tiles):
            place_tile(scr, ins, places[before:], turns[before:], k, modes_y, tiles)
            lanes = slice(k * LANES, (k + 1) * LANES)
            for j in range(rows):
                out[j, :, lanes] = scr[k, j * modes_y : (j + 1) * modes_y, :].astype(BF16)
            if k % 4 == 3:
                lanes = pl.ds((k - 3) * LANES, 4 * LANES)
                copies.append(pltpu.make_async_copy(out.at[:, :, lanes], g_ref.at[:, :, lanes], sem.at[k // 4]))
                copies[-1].start()
        for n, (chip, core) in enumerate(places):
            if n < known:
                stat[2 * chip + core] = e_ref[n]
            elif n < before:
                stat[2 * chip + core] = m_ref[n - known]
            else:
                stat[2 * chip + core] = read_sums(ins[n - before], full)
        total = stat[0]
        for n in range(1, total_count):
            total = total + stat[n]
        for k in range(chans // 8):
            piece = total[0:8] if k == 0 else pltpu.roll(total[0:8], LANES - k * chans, 1)
            l_ref[8 * k : 8 * k + 8, :] = piece[:, 0:chans]
        b_ref[...] = jnp.sum(total[8:16], axis=0, keepdims=True)[:, 0:chans]
        for copy in copies:
            copy.wait()

    shape = (rows, modes_y, 2 * full)
    return pl.pallas_call(
        kernel,
        in_specs=[smem()] + [vmem()] * (3 + count),
        out_specs=(vmem(), hbm(), vmem(), vmem()),
        out_shape=(
            jax.ShapeDtypeStruct(scr.shape, F32),
            pltpu.HBM(shape, BF16),
            jax.ShapeDtypeStruct((chans, chans), F32),
            jax.ShapeDtypeStruct((1, chans), F32),
        ),
        input_output_aliases={1: 0},
        scratch_shapes=[
            pltpu.VMEM((total_count, 16, LANES), F32),
            pltpu.VMEM(shape, BF16),
            pltpu.SemaphoreType.DMA((tiles // 4,)),
        ],
        compiler_params=params(),
        cost_estimate=cost(1000000, 8 * 1024 * 1024),
        name="assemble",
    )(me, scr, early, more, *shards_all)[1:]


def back_to_field(dpre, pencil, table_t, block_weight, chips, half):
    rows, length, width = dpre.shape
    chunk = 128

    def kernel(d_hbm, p_ref, tt_ref, w_ref, out_hbm, d_ref, out_ref, bscr, sem, out_sem):
        copies = start_all([(d_hbm.at[x], d_ref.at[x]) for x in range(rows)], sem)
        cut_lanes(bscr, p_ref)
        out_copies = []
        for x in range(rows):
            copies[x].wait()
            coeff = gather_rows(bscr, x, chips, half)
            for k in range(length // chunk):
                where = pl.ds(k * chunk, chunk)
                d = d_ref[x, where, :]
                spec = dot(tt_ref[where, :], coeff)
                for h in range(2):
                    lanes = slice(h * half, (h + 1) * half)
                    out_ref[x, where, lanes] = (spec[:, lanes] + dot(d[:, lanes], w_ref[...])).astype(BF16)
            out_copies.append(pltpu.make_async_copy(out_ref.at[x], out_hbm.at[x], out_sem.at[x]))
            out_copies[-1].start()
        for copy in out_copies:
            copy.wait()

    return pl.pallas_call(
        kernel,
        in_specs=[hbm()] + [vmem()] * 3,
        out_specs=hbm(),
        out_shape=pltpu.HBM(dpre.shape, BF16),
        scratch_shapes=[
            pltpu.VMEM(dpre.shape, BF16),
            pltpu.VMEM(dpre.shape, BF16),
            pltpu.VMEM(cut_shape(pencil.shape), F32),
            pltpu.SemaphoreType.DMA((rows,)),
            pltpu.SemaphoreType.DMA((rows,)),
        ],
        compiler_params=params(),
        cost_estimate=cost(dpre.size * 500, dpre.size * 4),
        name="back_to_field",
    )(*in_hbm(dpre), pencil, table_t, block_weight)


def exchange(pencil):
    return lax.all_to_all(pencil, "xy", split_axis=0, concat_axis=0, tiled=True)


class Ring:
    def __init__(self, shard, chips):
        order = [ring_chip_int(i, chips) for i in range(chips)]
        self.chips = chips
        self.hops = {
            way: [(2 * order[i] + c, 2 * order[(i + way) % chips] + c) for i in range(chips) for c in range(2)]
            for way in (1, -1)
        }
        self.swap = [(i, i ^ 1) for i in range(2 * chips)]
        self.step = 0
        self.ahead = self.back = shard
        self.parts, self.turns = [], []
        self.keep(shard, 0)

    def keep(self, piece, turn):
        self.parts.append(piece)
        self.turns.append((turn, False))
        self.parts.append(lax.ppermute(piece, "xy", self.swap))
        self.turns.append((turn, True))

    def hop(self):
        self.step += 1
        self.ahead = lax.ppermute(self.ahead, "xy", self.hops[1])
        if self.step < self.chips // 2:
            self.back = lax.ppermute(self.back, "xy", self.hops[-1])

    def settle(self):
        self.keep(self.ahead, self.step)
        if self.step < self.chips // 2:
            self.keep(self.back, self.chips - self.step)

    def tie(self, other):
        self.ahead, self.back, other = lax.optimization_barrier((self.ahead, self.back, other))
        return other

    def hold(self, other):
        self.ahead, other = lax.optimization_barrier((self.ahead, other))
        return other


def ring_chip_int(spot, chips):
    return 2 * spot if spot < chips // 2 else 2 * (chips - 1 - spot) + 1


def fast_shards(field, spectral_weight, local_weight, bias, cotangent):
    rows, length_y, width = field.shape
    chans = local_weight.shape[0]
    planes = width // chans
    modes_x, modes_y = spectral_weight.shape[:2]
    devices = lax.axis_size("xy")
    chips = devices // 2
    half = width // 2
    me = lax.axis_index("xy")
    table_y = np_ytable(modes_y, length_y, False)
    table_yw = np_ytable(modes_y, length_y, True)
    table_y_t, table_yw_t = (np.ascontiguousarray(t.T) for t in (table_y, table_yw))
    ones = np.ones((length_y, 3), table_yw_t.dtype)
    zeros = np.zeros((length_y, -(table_yw_t.shape[1] + 3) % 16), table_yw_t.dtype)
    table_yw_t = np.concatenate([table_yw_t, ones, zeros], axis=1)
    forward, inverse = np_xtables(modes_x, rows * devices)
    me_id = me.astype(jnp.int32)[None]

    send = rows_to_modes(field, table_y, chips, half)
    pencil = exchange(send)
    tables = [jnp.asarray(t) for t in (forward, inverse, table_yw_t, table_yw, table_y_t)]
    plain, turned, block, block_t, bias_row, *tables = prepare(
        me_id, spectral_weight, local_weight, bias[None, :], tables, chips, half
    )
    forward, inverse, table_yw_t, table_yw, table_y_t = tables
    spectrum, send, *first_rows = mode_step(pencil, plain, forward, inverse, field, cotangent, chans)
    pencil = exchange(send)
    output_field, dpre, send = pointwise(
        field, cotangent, first_rows, pencil, table_yw_t, table_yw, block, bias_row, chips, half
    )
    pencil = exchange(send)
    stats = local_sums(field, dpre, chans, half)
    pencil, stats = lax.optimization_barrier((pencil, stats))
    grads, own, shared = weight_sums(spectrum, pencil, forward, chans)
    other = lax.ppermute(shared, "xy", [(i, i ^ 1) for i in range(devices)])
    shard = make_shard(me_id, own, shared, other, stats)

    ring = Ring(shard, chips)
    grads = ring.tie(grads)
    ring.hop()
    send = adjoint_step(grads, turned, inverse, chans)
    send = ring.tie(send)
    ring.settle()
    first = list(ring.parts)
    ring.hop()
    pencil = exchange(send)
    ring.settle()
    early, turns = list(ring.parts), list(ring.turns)
    sums = early_sums(first, chans)
    sums = ring.tie(sums)
    ring.hop()
    pencil, sums = lax.optimization_barrier((pencil, sums))
    ring.settle()
    ring.hop()
    field_grad = back_to_field(dpre, pencil, table_y_t, block_t, chips, half)
    early[0], field_grad = lax.optimization_barrier((early[0], field_grad))
    scr, more = assemble_first(me_id, early, len(first), turns, modes_y, chans, chips)
    scr = ring.hold(scr)
    ring.settle()
    late = ring.parts[len(early) :]
    spectral_grad, local_grad, bias_grad = assemble(
        me_id, scr, sums, more, late, ring.turns, modes_y, chans, chips
    )
    return output_field, field_grad, spectral_grad, local_grad, bias_grad.reshape(chans)


def fits(field, spectral_weight, local_weight, devices):
    rows, length_y, width = field.shape
    chans = local_weight.shape[0]
    modes_x, modes_y = spectral_weight.shape[:2]
    return (
        rows == 4
        and chans == 32
        and width == 512
        and length_y % 128 == 0
        and modes_x == 24
        and devices == 16
        and 2 * modes_y == 3 * devices
    )


def shards(field, spectral_weight, local_weight, bias, cotangent):
    if fits(field, spectral_weight, local_weight, lax.axis_size("xy")):
        return fast_shards(field, spectral_weight, local_weight, bias, cotangent)
    return general_shards(field, spectral_weight, local_weight, bias, cotangent)


def solution(mesh):
    return jax.shard_map(
        shards,
        mesh=mesh,
        in_specs=(P(("groups", "xy"), None, None), P(), P(), P(), P(("groups", "xy"), None, None)),
        out_specs=(
            P(("groups", "xy"), None, None),
            P(("groups", "xy"), None, None),
            P("groups", None, None),
            P("groups", None),
            P("groups"),
        ),
        check_vma=False,
    )
```

```python
import math

import jax
import jax.numpy as jnp
import ml_dtypes
import numpy as np
from jax import lax
from jax.experimental import pallas as pl
from jax.experimental.pallas import tpu as pltpu
from jax.sharding import PartitionSpec as P


def ytable(count, length, weighted):
    modes = jnp.arange(count, dtype=jnp.int32)
    places = jnp.arange(length, dtype=jnp.int32)
    phase = 2.0 * math.pi * (modes[:, None] * places[None, :] % length).astype(jnp.float32) / length
    factor = (
        jnp.where(modes == 0, 1.0, 2.0).astype(jnp.float32)
        if weighted
        else jnp.ones((count,), jnp.float32)
    )
    scale = factor[:, None] / math.sqrt(length)
    return jnp.stack([scale * jnp.cos(phase), -scale * jnp.sin(phase)]).astype(jnp.bfloat16)


def xtable(count, length, places):
    index = jnp.arange(count, dtype=jnp.int32)
    modes = jnp.where(index < count // 2, index, length - count + index)
    phase = 2.0 * math.pi * (modes[:, None] * places[None, :] % length).astype(jnp.float32) / length
    return (jnp.stack([jnp.cos(phase), jnp.sin(phase)]) / math.sqrt(length)).astype(jnp.bfloat16)


def mult(form, left, right):
    return jnp.einsum(form, left, right, preferred_element_type=jnp.float32)


def to_slab(flat, table, planes):
    rows = flat.shape[0]
    count = table.shape[1]
    chans = flat.shape[2] // planes
    coeff = mult("smy,xyq->xsmq", table, flat).astype(jnp.bfloat16)
    coeff = coeff.reshape(rows, 2, count, planes, chans).transpose(0, 2, 3, 1, 4)
    return coeff.reshape(rows, count * planes, 2 * chans)


def from_slab(slab, table, planes):
    rows = slab.shape[0]
    count = table.shape[1]
    chans = slab.shape[2] // 2
    spread = slab.reshape(rows, count, planes, 2, chans)
    return mult("smy,xmpsc->xypc", table, spread).reshape(rows, table.shape[2], planes * chans)


def forward_x(table, pencil):
    proj = mult("ajx,xnsc->ajnsc", table, pencil)
    real_part = proj[0, :, :, 0] + proj[1, :, :, 1]
    imag_part = proj[0, :, :, 1] - proj[1, :, :, 0]
    return jnp.stack([real_part, imag_part], axis=2).astype(jnp.bfloat16)


def inverse_x(table, modes):
    proj = mult("ajx,jnsc->axnsc", table, modes)
    real_part = proj[0, :, :, 0] - proj[1, :, :, 1]
    imag_part = proj[0, :, :, 1] + proj[1, :, :, 0]
    return jnp.stack([real_part, imag_part], axis=2).astype(jnp.bfloat16)


def mix_modes(spectrum, weights):
    real_part = mult("jnc,jnco->jno", spectrum[:, :, 0], weights[:, :, 0]) - mult(
        "jnc,jnco->jno", spectrum[:, :, 1], weights[:, :, 1]
    )
    imag_part = mult("jnc,jnco->jno", spectrum[:, :, 0], weights[:, :, 1]) + mult(
        "jnc,jnco->jno", spectrum[:, :, 1], weights[:, :, 0]
    )
    return jnp.stack([real_part, imag_part], axis=2).astype(jnp.bfloat16)


def adjoint_mix(grads, weights):
    real_part = mult("jnco,jno->jnc", weights[:, :, 0], grads[:, :, 0]) + mult(
        "jnco,jno->jnc", weights[:, :, 1], grads[:, :, 1]
    )
    imag_part = mult("jnco,jno->jnc", weights[:, :, 0], grads[:, :, 1]) - mult(
        "jnco,jno->jnc", weights[:, :, 1], grads[:, :, 0]
    )
    return jnp.stack([real_part, imag_part], axis=2).astype(jnp.bfloat16)


def pair_grad(spectrum, grads):
    real_part = mult("jmpc,jmpo->jmco", spectrum[:, :, :, 0], grads[:, :, :, 0]) + mult(
        "jmpc,jmpo->jmco", spectrum[:, :, :, 1], grads[:, :, :, 1]
    )
    imag_part = mult("jmpc,jmpo->jmco", spectrum[:, :, :, 0], grads[:, :, :, 1]) - mult(
        "jmpc,jmpo->jmco", spectrum[:, :, :, 1], grads[:, :, :, 0]
    )
    return jnp.stack([real_part, imag_part], axis=2)


def to_modes(slab, table_full):
    count = table_full.shape[1]
    pencil = lax.all_to_all(slab, "xy", split_axis=1, concat_axis=0, tiled=True)
    chans = pencil.shape[2] // 2
    items = pencil.shape[1]
    spread = pencil.reshape(pencil.shape[0], items, 2, chans)
    return forward_x(table_full, spread).reshape(count, items, 2 * chans)


def to_space(modes, table_full):
    count, pairs_dev, twice, chans = modes.shape
    pencil = inverse_x(table_full, modes)
    moved = lax.all_to_all(
        pencil.reshape(pencil.shape[0], pairs_dev, 2 * chans),
        "xy",
        split_axis=0,
        concat_axis=1,
        tiled=True,
    )
    return moved


def general_shards(field, spectral_weight, local_weight, bias, cotangent):
    rows, length_y, width_all = field.shape
    chans = local_weight.shape[0]
    planes = width_all // chans
    modes_x, modes_y = (spectral_weight.shape[0], spectral_weight.shape[1])
    devices = lax.axis_size("xy")
    length_x = rows * devices
    pairs_dev = modes_y * planes // devices
    offset = lax.axis_index("xy")
    table_y = ytable(modes_y, length_y, False)
    table_yw = ytable(modes_y, length_y, True)
    table_x = xtable(modes_x, length_x, jnp.arange(length_x, dtype=jnp.int32))
    weight_all = spectral_weight.reshape(modes_x, modes_y, 2, chans, chans)
    ky_index = (offset * pairs_dev + jnp.arange(pairs_dev, dtype=jnp.int32)) // planes
    weight_pairs = jnp.take(weight_all, ky_index, axis=1)
    spectrum = to_modes(to_slab(field, table_y, planes), table_x).reshape(
        modes_x, pairs_dev, 2, chans
    )
    mixed = mix_modes(spectrum, weight_pairs)
    spatial = from_slab(to_space(mixed, table_x), table_yw, planes)
    field4 = field.reshape(rows, length_y, planes, chans)
    local_term = mult("xypc,co->xypo", field4, local_weight)
    preact = spatial.reshape(rows, length_y, planes, chans) + local_term + bias
    output_field = jax.nn.gelu(preact).astype(jnp.bfloat16).reshape(rows, length_y, width_all)
    unused, pullback = jax.vjp(jax.nn.gelu, preact)
    grad_pre = pullback(cotangent.reshape(rows, length_y, planes, chans).astype(jnp.float32))[
        0
    ].astype(jnp.bfloat16)
    bias_part = jnp.sum(grad_pre.astype(jnp.float32), axis=(0, 1, 2))
    weight_part = mult("xypc,xypo->co", field4, grad_pre)
    back_local = mult("xypo,co->xypc", grad_pre, local_weight)
    grad_slab = to_slab(grad_pre.reshape(rows, length_y, width_all), table_yw, planes)
    grad_modes = to_modes(grad_slab, table_x).reshape(modes_x, pairs_dev, 2, chans)
    grad_spec = adjoint_mix(grad_modes, weight_pairs)
    back_spec = from_slab(to_space(grad_spec, table_x), table_y, planes)
    field_grad = (back_spec + back_local.reshape(rows, length_y, width_all)).astype(jnp.bfloat16)
    per_pair = pair_grad(
        spectrum.reshape(modes_x, pairs_dev, 1, 2, chans),
        grad_modes.reshape(modes_x, pairs_dev, 1, 2, chans),
    )
    onehot = (ky_index[:, None] == jnp.arange(modes_y, dtype=jnp.int32)[None, :]).astype(
        jnp.float32
    )
    partial_grad = jnp.einsum("jnsco,nm->jmsco", per_pair, onehot, precision=lax.Precision.HIGHEST)
    total, local_grad, bias_grad = lax.psum((partial_grad, weight_part, bias_part), "xy")
    spectral_grad = total.reshape(modes_x, modes_y, 2 * chans * chans).astype(jnp.bfloat16)
    return (output_field, field_grad, spectral_grad, local_grad, bias_grad)


F32 = jnp.float32
BF16 = jnp.bfloat16
LANES = 128
VMEM_LIMIT = 24 * 1024 * 1024


def dot(left, right):
    return jnp.dot(left, right, preferred_element_type=F32)


def params(**kwargs):
    return pltpu.CompilerParams(vmem_limit_bytes=VMEM_LIMIT, **kwargs)


def cost(flops, bytes_accessed):
    return pl.CostEstimate(flops=flops, bytes_accessed=bytes_accessed, transcendentals=0)


def np_ytable(count, length, weighted):
    modes = np.arange(count)
    places = np.arange(length)
    phase = np.float32(2.0 * math.pi) * (modes[:, None] * places[None, :] % length).astype(np.float32) / np.float32(length)
    factor = np.where(modes == 0, 1.0, 2.0).astype(np.float32) if weighted else np.ones((count,), np.float32)
    scale = (factor / np.float32(math.sqrt(length)))[:, None]
    both = np.stack([scale * np.cos(phase), -scale * np.sin(phase)]).astype(ml_dtypes.bfloat16)
    return both.reshape(2 * count, length)


def np_xtables(count, length):
    index = np.arange(count)
    modes = np.where(index < count // 2, index, length - count + index)
    places = np.arange(length)
    phase = np.float32(2.0 * math.pi) * (modes[:, None] * places[None, :] % length).astype(np.float32) / np.float32(length)
    norm = np.float32(math.sqrt(length))
    cosines = np.cos(phase) / norm
    sines = np.sin(phase) / norm
    forward = np.stack([np.stack([cosines, sines], -1), np.stack([-sines, cosines], -1)])
    forward = forward.reshape(2 * count, 2 * length).astype(ml_dtypes.bfloat16)
    return forward, np.ascontiguousarray(forward.T)


def lane_equals(rows, lanes, divide, offset):
    row = lax.broadcasted_iota(jnp.int32, (rows, lanes), 0)
    lane = lax.broadcasted_iota(jnp.int32, (rows, lanes), 1)
    return jnp.where(row - divide(lane) == offset, 1.0, 0.0).astype(BF16)


def start_all(pairs, sem):
    copies = [pltpu.make_async_copy(src, dst, sem.at[n]) for n, (src, dst) in enumerate(pairs)]
    for copy in copies:
        copy.start()
    return copies


def hbm():
    return pl.BlockSpec(memory_space=pltpu.HBM)


def in_hbm(*arrays):
    return [pltpu.with_memory_space_constraint(a, pltpu.HBM) for a in arrays]


def vmem():
    return pl.BlockSpec(memory_space=pltpu.VMEM)


def smem():
    return pl.BlockSpec(memory_space=pltpu.SMEM)


def scatter_rows(dst, sums, place, chips, half):
    tiles = half // LANES
    for s in range(2):
        for core in range(2):
            where = pl.ds(core * 8 + 2 * place + s, chips, stride=16)
            own = (3 * s + 2 * core) * chips
            shared = (3 * s + 1) * chips
            for k in range(2 * tiles):
                dst[k, where, :] = sums[own : own + chips, k * LANES : (k + 1) * LANES]
            for k in range(tiles):
                at = (core * tiles + k) * LANES
                dst[2 * tiles + k, where, :] = sums[shared : shared + chips, at : at + LANES]


def gather_rows(src, place, chips, half):
    tiles = half // LANES
    out = []
    for s in range(2):
        one = pl.ds(2 * place + s, chips, stride=16)
        two = pl.ds(8 + 2 * place + s, chips, stride=16)
        own = range(2 * tiles)
        shared = range(2 * tiles, 3 * tiles)
        out.append(jnp.concatenate([src[k, one, :] for k in own], axis=1))
        out.append(jnp.concatenate([src[k, w, :] for w in (one, two) for k in shared], axis=1))
        out.append(jnp.concatenate([src[k, two, :] for k in own], axis=1))
    return jnp.concatenate(out, axis=0).astype(BF16)


def cut_lanes(dst, src):
    for k in range(dst.shape[0]):
        dst[k, 0 : src.shape[0], :] = src[:, k * LANES : (k + 1) * LANES].astype(F32)


def join_lanes(dst, src):
    for k in range(src.shape[0]):
        dst[:, k * LANES : (k + 1) * LANES] = src[k, 0 : dst.shape[0], :].astype(BF16)


def cut_shape(shape):
    return (shape[1] // LANES, shape[0] + 16, LANES)


def rows_to_modes(field, table, chips, half):
    rows, length, width = field.shape
    shape = (chips * 16, 3 * half)

    def kernel(u_hbm, t_hbm, out_hbm, u_ref, t_ref, scr, out_ref, sem, out_sem):
        copies = start_all([(t_hbm, t_ref)] + [(u_hbm.at[x], u_ref.at[x]) for x in range(rows)], sem)
        copies[0].wait()
        for x in range(rows):
            copies[1 + x].wait()
            scatter_rows(scr, dot(t_ref[...], u_ref[x]), x, chips, half)
        join_lanes(out_ref, scr)
        copy = pltpu.make_async_copy(out_ref, out_hbm, out_sem)
        copy.start()
        copy.wait()

    return pl.pallas_call(
        kernel,
        in_specs=[hbm(), hbm()],
        out_specs=hbm(),
        out_shape=pltpu.HBM(shape, BF16),
        scratch_shapes=[
            pltpu.VMEM(field.shape, BF16),
            pltpu.VMEM(table.shape, BF16),
            pltpu.VMEM(cut_shape(shape), F32),
            pltpu.VMEM(shape, BF16),
            pltpu.SemaphoreType.DMA((1 + rows,)),
            pltpu.SemaphoreType.DMA,
        ],
        compiler_params=params(),
        cost_estimate=cost(2 * table.size * rows * width, field.size * 2),
        name="rows_to_modes",
    )(*in_hbm(field, table))


def prepare(me, weights, local_weight, bias, tables, chips, half):
    modes_x, modes_y, full2 = weights.shape
    chans = local_weight.shape[0]
    tiles = full2 // LANES
    rows = 4 * modes_x
    groups = full2 // 2 // LANES
    batch = 6

    count = len(tables)

    def kernel(me_ref, w_hbm, l_ref, b_ref, *refs):
        tables_hbm, (plain_ref, turned_ref, block_ref, block_t_ref, bias_ref) = refs[:count], refs[count : count + 5]
        tables_ref, (w_ref, scr, pick, one, two, sem, table_sem) = refs[count + 5 : 2 * count + 5], refs[2 * count + 5 :]
        table_copies = start_all(list(zip(tables_hbm, tables_ref)), table_sem)
        cuts = [pl.ds(j, batch) for j in range(0, modes_x, batch)]
        copies = start_all([(w_hbm.at[cut], w_ref.at[cut]) for cut in cuts], sem)

        spread = lane_equals(chans, half, lambda l: l % chans, 0)
        row = lax.broadcasted_iota(jnp.int32, (half, half), 0) // chans
        lane = lax.broadcasted_iota(jnp.int32, (half, half), 1) // chans
        local = l_ref[...]
        for ref, dims in ((block_ref, 1), (block_t_ref, 0)):
            wide = lax.dot_general(local, spread, (((dims,), (0,)), ((), ())), preferred_element_type=F32)
            wide = jnp.concatenate([wide] * (half // chans), axis=0)
            ref[...] = jnp.where(row == lane, wide, 0.0).astype(BF16)
        value = jnp.concatenate([b_ref[...]] * 8, axis=0)
        high = value.astype(BF16)
        mid = (value - high.astype(F32)).astype(BF16)
        low = (value - high.astype(F32) - mid.astype(F32)).astype(BF16)
        wide = dot(high, spread) + dot(mid, spread) + dot(low, spread)
        bias_ref[...] = jnp.concatenate([wide, wide], axis=1)

        for n, first in enumerate(range(0, modes_x, batch)):
            copies[n].wait()
            for j in range(first, first + batch):
                for k in range(tiles):
                    scr[k, j * modes_y : (j + 1) * modes_y, :] = w_ref[j, :, k * LANES : (k + 1) * LANES].astype(F32)
        chip, core = me_ref[0] // 2, me_ref[0] % 2
        for w, mode in enumerate((chip + 2 * chips * core, chip + chips)):
            for k in range(tiles):
                s, g = divmod(k, groups)
                base = (2 * w + s) * modes_x
                pick[g, base : base + modes_x, :] = scr[k, pl.ds(mode, modes_x, stride=modes_y), :]
        per = LANES // chans
        repeat = jnp.concatenate(
            [lane_equals(LANES, LANES, lambda l: l % chans, chans * g) for g in range(per)], axis=1
        )
        pad = jnp.zeros((LANES - rows, LANES), F32)
        for g in range(groups):
            plain_ref[g] = dot(pick[g].astype(BF16), repeat).astype(BF16)
            one[g * LANES : (g + 1) * LANES, :] = jnp.transpose(jnp.concatenate([pick[g], pad]))
        for b in range(chans):
            two[b * chans : (b + 1) * chans, :] = one[pl.ds(b, chans, stride=chans), :]
        for g in range(groups):
            part = jnp.transpose(two[g * LANES : (g + 1) * LANES, :])[0:rows]
            turned_ref[g] = dot(part.astype(BF16), repeat).astype(BF16)
        for copy in table_copies:
            copy.wait()

    shape = (groups, rows, LANES * LANES // chans)
    wide = jax.ShapeDtypeStruct(shape, BF16)
    block = jax.ShapeDtypeStruct((half, half), BF16)
    held = tuple(jax.ShapeDtypeStruct(t.shape, t.dtype) for t in tables)
    return pl.pallas_call(
        kernel,
        in_specs=[smem(), hbm(), vmem(), vmem()] + [hbm()] * count,
        out_specs=(vmem(),) * (5 + count),
        out_shape=(wide, wide, block, block, jax.ShapeDtypeStruct((8, 2 * half), F32)) + held,
        scratch_shapes=[
            pltpu.VMEM(weights.shape, BF16),
            pltpu.VMEM((tiles, (modes_x + 1) * modes_y, LANES), F32),
            pltpu.VMEM((groups, rows, LANES), F32),
            pltpu.VMEM((full2 // 2 + chans, LANES), F32),
            pltpu.VMEM((full2 // 2, LANES), F32),
            pltpu.SemaphoreType.DMA((modes_x // batch,)),
            pltpu.SemaphoreType.DMA((count,)),
        ],
        compiler_params=params(),
        cost_estimate=cost(1000000, 4 * 1024 * 1024),
        name="prepare",
    )(me, *in_hbm(weights), local_weight, bias, *in_hbm(*tables))


def weigh(spec, w_ref, chans, modes_x, adjoint):
    tiles = spec.shape[1] // LANES
    groups = LANES // chans
    stack = jnp.concatenate([spec[:, k * LANES : (k + 1) * LANES] for k in range(tiles)], axis=0)
    real = [None] * tiles
    imag = [None] * tiles
    for pair in range(chans // 2):
        two = [lane_equals(LANES, LANES, lambda l: l // chans * chans, c) for c in (2 * pair, 2 * pair + 1)]
        wide_rows = dot(stack, jnp.concatenate(two, axis=1))
        for c in (2 * pair, 2 * pair + 1):
            lanes = slice((c % 2) * LANES, (c % 2 + 1) * LANES)
            wl = slice((c % groups) * LANES, (c % groups + 1) * LANES)
            for own in range(2):
                base = 2 * own * modes_x
                wr = w_ref[c // groups, base : base + modes_x, wl].astype(F32)
                wi = w_ref[c // groups, base + modes_x : base + 2 * modes_x, wl].astype(F32)
                for k in range(0, 2 * tiles // 3) if own == 0 else range(2 * tiles // 3, tiles):
                    xr = wide_rows[2 * k * modes_x : (2 * k + 1) * modes_x, lanes]
                    xi = wide_rows[(2 * k + 1) * modes_x : (2 * k + 2) * modes_x, lanes]
                    if adjoint:
                        r, i = xr * wr + xi * wi, xi * wr - xr * wi
                    else:
                        r, i = xr * wr - xi * wi, xr * wi + xi * wr
                    real[k] = r if real[k] is None else real[k] + r
                    imag[k] = i if imag[k] is None else imag[k] + i
    return jnp.concatenate([jnp.concatenate(real, axis=1), jnp.concatenate(imag, axis=1)], axis=0).astype(BF16)


def mode_step(pencil, spread_w, forward, inverse, field, cotangent, chans):
    modes_x = forward.shape[0] // 2

    def kernel(p_ref, w_ref, f_ref, i_ref, u_hbm, c_hbm, spec_ref, out_ref, u_ref, c_ref, sem):
        copies = start_all([(u_hbm.at[0], u_ref), (c_hbm.at[0], c_ref)], sem)
        spec = dot(f_ref[...], p_ref[...]).astype(BF16)
        spec_ref[...] = spec
        mixed = weigh(spec, w_ref, chans, modes_x, False)
        out_ref[...] = dot(i_ref[...], mixed).astype(BF16)
        for copy in copies:
            copy.wait()

    return pl.pallas_call(
        kernel,
        in_specs=[vmem()] * 4 + [hbm()] * 2,
        out_specs=(vmem(),) * 4,
        out_shape=(
            jax.ShapeDtypeStruct((2 * modes_x, pencil.shape[1]), BF16),
            jax.ShapeDtypeStruct(pencil.shape, BF16),
            jax.ShapeDtypeStruct(field.shape[1:], BF16),
            jax.ShapeDtypeStruct(field.shape[1:], BF16),
        ),
        scratch_shapes=[pltpu.SemaphoreType.DMA((2,))],
        compiler_params=params(),
        cost_estimate=cost(2 * 48 * 6 * 128 * 4096, spread_w.size * 4),
        name="mode_step",
    )(pencil, spread_w, forward, inverse, *in_hbm(field, cotangent))


def adjoint_step(grads, spread_w, inverse, chans):
    modes_x = grads.shape[0] // 2
    shape = (inverse.shape[0], grads.shape[1])

    def kernel(g_ref, w_ref, i_ref, out_hbm, out_ref, out_sem):
        mixed = weigh(g_ref[...], w_ref, chans, modes_x, True)
        out_ref[...] = dot(i_ref[...], mixed).astype(BF16)
        copy = pltpu.make_async_copy(out_ref, out_hbm, out_sem)
        copy.start()
        copy.wait()

    return pl.pallas_call(
        kernel,
        in_specs=[vmem()] * 3,
        out_specs=hbm(),
        out_shape=pltpu.HBM(shape, BF16),
        scratch_shapes=[pltpu.VMEM(shape, BF16), pltpu.SemaphoreType.DMA],
        compiler_params=params(),
        cost_estimate=cost(2 * 48 * 6 * 128 * 4096, spread_w.size * 4),
        name="adjoint_step",
    )(grads, spread_w, inverse)


def pointwise(field, cotangent, first_rows, pencil, table_t, table, block_weight, bias_row, chips, half):
    rows, length, width = field.shape
    chunk, sub = 128, 16
    modes = table.shape[0]
    depth = table_t.shape[1]

    def kernel(
        u_hbm, c_hbm, u_first, c_first, p_ref, tt_ref, t_ref, w_ref, b_ref, out_hbm, dpre_hbm, send_hbm,
        u_rest, c_rest, out_ref, dpre_ref, send_ref, bscr, dscr, sem, out_sem,
    ):
        copies = []
        for x in range(1, rows):
            pairs = [(u_hbm.at[x], u_rest.at[x - 1]), (c_hbm.at[x], c_rest.at[x - 1])]
            copies.append(start_all(pairs, sem.at[x - 1]))
        cut_lanes(bscr, p_ref)
        root = math.sqrt(2.0 / math.pi)
        bias = b_ref[0:1, :]
        high = bias.astype(BF16)
        mid = (bias - high.astype(F32)).astype(BF16)
        low = (bias - high.astype(F32) - mid.astype(F32)).astype(BF16)
        parts = [t.astype(F32) for t in (high, mid, low)]
        bias = jnp.concatenate(parts + [jnp.zeros((depth - modes - 3, width), F32)], axis=0)
        bias = (0.5 * bias).astype(BF16)
        weight = (0.5 * w_ref[...].astype(F32)).astype(BF16)

        def transform_row(x):
            scatter_rows(dscr, dot(t_ref[...], dpre_ref[x]), x, chips, half)

        def one_row(x):
            if x > 0:
                for copy in copies[x - 1]:
                    copy.wait()
            u_ref = u_rest.at[x - 1] if x > 0 else u_first
            c_ref = c_rest.at[x - 1] if x > 0 else c_first
            coeff = (0.5 * gather_rows(bscr, x, chips, half).astype(F32)).astype(BF16)
            coeff = jnp.concatenate([coeff, bias], axis=0)
            for k in range(length // chunk):
                where = pl.ds(k * chunk, chunk)
                for h in range(2):
                    lanes = slice(h * half, (h + 1) * half)
                    left = jnp.concatenate([u_ref[where, lanes], tt_ref[where, :]], axis=1)
                    right = jnp.concatenate([weight, coeff[:, lanes]], axis=0)
                    halved = dot(left, right)
                    for at in range(0, chunk, sub):
                        place = pl.ds(k * chunk + at, sub)
                        p = halved[at : at + sub]
                        inner = p * (2.0 * root + (8.0 * root * 0.044715) * (p * p))
                        th = jnp.tanh(inner)
                        twice = 1.0 + th
                        out_ref[x, place, lanes] = (p * twice).astype(BF16)
                        slope = 1.5 * inner - (2.0 * root) * p
                        grad = twice * (0.5 + (1.0 - th) * slope)
                        dpre_ref[x, place, lanes] = (c_ref[place, lanes].astype(F32) * grad).astype(BF16)
            pltpu.make_async_copy(out_ref.at[x], out_hbm.at[x], out_sem.at[x]).start()
            pltpu.make_async_copy(dpre_ref.at[x], dpre_hbm.at[x], out_sem.at[rows + x]).start()
            if x > 0:
                transform_row(x - 1)

        for x in range(rows):
            one_row(x)
        transform_row(rows - 1)
        join_lanes(send_ref, dscr)
        pltpu.make_async_copy(send_ref, send_hbm, out_sem.at[2 * rows]).start()
        for x in range(rows):
            pltpu.make_async_copy(out_ref.at[x], out_hbm.at[x], out_sem.at[x]).wait()
            pltpu.make_async_copy(dpre_ref.at[x], dpre_hbm.at[x], out_sem.at[rows + x]).wait()
        pltpu.make_async_copy(send_ref, send_hbm, out_sem.at[2 * rows]).wait()

    return pl.pallas_call(
        kernel,
        in_specs=[hbm(), hbm()] + [vmem()] * 7,
        out_specs=(hbm(), hbm(), hbm()),
        out_shape=(
            pltpu.HBM(field.shape, BF16),
            pltpu.HBM(field.shape, BF16),
            pltpu.HBM(pencil.shape, BF16),
        ),
        scratch_shapes=[
            pltpu.VMEM((rows - 1, length, width), BF16),
            pltpu.VMEM((rows - 1, length, width), BF16),
            pltpu.VMEM(field.shape, BF16),
            pltpu.VMEM(field.shape, BF16),
            pltpu.VMEM(pencil.shape, BF16),
            pltpu.VMEM(cut_shape(pencil.shape), F32),
            pltpu.VMEM(cut_shape(pencil.shape), F32),
            pltpu.SemaphoreType.DMA((rows - 1, 2)),
            pltpu.SemaphoreType.DMA((2 * rows + 1,)),
        ],
        compiler_params=params(),
        cost_estimate=cost(field.size * 1000, field.size * 8),
        name="pointwise",
    )(*in_hbm(field, cotangent), *first_rows, pencil, table_t, table, block_weight, bias_row)


def local_sums(field, dpre, chans, half):
    rows, length, width = field.shape
    slices = half // chans

    def kernel(u_hbm, d_hbm, out_ref, u_ref, d_ref, sem):
        copies = start_all(
            [(u_hbm.at[x], u_ref.at[x]) for x in range(rows)] + [(d_hbm.at[x], d_ref.at[x]) for x in range(rows)], sem
        )
        both = bias = None
        ones = jnp.ones((16, length), BF16)
        for x in range(rows):
            copies[x].wait()
            copies[rows + x].wait()
            for h in range(2):
                lanes = slice(h * half, (h + 1) * half)
                part = lax.dot_general(
                    u_ref[x, :, lanes], d_ref[x, :, lanes], (((0,), (0,)), ((), ())), preferred_element_type=F32
                )
                both = part if both is None else both + part
            part = dot(ones, d_ref[x])[0:8]
            bias = part if bias is None else bias + part
        group = lax.broadcasted_iota(jnp.int32, (chans, half), 1) // chans
        total = jnp.zeros((chans, half), F32)
        for p in range(slices):
            total = jnp.where(group == p, both[p * chans : (p + 1) * chans], total)
        total = sum(total[:, k * LANES : (k + 1) * LANES] for k in range(half // LANES))
        bias = sum(bias[:, k * LANES : (k + 1) * LANES] for k in range(width // LANES))
        shift = LANES // 2
        while shift >= chans:
            total = total + pltpu.roll(total, shift, 1)
            bias = bias + pltpu.roll(bias, shift, 1)
            shift //= 2
        group8 = lax.broadcasted_iota(jnp.int32, (8, LANES), 1) // chans
        folded = jnp.zeros((8, LANES), F32)
        for k in range(chans // 8):
            folded = jnp.where(group8 == k, total[8 * k : 8 * k + 8], folded)
        high = folded.astype(BF16).astype(F32)
        rest = (folded - high).astype(BF16).astype(F32)
        bias_high = bias.astype(BF16).astype(F32)
        bias_mid = (bias - bias_high).astype(BF16).astype(F32)
        bias_low = bias - bias_high - bias_mid
        row = lax.broadcasted_iota(jnp.int32, (8, LANES), 0)
        terms = jnp.where(row == 0, bias_high, jnp.where(row == 1, bias_mid, jnp.where(row == 2, bias_low, 0.0)))
        out_ref[...] = jnp.concatenate([high, rest, terms], axis=0).astype(BF16)

    return pl.pallas_call(
        kernel,
        in_specs=[hbm(), hbm()],
        out_specs=vmem(),
        out_shape=jax.ShapeDtypeStruct((24, LANES), BF16),
        scratch_shapes=[
            pltpu.VMEM(field.shape, BF16),
            pltpu.VMEM(field.shape, BF16),
            pltpu.SemaphoreType.DMA((2 * rows,)),
        ],
        compiler_params=params(),
        cost_estimate=cost(field.size * 1000, field.size * 4),
        name="local_sums",
    )(*in_hbm(field, dpre))


def weight_sums(spectrum, pencil, forward, chans):
    modes_x = spectrum.shape[0] // 2
    tiles = spectrum.shape[1] // LANES
    groups = LANES // chans
    step = 2 * LANES
    full = chans * chans
    parts = full // step

    def kernel(u_ref, p_ref, f_ref, d_ref, own_ref, shared_ref):
        def stack(ref):
            return jnp.concatenate([ref[:, k * LANES : (k + 1) * LANES] for k in range(tiles)], axis=0)

        left = stack(u_ref)
        d_ref[...] = dot(f_ref[...], p_ref[...]).astype(BF16)
        repeat = jnp.concatenate(
            [lane_equals(LANES, LANES, lambda l: l % chans, chans * g) for g in range(groups)], axis=1
        )
        right = dot(stack(d_ref), repeat)
        for a in range(parts):
            sums = {}
            for g in range(groups):
                pick = lane_equals(LANES, step, lambda l: l // chans, g * chans + a * (step // chans))
                spread_u = dot(left, pick)
                for k in range(tiles):
                    kind = 0 if k < 2 * tiles // 3 else 1
                    re = slice(2 * k * modes_x, (2 * k + 1) * modes_x)
                    im = slice((2 * k + 1) * modes_x, (2 * k + 2) * modes_x)
                    for z in range(2):
                        lanes = slice(z * LANES, (z + 1) * LANES)
                        ur, ui = spread_u[re, lanes], spread_u[im, lanes]
                        dr = right[re, g * LANES : (g + 1) * LANES]
                        di = right[im, g * LANES : (g + 1) * LANES]
                        for t, term in ((0, ur * dr + ui * di), (1, ur * di - ui * dr)):
                            key = (kind, t, z)
                            sums[key] = term if key not in sums else sums[key] + term
            for t in range(2):
                lanes = slice(t * full + a * step, t * full + (a + 1) * step)
                own_ref[:, lanes] = jnp.concatenate([sums[0, t, 0], sums[0, t, 1]], axis=1).astype(BF16)
                shared_ref[:, lanes] = jnp.concatenate([sums[1, t, 0], sums[1, t, 1]], axis=1)

    return pl.pallas_call(
        kernel,
        in_specs=[vmem()] * 3,
        out_shape=(
            jax.ShapeDtypeStruct(spectrum.shape, BF16),
            jax.ShapeDtypeStruct((modes_x, 2 * full), BF16),
            jax.ShapeDtypeStruct((modes_x, 2 * full), F32),
        ),
        compiler_params=params(),
        cost_estimate=cost(2 * 288 * 128 * 4096, 4 * 1024 * 1024),
        name="weight_sums",
    )(spectrum, pencil, forward)


def make_shard(me, own, shared, other, stats):
    rows, full2 = own.shape
    full = full2 // 2
    half = full // 2
    width = full2 + full + stats.shape[1]

    def kernel(me_ref, o_ref, s_ref, r_ref, st_ref, out_ref):
        first = me_ref[0] % 2 == 0
        out_ref[:, 0:full2] = o_ref[...]
        for t in range(2):
            low = slice(t * full, t * full + half)
            high = slice(t * full + half, (t + 1) * full)
            mine = jnp.where(first, s_ref[:, low], s_ref[:, high])
            theirs = jnp.where(first, r_ref[:, low], r_ref[:, high])
            out_ref[:, full2 + t * half : full2 + (t + 1) * half] = (mine + theirs).astype(BF16)
        out_ref[:, full2 + full :] = st_ref[...]

    return pl.pallas_call(
        kernel,
        in_specs=[smem()] + [vmem()] * 4,
        out_shape=jax.ShapeDtypeStruct((rows, width), BF16),
        compiler_params=params(),
        cost_estimate=cost(100000, 1000000),
        name="make_shard",
    )(me, own, shared, other, stats)


def ring_chip(spot, chips):
    return jnp.where(spot < chips // 2, 2 * spot, 2 * (chips - 1 - spot) + 1)


def ring_spot(chip, chips):
    return jnp.where(chip % 2 == 0, chip // 2, chips - 1 - chip // 2)


def read_sums(ref, full):
    sums = ref[:, 3 * full : 3 * full + LANES].astype(F32)
    return jnp.concatenate([sums[0:8] + sums[8:16], sums[16:24]], axis=0)


def early_sums(shards_all, chans):
    count = len(shards_all)

    def kernel(*refs):
        for n in range(count):
            refs[count][n] = read_sums(refs[n], chans * chans)

    return pl.pallas_call(
        kernel,
        in_specs=[vmem()] * count,
        out_specs=vmem(),
        out_shape=jax.ShapeDtypeStruct((count, 16, LANES), F32),
        compiler_params=params(),
        cost_estimate=cost(3 * 10**10, 4 * 1024 * 1024),
        name="early_sums",
    )(*shards_all)


def shard_places(me, turns, chips):
    spot = ring_spot(me // 2, chips)
    core = me % 2
    return [
        (ring_chip((spot + chips - back) % chips, chips), 1 - core if swapped else core) for back, swapped in turns
    ]


def place_tile(scr, refs, places, turns, k, modes_y, tiles):
    rows = refs[0].shape[0]
    part = tiles // 4
    chips = modes_y // 3
    keeper = k % (2 * part) // part
    at = tiles + k // (2 * part) * part + k % part
    for n, (chip, core) in enumerate(places):
        own = pl.ds(chip + 2 * chips * core, rows, stride=modes_y)
        scr[k, own, :] = refs[n][:, k * LANES : (k + 1) * LANES].astype(F32)
        if turns[n][1]:
            continue
        mate = turns.index((turns[n][0], True))
        lanes = slice(at * LANES, (at + 1) * LANES)
        shared = pl.ds(chip + chips, rows, stride=modes_y)
        scr[k, shared, :] = jnp.where(core == keeper, refs[n][:, lanes], refs[mate][:, lanes]).astype(F32)


def assemble_first(me, shards_all, known, turns, modes_y, chans, chips):
    rows = shards_all[0].shape[0]
    count = len(shards_all)
    tiles = 2 * chans * chans // LANES

    def kernel(me_ref, *refs):
        places = shard_places(me_ref[0], turns, chips)
        for k in range(tiles):
            place_tile(refs[count], refs[:count], places, turns, k, modes_y, tiles)
        for n in range(known, count):
            refs[count + 1][n - known] = read_sums(refs[n], chans * chans)

    return pl.pallas_call(
        kernel,
        in_specs=[smem()] + [vmem()] * count,
        out_specs=(vmem(), vmem()),
        out_shape=(
            jax.ShapeDtypeStruct((tiles, (rows + 1) * modes_y, LANES), F32),
            jax.ShapeDtypeStruct((count - known, 16, LANES), F32),
        ),
        compiler_params=params(),
        cost_estimate=cost(1000000, 4 * 1024 * 1024),
        name="assemble_first",
    )(me, *shards_all)


def assemble(me, scr, early, more, shards_all, turns, modes_y, chans, chips):
    rows = shards_all[0].shape[0]
    full = chans * chans
    tiles = 2 * full // LANES
    count = len(shards_all)
    total_count = len(turns)
    before = total_count - count
    known = early.shape[0]

    def kernel(me_ref, scr_in, e_ref, m_ref, *refs):
        ins, (scr, g_ref, l_ref, b_ref, stat, out, sem) = refs[:count], refs[count:]
        places = shard_places(me_ref[0], turns, chips)
        copies = []
        for k in range(tiles):
            place_tile(scr, ins, places[before:], turns[before:], k, modes_y, tiles)
            lanes = slice(k * LANES, (k + 1) * LANES)
            for j in range(rows):
                out[j, :, lanes] = scr[k, j * modes_y : (j + 1) * modes_y, :].astype(BF16)
            if k % 4 == 3:
                lanes = pl.ds((k - 3) * LANES, 4 * LANES)
                copies.append(pltpu.make_async_copy(out.at[:, :, lanes], g_ref.at[:, :, lanes], sem.at[k // 4]))
                copies[-1].start()
        for n, (chip, core) in enumerate(places):
            if n < known:
                stat[2 * chip + core] = e_ref[n]
            elif n < before:
                stat[2 * chip + core] = m_ref[n - known]
            else:
                stat[2 * chip + core] = read_sums(ins[n - before], full)
        total = stat[0]
        for n in range(1, total_count):
            total = total + stat[n]
        for k in range(chans // 8):
            piece = total[0:8] if k == 0 else pltpu.roll(total[0:8], LANES - k * chans, 1)
            l_ref[8 * k : 8 * k + 8, :] = piece[:, 0:chans]
        b_ref[...] = jnp.sum(total[8:16], axis=0, keepdims=True)[:, 0:chans]
        for copy in copies:
            copy.wait()

    shape = (rows, modes_y, 2 * full)
    return pl.pallas_call(
        kernel,
        in_specs=[smem()] + [vmem()] * (3 + count),
        out_specs=(vmem(), hbm(), vmem(), vmem()),
        out_shape=(
            jax.ShapeDtypeStruct(scr.shape, F32),
            pltpu.HBM(shape, BF16),
            jax.ShapeDtypeStruct((chans, chans), F32),
            jax.ShapeDtypeStruct((1, chans), F32),
        ),
        input_output_aliases={1: 0},
        scratch_shapes=[
            pltpu.VMEM((total_count, 16, LANES), F32),
            pltpu.VMEM(shape, BF16),
            pltpu.SemaphoreType.DMA((tiles // 4,)),
        ],
        compiler_params=params(),
        cost_estimate=cost(1000000, 8 * 1024 * 1024),
        name="assemble",
    )(me, scr, early, more, *shards_all)[1:]


def back_to_field(dpre, pencil, table_t, block_weight, chips, half):
    rows, length, width = dpre.shape
    chunk = 128

    def kernel(d_hbm, p_ref, tt_ref, w_ref, out_hbm, d_ref, out_ref, bscr, sem, out_sem):
        copies = start_all([(d_hbm.at[x], d_ref.at[x]) for x in range(rows)], sem)
        cut_lanes(bscr, p_ref)
        out_copies = []
        for x in range(rows):
            copies[x].wait()
            coeff = gather_rows(bscr, x, chips, half)
            for k in range(length // chunk):
                where = pl.ds(k * chunk, chunk)
                d = d_ref[x, where, :]
                spec = dot(tt_ref[where, :], coeff)
                for h in range(2):
                    lanes = slice(h * half, (h + 1) * half)
                    out_ref[x, where, lanes] = (spec[:, lanes] + dot(d[:, lanes], w_ref[...])).astype(BF16)
            out_copies.append(pltpu.make_async_copy(out_ref.at[x], out_hbm.at[x], out_sem.at[x]))
            out_copies[-1].start()
        for copy in out_copies:
            copy.wait()

    return pl.pallas_call(
        kernel,
        in_specs=[hbm()] + [vmem()] * 3,
        out_specs=hbm(),
        out_shape=pltpu.HBM(dpre.shape, BF16),
        scratch_shapes=[
            pltpu.VMEM(dpre.shape, BF16),
            pltpu.VMEM(dpre.shape, BF16),
            pltpu.VMEM(cut_shape(pencil.shape), F32),
            pltpu.SemaphoreType.DMA((rows,)),
            pltpu.SemaphoreType.DMA((rows,)),
        ],
        compiler_params=params(),
        cost_estimate=cost(dpre.size * 500, dpre.size * 4),
        name="back_to_field",
    )(*in_hbm(dpre), pencil, table_t, block_weight)


def exchange(pencil):
    return lax.all_to_all(pencil, "xy", split_axis=0, concat_axis=0, tiled=True)


class Ring:
    def __init__(self, shard, chips):
        order = [ring_chip_int(i, chips) for i in range(chips)]
        self.chips = chips
        self.hops = {
            way: [(2 * order[i] + c, 2 * order[(i + way) % chips] + c) for i in range(chips) for c in range(2)]
            for way in (1, -1)
        }
        self.swap = [(i, i ^ 1) for i in range(2 * chips)]
        self.step = 0
        self.ahead = self.back = shard
        self.parts, self.turns = [], []
        self.keep(shard, 0)

    def keep(self, piece, turn):
        self.parts.append(piece)
        self.turns.append((turn, False))
        self.parts.append(lax.ppermute(piece, "xy", self.swap))
        self.turns.append((turn, True))

    def hop(self):
        self.step += 1
        self.ahead = lax.ppermute(self.ahead, "xy", self.hops[1])
        if self.step < self.chips // 2:
            self.back = lax.ppermute(self.back, "xy", self.hops[-1])

    def settle(self):
        self.keep(self.ahead, self.step)
        if self.step < self.chips // 2:
            self.keep(self.back, self.chips - self.step)

    def tie(self, other):
        self.ahead, self.back, other = lax.optimization_barrier((self.ahead, self.back, other))
        return other

    def hold(self, other):
        self.ahead, other = lax.optimization_barrier((self.ahead, other))
        return other


def ring_chip_int(spot, chips):
    return 2 * spot if spot < chips // 2 else 2 * (chips - 1 - spot) + 1


def fast_shards(field, spectral_weight, local_weight, bias, cotangent):
    rows, length_y, width = field.shape
    chans = local_weight.shape[0]
    planes = width // chans
    modes_x, modes_y = spectral_weight.shape[:2]
    devices = lax.axis_size("xy")
    chips = devices // 2
    half = width // 2
    me = lax.axis_index("xy")
    table_y = np_ytable(modes_y, length_y, False)
    table_yw = np_ytable(modes_y, length_y, True)
    table_y_t, table_yw_t = (np.ascontiguousarray(t.T) for t in (table_y, table_yw))
    ones = np.ones((length_y, 3), table_yw_t.dtype)
    zeros = np.zeros((length_y, -(table_yw_t.shape[1] + 3) % 16), table_yw_t.dtype)
    table_yw_t = np.concatenate([table_yw_t, ones, zeros], axis=1)
    forward, inverse = np_xtables(modes_x, rows * devices)
    me_id = me.astype(jnp.int32)[None]

    send = rows_to_modes(field, table_y, chips, half)
    pencil = exchange(send)
    tables = [jnp.asarray(t) for t in (forward, inverse, table_yw_t, table_yw, table_y_t)]
    plain, turned, block, block_t, bias_row, *tables = prepare(
        me_id, spectral_weight, local_weight, bias[None, :], tables, chips, half
    )
    forward, inverse, table_yw_t, table_yw, table_y_t = tables
    spectrum, send, *first_rows = mode_step(pencil, plain, forward, inverse, field, cotangent, chans)
    pencil = exchange(send)
    output_field, dpre, send = pointwise(
        field, cotangent, first_rows, pencil, table_yw_t, table_yw, block, bias_row, chips, half
    )
    pencil = exchange(send)
    stats = local_sums(field, dpre, chans, half)
    pencil, stats = lax.optimization_barrier((pencil, stats))
    grads, own, shared = weight_sums(spectrum, pencil, forward, chans)
    other = lax.ppermute(shared, "xy", [(i, i ^ 1) for i in range(devices)])
    shard = make_shard(me_id, own, shared, other, stats)

    ring = Ring(shard, chips)
    grads = ring.tie(grads)
    ring.hop()
    send = adjoint_step(grads, turned, inverse, chans)
    send = ring.tie(send)
    ring.settle()
    first = list(ring.parts)
    ring.hop()
    pencil = exchange(send)
    ring.settle()
    early, turns = list(ring.parts), list(ring.turns)
    sums = early_sums(first, chans)
    sums = ring.tie(sums)
    ring.hop()
    pencil, sums = lax.optimization_barrier((pencil, sums))
    ring.settle()
    ring.hop()
    field_grad = back_to_field(dpre, pencil, table_y_t, block_t, chips, half)
    early[0], field_grad = lax.optimization_barrier((early[0], field_grad))
    scr, more = assemble_first(me_id, early, len(first), turns, modes_y, chans, chips)
    scr = ring.hold(scr)
    ring.settle()
    late = ring.parts[len(early) :]
    spectral_grad, local_grad, bias_grad = assemble(
        me_id, scr, sums, more, late, ring.turns, modes_y, chans, chips
    )
    return output_field, field_grad, spectral_grad, local_grad, bias_grad.reshape(chans)


def fits(field, spectral_weight, local_weight, devices):
    rows, length_y, width = field.shape
    chans = local_weight.shape[0]
    modes_x, modes_y = spectral_weight.shape[:2]
    return (
        rows == 4
        and chans == 32
        and width == 512
        and length_y % 128 == 0
        and modes_x == 24
        and devices == 16
        and 2 * modes_y == 3 * devices
    )


def shards(field, spectral_weight, local_weight, bias, cotangent):
    if fits(field, spectral_weight, local_weight, lax.axis_size("xy")):
        return fast_shards(field, spectral_weight, local_weight, bias, cotangent)
    return general_shards(field, spectral_weight, local_weight, bias, cotangent)


def solution(mesh):
    return jax.shard_map(
        shards,
        mesh=mesh,
        in_specs=(P(("groups", "xy"), None, None), P(), P(), P(), P(("groups", "xy"), None, None)),
        out_specs=(
            P(("groups", "xy"), None, None),
            P(("groups", "xy"), None, None),
            P("groups", None, None),
            P("groups", None),
            P("groups"),
        ),
        check_vma=False,
    )
```

```python
import math

import jax
import jax.numpy as jnp
import ml_dtypes
import numpy as np
from jax import lax
from jax.experimental import pallas as pl
from jax.experimental.pallas import tpu as pltpu
from jax.sharding import PartitionSpec as P


def ytable(count, length, weighted):
    modes = jnp.arange(count, dtype=jnp.int32)
    places = jnp.arange(length, dtype=jnp.int32)
    phase = 2.0 * math.pi * (modes[:, None] * places[None, :] % length).astype(jnp.float32) / length
    factor = (
        jnp.where(modes == 0, 1.0, 2.0).astype(jnp.float32)
        if weighted
        else jnp.ones((count,), jnp.float32)
    )
    scale = factor[:, None] / math.sqrt(length)
    return jnp.stack([scale * jnp.cos(phase), -scale * jnp.sin(phase)]).astype(jnp.bfloat16)


def xtable(count, length, places):
    index = jnp.arange(count, dtype=jnp.int32)
    modes = jnp.where(index < count // 2, index, length - count + index)
    phase = 2.0 * math.pi * (modes[:, None] * places[None, :] % length).astype(jnp.float32) / length
    return (jnp.stack([jnp.cos(phase), jnp.sin(phase)]) / math.sqrt(length)).astype(jnp.bfloat16)


def mult(form, left, right):
    return jnp.einsum(form, left, right, preferred_element_type=jnp.float32)


def to_slab(flat, table, planes):
    rows = flat.shape[0]
    count = table.shape[1]
    chans = flat.shape[2] // planes
    coeff = mult("smy,xyq->xsmq", table, flat).astype(jnp.bfloat16)
    coeff = coeff.reshape(rows, 2, count, planes, chans).transpose(0, 2, 3, 1, 4)
    return coeff.reshape(rows, count * planes, 2 * chans)


def from_slab(slab, table, planes):
    rows = slab.shape[0]
    count = table.shape[1]
    chans = slab.shape[2] // 2
    spread = slab.reshape(rows, count, planes, 2, chans)
    return mult("smy,xmpsc->xypc", table, spread).reshape(rows, table.shape[2], planes * chans)


def forward_x(table, pencil):
    proj = mult("ajx,xnsc->ajnsc", table, pencil)
    real_part = proj[0, :, :, 0] + proj[1, :, :, 1]
    imag_part = proj[0, :, :, 1] - proj[1, :, :, 0]
    return jnp.stack([real_part, imag_part], axis=2).astype(jnp.bfloat16)


def inverse_x(table, modes):
    proj = mult("ajx,jnsc->axnsc", table, modes)
    real_part = proj[0, :, :, 0] - proj[1, :, :, 1]
    imag_part = proj[0, :, :, 1] + proj[1, :, :, 0]
    return jnp.stack([real_part, imag_part], axis=2).astype(jnp.bfloat16)


def mix_modes(spectrum, weights):
    real_part = mult("jnc,jnco->jno", spectrum[:, :, 0], weights[:, :, 0]) - mult(
        "jnc,jnco->jno", spectrum[:, :, 1], weights[:, :, 1]
    )
    imag_part = mult("jnc,jnco->jno", spectrum[:, :, 0], weights[:, :, 1]) + mult(
        "jnc,jnco->jno", spectrum[:, :, 1], weights[:, :, 0]
    )
    return jnp.stack([real_part, imag_part], axis=2).astype(jnp.bfloat16)


def adjoint_mix(grads, weights):
    real_part = mult("jnco,jno->jnc", weights[:, :, 0], grads[:, :, 0]) + mult(
        "jnco,jno->jnc", weights[:, :, 1], grads[:, :, 1]
    )
    imag_part = mult("jnco,jno->jnc", weights[:, :, 0], grads[:, :, 1]) - mult(
        "jnco,jno->jnc", weights[:, :, 1], grads[:, :, 0]
    )
    return jnp.stack([real_part, imag_part], axis=2).astype(jnp.bfloat16)


def pair_grad(spectrum, grads):
    real_part = mult("jmpc,jmpo->jmco", spectrum[:, :, :, 0], grads[:, :, :, 0]) + mult(
        "jmpc,jmpo->jmco", spectrum[:, :, :, 1], grads[:, :, :, 1]
    )
    imag_part = mult("jmpc,jmpo->jmco", spectrum[:, :, :, 0], grads[:, :, :, 1]) - mult(
        "jmpc,jmpo->jmco", spectrum[:, :, :, 1], grads[:, :, :, 0]
    )
    return jnp.stack([real_part, imag_part], axis=2)


def to_modes(slab, table_full):
    count = table_full.shape[1]
    pencil = lax.all_to_all(slab, "xy", split_axis=1, concat_axis=0, tiled=True)
    chans = pencil.shape[2] // 2
    items = pencil.shape[1]
    spread = pencil.reshape(pencil.shape[0], items, 2, chans)
    return forward_x(table_full, spread).reshape(count, items, 2 * chans)


def to_space(modes, table_full):
    count, pairs_dev, twice, chans = modes.shape
    pencil = inverse_x(table_full, modes)
    moved = lax.all_to_all(
        pencil.reshape(pencil.shape[0], pairs_dev, 2 * chans),
        "xy",
        split_axis=0,
        concat_axis=1,
        tiled=True,
    )
    return moved


def general_shards(field, spectral_weight, local_weight, bias, cotangent):
    rows, length_y, width_all = field.shape
    chans = local_weight.shape[0]
    planes = width_all // chans
    modes_x, modes_y = (spectral_weight.shape[0], spectral_weight.shape[1])
    devices = lax.axis_size("xy")
    length_x = rows * devices
    pairs_dev = modes_y * planes // devices
    offset = lax.axis_index("xy")
    table_y = ytable(modes_y, length_y, False)
    table_yw = ytable(modes_y, length_y, True)
    table_x = xtable(modes_x, length_x, jnp.arange(length_x, dtype=jnp.int32))
    weight_all = spectral_weight.reshape(modes_x, modes_y, 2, chans, chans)
    ky_index = (offset * pairs_dev + jnp.arange(pairs_dev, dtype=jnp.int32)) // planes
    weight_pairs = jnp.take(weight_all, ky_index, axis=1)
    spectrum = to_modes(to_slab(field, table_y, planes), table_x).reshape(
        modes_x, pairs_dev, 2, chans
    )
    mixed = mix_modes(spectrum, weight_pairs)
    spatial = from_slab(to_space(mixed, table_x), table_yw, planes)
    field4 = field.reshape(rows, length_y, planes, chans)
    local_term = mult("xypc,co->xypo", field4, local_weight)
    preact = spatial.reshape(rows, length_y, planes, chans) + local_term + bias
    output_field = jax.nn.gelu(preact).astype(jnp.bfloat16).reshape(rows, length_y, width_all)
    unused, pullback = jax.vjp(jax.nn.gelu, preact)
    grad_pre = pullback(cotangent.reshape(rows, length_y, planes, chans).astype(jnp.float32))[
        0
    ].astype(jnp.bfloat16)
    bias_part = jnp.sum(grad_pre.astype(jnp.float32), axis=(0, 1, 2))
    weight_part = mult("xypc,xypo->co", field4, grad_pre)
    back_local = mult("xypo,co->xypc", grad_pre, local_weight)
    grad_slab = to_slab(grad_pre.reshape(rows, length_y, width_all), table_yw, planes)
    grad_modes = to_modes(grad_slab, table_x).reshape(modes_x, pairs_dev, 2, chans)
    grad_spec = adjoint_mix(grad_modes, weight_pairs)
    back_spec = from_slab(to_space(grad_spec, table_x), table_y, planes)
    field_grad = (back_spec + back_local.reshape(rows, length_y, width_all)).astype(jnp.bfloat16)
    per_pair = pair_grad(
        spectrum.reshape(modes_x, pairs_dev, 1, 2, chans),
        grad_modes.reshape(modes_x, pairs_dev, 1, 2, chans),
    )
    onehot = (ky_index[:, None] == jnp.arange(modes_y, dtype=jnp.int32)[None, :]).astype(
        jnp.float32
    )
    partial_grad = jnp.einsum("jnsco,nm->jmsco", per_pair, onehot, precision=lax.Precision.HIGHEST)
    total, local_grad, bias_grad = lax.psum((partial_grad, weight_part, bias_part), "xy")
    spectral_grad = total.reshape(modes_x, modes_y, 2 * chans * chans).astype(jnp.bfloat16)
    return (output_field, field_grad, spectral_grad, local_grad, bias_grad)


F32 = jnp.float32
BF16 = jnp.bfloat16
LANES = 128
VMEM_LIMIT = 24 * 1024 * 1024


def dot(left, right):
    return jnp.dot(left, right, preferred_element_type=F32)


def params(**kwargs):
    return pltpu.CompilerParams(vmem_limit_bytes=VMEM_LIMIT, **kwargs)


def cost(flops, bytes_accessed):
    return pl.CostEstimate(flops=flops, bytes_accessed=bytes_accessed, transcendentals=0)


def np_ytable(count, length, weighted):
    modes = np.arange(count)
    places = np.arange(length)
    phase = np.float32(2.0 * math.pi) * (modes[:, None] * places[None, :] % length).astype(np.float32) / np.float32(length)
    factor = np.where(modes == 0, 1.0, 2.0).astype(np.float32) if weighted else np.ones((count,), np.float32)
    scale = (factor / np.float32(math.sqrt(length)))[:, None]
    both = np.stack([scale * np.cos(phase), -scale * np.sin(phase)]).astype(ml_dtypes.bfloat16)
    return both.reshape(2 * count, length)


def np_xtables(count, length):
    index = np.arange(count)
    modes = np.where(index < count // 2, index, length - count + index)
    places = np.arange(length)
    phase = np.float32(2.0 * math.pi) * (modes[:, None] * places[None, :] % length).astype(np.float32) / np.float32(length)
    norm = np.float32(math.sqrt(length))
    cosines = np.cos(phase) / norm
    sines = np.sin(phase) / norm
    forward = np.stack([np.stack([cosines, sines], -1), np.stack([-sines, cosines], -1)])
    forward = forward.reshape(2 * count, 2 * length).astype(ml_dtypes.bfloat16)
    return forward, np.ascontiguousarray(forward.T)


def lane_equals(rows, lanes, divide, offset):
    row = lax.broadcasted_iota(jnp.int32, (rows, lanes), 0)
    lane = lax.broadcasted_iota(jnp.int32, (rows, lanes), 1)
    return jnp.where(row - divide(lane) == offset, 1.0, 0.0).astype(BF16)


def start_all(pairs, sem):
    copies = [pltpu.make_async_copy(src, dst, sem.at[n]) for n, (src, dst) in enumerate(pairs)]
    for copy in copies:
        copy.start()
    return copies


def hbm():
    return pl.BlockSpec(memory_space=pltpu.HBM)


def in_hbm(*arrays):
    return [pltpu.with_memory_space_constraint(a, pltpu.HBM) for a in arrays]


def vmem():
    return pl.BlockSpec(memory_space=pltpu.VMEM)


def smem():
    return pl.BlockSpec(memory_space=pltpu.SMEM)


def scatter_rows(dst, sums, place, chips, half):
    tiles = half // LANES
    for s in range(2):
        for core in range(2):
            where = pl.ds(core * 8 + 2 * place + s, chips, stride=16)
            own = (3 * s + 2 * core) * chips
            shared = (3 * s + 1) * chips
            for k in range(2 * tiles):
                dst[k, where, :] = sums[own : own + chips, k * LANES : (k + 1) * LANES]
            for k in range(tiles):
                at = (core * tiles + k) * LANES
                dst[2 * tiles + k, where, :] = sums[shared : shared + chips, at : at + LANES]


def gather_rows(src, place, chips, half):
    tiles = half // LANES
    out = []
    for s in range(2):
        one = pl.ds(2 * place + s, chips, stride=16)
        two = pl.ds(8 + 2 * place + s, chips, stride=16)
        own = range(2 * tiles)
        shared = range(2 * tiles, 3 * tiles)
        out.append(jnp.concatenate([src[k, one, :] for k in own], axis=1))
        out.append(jnp.concatenate([src[k, w, :] for w in (one, two) for k in shared], axis=1))
        out.append(jnp.concatenate([src[k, two, :] for k in own], axis=1))
    return jnp.concatenate(out, axis=0).astype(BF16)


def cut_lanes(dst, src):
    for k in range(dst.shape[0]):
        dst[k, 0 : src.shape[0], :] = src[:, k * LANES : (k + 1) * LANES].astype(F32)


def join_lanes(dst, src):
    for k in range(src.shape[0]):
        dst[:, k * LANES : (k + 1) * LANES] = src[k, 0 : dst.shape[0], :].astype(BF16)


def cut_shape(shape):
    return (shape[1] // LANES, shape[0] + 16, LANES)


def rows_to_modes(field, table, chips, half):
    rows, length, width = field.shape
    shape = (chips * 16, 3 * half)

    def kernel(u_hbm, t_hbm, out_hbm, u_ref, t_ref, scr, out_ref, sem, out_sem):
        copies = start_all([(t_hbm, t_ref)] + [(u_hbm.at[x], u_ref.at[x]) for x in range(rows)], sem)
        copies[0].wait()
        for x in range(rows):
            copies[1 + x].wait()
            scatter_rows(scr, dot(t_ref[...], u_ref[x]), x, chips, half)
        join_lanes(out_ref, scr)
        copy = pltpu.make_async_copy(out_ref, out_hbm, out_sem)
        copy.start()
        copy.wait()

    return pl.pallas_call(
        kernel,
        in_specs=[hbm(), hbm()],
        out_specs=hbm(),
        out_shape=pltpu.HBM(shape, BF16),
        scratch_shapes=[
            pltpu.VMEM(field.shape, BF16),
            pltpu.VMEM(table.shape, BF16),
            pltpu.VMEM(cut_shape(shape), F32),
            pltpu.VMEM(shape, BF16),
            pltpu.SemaphoreType.DMA((1 + rows,)),
            pltpu.SemaphoreType.DMA,
        ],
        compiler_params=params(),
        cost_estimate=cost(2 * table.size * rows * width, field.size * 2),
        name="rows_to_modes",
    )(*in_hbm(field, table))


def prepare(me, weights, local_weight, bias, tables, chips, half):
    modes_x, modes_y, full2 = weights.shape
    chans = local_weight.shape[0]
    tiles = full2 // LANES
    rows = 4 * modes_x
    groups = full2 // 2 // LANES
    batch = 6

    count = len(tables)

    def kernel(me_ref, w_hbm, l_ref, b_ref, *refs):
        tables_hbm, (plain_ref, turned_ref, block_ref, block_t_ref, bias_ref) = refs[:count], refs[count : count + 5]
        tables_ref, (w_ref, scr, pick, one, two, sem, table_sem) = refs[count + 5 : 2 * count + 5], refs[2 * count + 5 :]
        table_copies = start_all(list(zip(tables_hbm, tables_ref)), table_sem)
        cuts = [pl.ds(j, batch) for j in range(0, modes_x, batch)]
        copies = start_all([(w_hbm.at[cut], w_ref.at[cut]) for cut in cuts], sem)

        spread = lane_equals(chans, half, lambda l: l % chans, 0)
        row = lax.broadcasted_iota(jnp.int32, (half, half), 0) // chans
        lane = lax.broadcasted_iota(jnp.int32, (half, half), 1) // chans
        local = l_ref[...]
        for ref, dims in ((block_ref, 1), (block_t_ref, 0)):
            wide = lax.dot_general(local, spread, (((dims,), (0,)), ((), ())), preferred_element_type=F32)
            wide = jnp.concatenate([wide] * (half // chans), axis=0)
            ref[...] = jnp.where(row == lane, wide, 0.0).astype(BF16)
        value = jnp.concatenate([b_ref[...]] * 8, axis=0)
        high = value.astype(BF16)
        mid = (value - high.astype(F32)).astype(BF16)
        low = (value - high.astype(F32) - mid.astype(F32)).astype(BF16)
        wide = dot(high, spread) + dot(mid, spread) + dot(low, spread)
        bias_ref[...] = jnp.concatenate([wide, wide], axis=1)

        for n, first in enumerate(range(0, modes_x, batch)):
            copies[n].wait()
            for j in range(first, first + batch):
                for k in range(tiles):
                    scr[k, j * modes_y : (j + 1) * modes_y, :] = w_ref[j, :, k * LANES : (k + 1) * LANES].astype(F32)
        chip, core = me_ref[0] // 2, me_ref[0] % 2
        for w, mode in enumerate((chip + 2 * chips * core, chip + chips)):
            for k in range(tiles):
                s, g = divmod(k, groups)
                base = (2 * w + s) * modes_x
                pick[g, base : base + modes_x, :] = scr[k, pl.ds(mode, modes_x, stride=modes_y), :]
        per = LANES // chans
        repeat = jnp.concatenate(
            [lane_equals(LANES, LANES, lambda l: l % chans, chans * g) for g in range(per)], axis=1
        )
        pad = jnp.zeros((LANES - rows, LANES), F32)
        for g in range(groups):
            plain_ref[g] = dot(pick[g].astype(BF16), repeat).astype(BF16)
            one[g * LANES : (g + 1) * LANES, :] = jnp.transpose(jnp.concatenate([pick[g], pad]))
        for b in range(chans):
            two[b * chans : (b + 1) * chans, :] = one[pl.ds(b, chans, stride=chans), :]
        for g in range(groups):
            part = jnp.transpose(two[g * LANES : (g + 1) * LANES, :])[0:rows]
            turned_ref[g] = dot(part.astype(BF16), repeat).astype(BF16)
        for copy in table_copies:
            copy.wait()

    shape = (groups, rows, LANES * LANES // chans)
    wide = jax.ShapeDtypeStruct(shape, BF16)
    block = jax.ShapeDtypeStruct((half, half), BF16)
    held = tuple(jax.ShapeDtypeStruct(t.shape, t.dtype) for t in tables)
    return pl.pallas_call(
        kernel,
        in_specs=[smem(), hbm(), vmem(), vmem()] + [hbm()] * count,
        out_specs=(vmem(),) * (5 + count),
        out_shape=(wide, wide, block, block, jax.ShapeDtypeStruct((8, 2 * half), F32)) + held,
        scratch_shapes=[
            pltpu.VMEM(weights.shape, BF16),
            pltpu.VMEM((tiles, (modes_x + 1) * modes_y, LANES), F32),
            pltpu.VMEM((groups, rows, LANES), F32),
            pltpu.VMEM((full2 // 2 + chans, LANES), F32),
            pltpu.VMEM((full2 // 2, LANES), F32),
            pltpu.SemaphoreType.DMA((modes_x // batch,)),
            pltpu.SemaphoreType.DMA((count,)),
        ],
        compiler_params=params(),
        cost_estimate=cost(1000000, 4 * 1024 * 1024),
        name="prepare",
    )(me, *in_hbm(weights), local_weight, bias, *in_hbm(*tables))


def weigh(spec, w_ref, chans, modes_x, adjoint):
    tiles = spec.shape[1] // LANES
    groups = LANES // chans
    stack = jnp.concatenate([spec[:, k * LANES : (k + 1) * LANES] for k in range(tiles)], axis=0)
    real = [None] * tiles
    imag = [None] * tiles
    for pair in range(chans // 2):
        two = [lane_equals(LANES, LANES, lambda l: l // chans * chans, c) for c in (2 * pair, 2 * pair + 1)]
        wide_rows = dot(stack, jnp.concatenate(two, axis=1))
        for c in (2 * pair, 2 * pair + 1):
            lanes = slice((c % 2) * LANES, (c % 2 + 1) * LANES)
            wl = slice((c % groups) * LANES, (c % groups + 1) * LANES)
            for own in range(2):
                base = 2 * own * modes_x
                wr = w_ref[c // groups, base : base + modes_x, wl].astype(F32)
                wi = w_ref[c // groups, base + modes_x : base + 2 * modes_x, wl].astype(F32)
                for k in range(0, 2 * tiles // 3) if own == 0 else range(2 * tiles // 3, tiles):
                    xr = wide_rows[2 * k * modes_x : (2 * k + 1) * modes_x, lanes]
                    xi = wide_rows[(2 * k + 1) * modes_x : (2 * k + 2) * modes_x, lanes]
                    if adjoint:
                        r, i = xr * wr + xi * wi, xi * wr - xr * wi
                    else:
                        r, i = xr * wr - xi * wi, xr * wi + xi * wr
                    real[k] = r if real[k] is None else real[k] + r
                    imag[k] = i if imag[k] is None else imag[k] + i
    return jnp.concatenate([jnp.concatenate(real, axis=1), jnp.concatenate(imag, axis=1)], axis=0).astype(BF16)


def mode_step(pencil, spread_w, forward, inverse, field, cotangent, chans):
    modes_x = forward.shape[0] // 2

    def kernel(p_ref, w_ref, f_ref, i_ref, u_hbm, c_hbm, spec_ref, out_ref, u_ref, c_ref, sem):
        copies = start_all([(u_hbm.at[0], u_ref), (c_hbm.at[0], c_ref)], sem)
        spec = dot(f_ref[...], p_ref[...]).astype(BF16)
        spec_ref[...] = spec
        mixed = weigh(spec, w_ref, chans, modes_x, False)
        out_ref[...] = dot(i_ref[...], mixed).astype(BF16)
        for copy in copies:
            copy.wait()

    return pl.pallas_call(
        kernel,
        in_specs=[vmem()] * 4 + [hbm()] * 2,
        out_specs=(vmem(),) * 4,
        out_shape=(
            jax.ShapeDtypeStruct((2 * modes_x, pencil.shape[1]), BF16),
            jax.ShapeDtypeStruct(pencil.shape, BF16),
            jax.ShapeDtypeStruct(field.shape[1:], BF16),
            jax.ShapeDtypeStruct(field.shape[1:], BF16),
        ),
        scratch_shapes=[pltpu.SemaphoreType.DMA((2,))],
        compiler_params=params(),
        cost_estimate=cost(2 * 48 * 6 * 128 * 4096, spread_w.size * 4),
        name="mode_step",
    )(pencil, spread_w, forward, inverse, *in_hbm(field, cotangent))


def adjoint_step(grads, spread_w, inverse, chans):
    modes_x = grads.shape[0] // 2
    shape = (inverse.shape[0], grads.shape[1])

    def kernel(g_ref, w_ref, i_ref, out_hbm, out_ref, out_sem):
        mixed = weigh(g_ref[...], w_ref, chans, modes_x, True)
        out_ref[...] = dot(i_ref[...], mixed).astype(BF16)
        copy = pltpu.make_async_copy(out_ref, out_hbm, out_sem)
        copy.start()
        copy.wait()

    return pl.pallas_call(
        kernel,
        in_specs=[vmem()] * 3,
        out_specs=hbm(),
        out_shape=pltpu.HBM(shape, BF16),
        scratch_shapes=[pltpu.VMEM(shape, BF16), pltpu.SemaphoreType.DMA],
        compiler_params=params(),
        cost_estimate=cost(2 * 48 * 6 * 128 * 4096, spread_w.size * 4),
        name="adjoint_step",
    )(grads, spread_w, inverse)


def pointwise(field, cotangent, first_rows, pencil, table_t, table, block_weight, bias_row, chips, half):
    rows, length, width = field.shape
    chunk, sub = 128, 16
    modes = table.shape[0]
    depth = table_t.shape[1]

    def kernel(
        u_hbm, c_hbm, u_first, c_first, p_ref, tt_ref, t_ref, w_ref, b_ref, out_hbm, dpre_hbm, send_hbm,
        u_rest, c_rest, out_ref, dpre_ref, send_ref, bscr, dscr, sem, out_sem,
    ):
        copies = []
        for x in range(1, rows):
            pairs = [(u_hbm.at[x], u_rest.at[x - 1]), (c_hbm.at[x], c_rest.at[x - 1])]
            copies.append(start_all(pairs, sem.at[x - 1]))
        cut_lanes(bscr, p_ref)
        root = math.sqrt(2.0 / math.pi)
        bias = b_ref[0:1, :]
        high = bias.astype(BF16)
        mid = (bias - high.astype(F32)).astype(BF16)
        low = (bias - high.astype(F32) - mid.astype(F32)).astype(BF16)
        parts = [t.astype(F32) for t in (high, mid, low)]
        bias = jnp.concatenate(parts + [jnp.zeros((depth - modes - 3, width), F32)], axis=0)
        bias = (0.5 * bias).astype(BF16)
        weight = (0.5 * w_ref[...].astype(F32)).astype(BF16)

        def transform_row(x):
            scatter_rows(dscr, dot(t_ref[...], dpre_ref[x]), x, chips, half)

        def one_row(x):
            if x > 0:
                for copy in copies[x - 1]:
                    copy.wait()
            u_ref = u_rest.at[x - 1] if x > 0 else u_first
            c_ref = c_rest.at[x - 1] if x > 0 else c_first
            coeff = (0.5 * gather_rows(bscr, x, chips, half).astype(F32)).astype(BF16)
            coeff = jnp.concatenate([coeff, bias], axis=0)
            for k in range(length // chunk):
                where = pl.ds(k * chunk, chunk)
                for h in range(2):
                    lanes = slice(h * half, (h + 1) * half)
                    left = jnp.concatenate([u_ref[where, lanes], tt_ref[where, :]], axis=1)
                    right = jnp.concatenate([weight, coeff[:, lanes]], axis=0)
                    halved = dot(left, right)
                    for at in range(0, chunk, sub):
                        place = pl.ds(k * chunk + at, sub)
                        p = halved[at : at + sub]
                        inner = p * (2.0 * root + (8.0 * root * 0.044715) * (p * p))
                        th = jnp.tanh(inner)
                        twice = 1.0 + th
                        out_ref[x, place, lanes] = (p * twice).astype(BF16)
                        slope = 1.5 * inner - (2.0 * root) * p
                        grad = twice * (0.5 + (1.0 - th) * slope)
                        dpre_ref[x, place, lanes] = (c_ref[place, lanes].astype(F32) * grad).astype(BF16)
            pltpu.make_async_copy(out_ref.at[x], out_hbm.at[x], out_sem.at[x]).start()
            pltpu.make_async_copy(dpre_ref.at[x], dpre_hbm.at[x], out_sem.at[rows + x]).start()
            if x > 0:
                transform_row(x - 1)

        for x in range(rows):
            one_row(x)
        transform_row(rows - 1)
        join_lanes(send_ref, dscr)
        pltpu.make_async_copy(send_ref, send_hbm, out_sem.at[2 * rows]).start()
        for x in range(rows):
            pltpu.make_async_copy(out_ref.at[x], out_hbm.at[x], out_sem.at[x]).wait()
            pltpu.make_async_copy(dpre_ref.at[x], dpre_hbm.at[x], out_sem.at[rows + x]).wait()
        pltpu.make_async_copy(send_ref, send_hbm, out_sem.at[2 * rows]).wait()

    return pl.pallas_call(
        kernel,
        in_specs=[hbm(), hbm()] + [vmem()] * 7,
        out_specs=(hbm(), hbm(), hbm()),
        out_shape=(
            pltpu.HBM(field.shape, BF16),
            pltpu.HBM(field.shape, BF16),
            pltpu.HBM(pencil.shape, BF16),
        ),
        scratch_shapes=[
            pltpu.VMEM((rows - 1, length, width), BF16),
            pltpu.VMEM((rows - 1, length, width), BF16),
            pltpu.VMEM(field.shape, BF16),
            pltpu.VMEM(field.shape, BF16),
            pltpu.VMEM(pencil.shape, BF16),
            pltpu.VMEM(cut_shape(pencil.shape), F32),
            pltpu.VMEM(cut_shape(pencil.shape), F32),
            pltpu.SemaphoreType.DMA((rows - 1, 2)),
            pltpu.SemaphoreType.DMA((2 * rows + 1,)),
        ],
        compiler_params=params(),
        cost_estimate=cost(field.size * 1000, field.size * 8),
        name="pointwise",
    )(*in_hbm(field, cotangent), *first_rows, pencil, table_t, table, block_weight, bias_row)


def local_sums(field, dpre, chans, half):
    rows, length, width = field.shape
    slices = half // chans

    def kernel(u_hbm, d_hbm, out_ref, u_ref, d_ref, sem):
        copies = start_all(
            [(u_hbm.at[x], u_ref.at[x]) for x in range(rows)] + [(d_hbm.at[x], d_ref.at[x]) for x in range(rows)], sem
        )
        both = bias = None
        ones = jnp.ones((16, length), BF16)
        for x in range(rows):
            copies[x].wait()
            copies[rows + x].wait()
            for h in range(2):
                lanes = slice(h * half, (h + 1) * half)
                part = lax.dot_general(
                    u_ref[x, :, lanes], d_ref[x, :, lanes], (((0,), (0,)), ((), ())), preferred_element_type=F32
                )
                both = part if both is None else both + part
            part = dot(ones, d_ref[x])[0:8]
            bias = part if bias is None else bias + part
        group = lax.broadcasted_iota(jnp.int32, (chans, half), 1) // chans
        total = jnp.zeros((chans, half), F32)
        for p in range(slices):
            total = jnp.where(group == p, both[p * chans : (p + 1) * chans], total)
        total = sum(total[:, k * LANES : (k + 1) * LANES] for k in range(half // LANES))
        bias = sum(bias[:, k * LANES : (k + 1) * LANES] for k in range(width // LANES))
        shift = LANES // 2
        while shift >= chans:
            total = total + pltpu.roll(total, shift, 1)
            bias = bias + pltpu.roll(bias, shift, 1)
            shift //= 2
        group8 = lax.broadcasted_iota(jnp.int32, (8, LANES), 1) // chans
        folded = jnp.zeros((8, LANES), F32)
        for k in range(chans // 8):
            folded = jnp.where(group8 == k, total[8 * k : 8 * k + 8], folded)
        high = folded.astype(BF16).astype(F32)
        rest = (folded - high).astype(BF16).astype(F32)
        bias_high = bias.astype(BF16).astype(F32)
        bias_mid = (bias - bias_high).astype(BF16).astype(F32)
        bias_low = bias - bias_high - bias_mid
        row = lax.broadcasted_iota(jnp.int32, (8, LANES), 0)
        terms = jnp.where(row == 0, bias_high, jnp.where(row == 1, bias_mid, jnp.where(row == 2, bias_low, 0.0)))
        out_ref[...] = jnp.concatenate([high, rest, terms], axis=0).astype(BF16)

    return pl.pallas_call(
        kernel,
        in_specs=[hbm(), hbm()],
        out_specs=vmem(),
        out_shape=jax.ShapeDtypeStruct((24, LANES), BF16),
        scratch_shapes=[
            pltpu.VMEM(field.shape, BF16),
            pltpu.VMEM(field.shape, BF16),
            pltpu.SemaphoreType.DMA((2 * rows,)),
        ],
        compiler_params=params(),
        cost_estimate=cost(field.size * 1000, field.size * 4),
        name="local_sums",
    )(*in_hbm(field, dpre))


def weight_sums(spectrum, pencil, forward, chans):
    modes_x = spectrum.shape[0] // 2
    tiles = spectrum.shape[1] // LANES
    groups = LANES // chans
    step = 2 * LANES
    full = chans * chans
    parts = full // step

    def kernel(u_ref, p_ref, f_ref, d_ref, own_ref, shared_ref):
        def stack(ref):
            return jnp.concatenate([ref[:, k * LANES : (k + 1) * LANES] for k in range(tiles)], axis=0)

        left = stack(u_ref)
        d_ref[...] = dot(f_ref[...], p_ref[...]).astype(BF16)
        repeat = jnp.concatenate(
            [lane_equals(LANES, LANES, lambda l: l % chans, chans * g) for g in range(groups)], axis=1
        )
        right = dot(stack(d_ref), repeat)
        for a in range(parts):
            sums = {}
            for g in range(groups):
                pick = lane_equals(LANES, step, lambda l: l // chans, g * chans + a * (step // chans))
                spread_u = dot(left, pick)
                for k in range(tiles):
                    kind = 0 if k < 2 * tiles // 3 else 1
                    re = slice(2 * k * modes_x, (2 * k + 1) * modes_x)
                    im = slice((2 * k + 1) * modes_x, (2 * k + 2) * modes_x)
                    for z in range(2):
                        lanes = slice(z * LANES, (z + 1) * LANES)
                        ur, ui = spread_u[re, lanes], spread_u[im, lanes]
                        dr = right[re, g * LANES : (g + 1) * LANES]
                        di = right[im, g * LANES : (g + 1) * LANES]
                        for t, term in ((0, ur * dr + ui * di), (1, ur * di - ui * dr)):
                            key = (kind, t, z)
                            sums[key] = term if key not in sums else sums[key] + term
            for t in range(2):
                lanes = slice(t * full + a * step, t * full + (a + 1) * step)
                own_ref[:, lanes] = jnp.concatenate([sums[0, t, 0], sums[0, t, 1]], axis=1).astype(BF16)
                shared_ref[:, lanes] = jnp.concatenate([sums[1, t, 0], sums[1, t, 1]], axis=1)

    return pl.pallas_call(
        kernel,
        in_specs=[vmem()] * 3,
        out_shape=(
            jax.ShapeDtypeStruct(spectrum.shape, BF16),
            jax.ShapeDtypeStruct((modes_x, 2 * full), BF16),
            jax.ShapeDtypeStruct((modes_x, 2 * full), F32),
        ),
        compiler_params=params(),
        cost_estimate=cost(2 * 288 * 128 * 4096, 4 * 1024 * 1024),
        name="weight_sums",
    )(spectrum, pencil, forward)


def make_shard(me, own, shared, other, stats):
    rows, full2 = own.shape
    full = full2 // 2
    half = full // 2
    width = full2 + full + stats.shape[1]

    def kernel(me_ref, o_ref, s_ref, r_ref, st_ref, out_ref):
        first = me_ref[0] % 2 == 0
        out_ref[:, 0:full2] = o_ref[...]
        for t in range(2):
            low = slice(t * full, t * full + half)
            high = slice(t * full + half, (t + 1) * full)
            mine = jnp.where(first, s_ref[:, low], s_ref[:, high])
            theirs = jnp.where(first, r_ref[:, low], r_ref[:, high])
            out_ref[:, full2 + t * half : full2 + (t + 1) * half] = (mine + theirs).astype(BF16)
        out_ref[:, full2 + full :] = st_ref[...]

    return pl.pallas_call(
        kernel,
        in_specs=[smem()] + [vmem()] * 4,
        out_shape=jax.ShapeDtypeStruct((rows, width), BF16),
        compiler_params=params(),
        cost_estimate=cost(100000, 1000000),
        name="make_shard",
    )(me, own, shared, other, stats)


def ring_chip(spot, chips):
    return jnp.where(spot < chips // 2, 2 * spot, 2 * (chips - 1 - spot) + 1)


def ring_spot(chip, chips):
    return jnp.where(chip % 2 == 0, chip // 2, chips - 1 - chip // 2)


def read_sums(ref, full):
    sums = ref[:, 3 * full : 3 * full + LANES].astype(F32)
    return jnp.concatenate([sums[0:8] + sums[8:16], sums[16:24]], axis=0)


def early_sums(shards_all, chans):
    count = len(shards_all)

    def kernel(*refs):
        for n in range(count):
            refs[count][n] = read_sums(refs[n], chans * chans)

    return pl.pallas_call(
        kernel,
        in_specs=[vmem()] * count,
        out_specs=vmem(),
        out_shape=jax.ShapeDtypeStruct((count, 16, LANES), F32),
        compiler_params=params(),
        cost_estimate=cost(3 * 10**10, 4 * 1024 * 1024),
        name="early_sums",
    )(*shards_all)


def shard_places(me, turns, chips):
    spot = ring_spot(me // 2, chips)
    core = me % 2
    return [
        (ring_chip((spot + chips - back) % chips, chips), 1 - core if swapped else core) for back, swapped in turns
    ]


def place_tile(scr, refs, places, turns, k, modes_y, tiles):
    rows = refs[0].shape[0]
    part = tiles // 4
    chips = modes_y // 3
    keeper = k % (2 * part) // part
    at = tiles + k // (2 * part) * part + k % part
    for n, (chip, core) in enumerate(places):
        own = pl.ds(chip + 2 * chips * core, rows, stride=modes_y)
        scr[k, own, :] = refs[n][:, k * LANES : (k + 1) * LANES].astype(F32)
        if turns[n][1]:
            continue
        mate = turns.index((turns[n][0], True))
        lanes = slice(at * LANES, (at + 1) * LANES)
        shared = pl.ds(chip + chips, rows, stride=modes_y)
        scr[k, shared, :] = jnp.where(core == keeper, refs[n][:, lanes], refs[mate][:, lanes]).astype(F32)


def assemble_first(me, shards_all, known, turns, modes_y, chans, chips):
    rows = shards_all[0].shape[0]
    count = len(shards_all)
    tiles = 2 * chans * chans // LANES

    def kernel(me_ref, *refs):
        places = shard_places(me_ref[0], turns, chips)
        for k in range(tiles):
            place_tile(refs[count], refs[:count], places, turns, k, modes_y, tiles)
        for n in range(known, count):
            refs[count + 1][n - known] = read_sums(refs[n], chans * chans)

    return pl.pallas_call(
        kernel,
        in_specs=[smem()] + [vmem()] * count,
        out_specs=(vmem(), vmem()),
        out_shape=(
            jax.ShapeDtypeStruct((tiles, (rows + 1) * modes_y, LANES), F32),
            jax.ShapeDtypeStruct((count - known, 16, LANES), F32),
        ),
        compiler_params=params(),
        cost_estimate=cost(1000000, 4 * 1024 * 1024),
        name="assemble_first",
    )(me, *shards_all)


def assemble(me, scr, early, more, shards_all, turns, modes_y, chans, chips):
    rows = shards_all[0].shape[0]
    full = chans * chans
    tiles = 2 * full // LANES
    count = len(shards_all)
    total_count = len(turns)
    before = total_count - count
    known = early.shape[0]

    def kernel(me_ref, scr_in, e_ref, m_ref, *refs):
        ins, (scr, g_ref, l_ref, b_ref, stat, out, sem) = refs[:count], refs[count:]
        places = shard_places(me_ref[0], turns, chips)
        copies = []
        for k in range(tiles):
            place_tile(scr, ins, places[before:], turns[before:], k, modes_y, tiles)
            lanes = slice(k * LANES, (k + 1) * LANES)
            for j in range(rows):
                out[j, :, lanes] = scr[k, j * modes_y : (j + 1) * modes_y, :].astype(BF16)
            if k % 4 == 3:
                lanes = pl.ds((k - 3) * LANES, 4 * LANES)
                copies.append(pltpu.make_async_copy(out.at[:, :, lanes], g_ref.at[:, :, lanes], sem.at[k // 4]))
                copies[-1].start()
        for n, (chip, core) in enumerate(places):
            if n < known:
                stat[2 * chip + core] = e_ref[n]
            elif n < before:
                stat[2 * chip + core] = m_ref[n - known]
            else:
                stat[2 * chip + core] = read_sums(ins[n - before], full)
        total = stat[0]
        for n in range(1, total_count):
            total = total + stat[n]
        for k in range(chans // 8):
            piece = total[0:8] if k == 0 else pltpu.roll(total[0:8], LANES - k * chans, 1)
            l_ref[8 * k : 8 * k + 8, :] = piece[:, 0:chans]
        b_ref[...] = jnp.sum(total[8:16], axis=0, keepdims=True)[:, 0:chans]
        for copy in copies:
            copy.wait()

    shape = (rows, modes_y, 2 * full)
    return pl.pallas_call(
        kernel,
        in_specs=[smem()] + [vmem()] * (3 + count),
        out_specs=(vmem(), hbm(), vmem(), vmem()),
        out_shape=(
            jax.ShapeDtypeStruct(scr.shape, F32),
            pltpu.HBM(shape, BF16),
            jax.ShapeDtypeStruct((chans, chans), F32),
            jax.ShapeDtypeStruct((1, chans), F32),
        ),
        input_output_aliases={1: 0},
        scratch_shapes=[
            pltpu.VMEM((total_count, 16, LANES), F32),
            pltpu.VMEM(shape, BF16),
            pltpu.SemaphoreType.DMA((tiles // 4,)),
        ],
        compiler_params=params(),
        cost_estimate=cost(1000000, 8 * 1024 * 1024),
        name="assemble",
    )(me, scr, early, more, *shards_all)[1:]


def back_to_field(dpre, pencil, table_t, block_weight, chips, half):
    rows, length, width = dpre.shape
    chunk = 128

    def kernel(d_hbm, p_ref, tt_ref, w_ref, out_hbm, d_ref, out_ref, bscr, sem, out_sem):
        copies = start_all([(d_hbm.at[x], d_ref.at[x]) for x in range(rows)], sem)
        cut_lanes(bscr, p_ref)
        out_copies = []
        for x in range(rows):
            copies[x].wait()
            coeff = gather_rows(bscr, x, chips, half)
            for k in range(length // chunk):
                where = pl.ds(k * chunk, chunk)
                d = d_ref[x, where, :]
                spec = dot(tt_ref[where, :], coeff)
                for h in range(2):
                    lanes = slice(h * half, (h + 1) * half)
                    out_ref[x, where, lanes] = (spec[:, lanes] + dot(d[:, lanes], w_ref[...])).astype(BF16)
            out_copies.append(pltpu.make_async_copy(out_ref.at[x], out_hbm.at[x], out_sem.at[x]))
            out_copies[-1].start()
        for copy in out_copies:
            copy.wait()

    return pl.pallas_call(
        kernel,
        in_specs=[hbm()] + [vmem()] * 3,
        out_specs=hbm(),
        out_shape=pltpu.HBM(dpre.shape, BF16),
        scratch_shapes=[
            pltpu.VMEM(dpre.shape, BF16),
            pltpu.VMEM(dpre.shape, BF16),
            pltpu.VMEM(cut_shape(pencil.shape), F32),
            pltpu.SemaphoreType.DMA((rows,)),
            pltpu.SemaphoreType.DMA((rows,)),
        ],
        compiler_params=params(),
        cost_estimate=cost(dpre.size * 500, dpre.size * 4),
        name="back_to_field",
    )(*in_hbm(dpre), pencil, table_t, block_weight)


def exchange(pencil):
    return lax.all_to_all(pencil, "xy", split_axis=0, concat_axis=0, tiled=True)


class Ring:
    def __init__(self, shard, chips):
        order = [ring_chip_int(i, chips) for i in range(chips)]
        self.chips = chips
        self.hops = {
            way: [(2 * order[i] + c, 2 * order[(i + way) % chips] + c) for i in range(chips) for c in range(2)]
            for way in (1, -1)
        }
        self.swap = [(i, i ^ 1) for i in range(2 * chips)]
        self.step = 0
        self.ahead = self.back = shard
        self.parts, self.turns = [], []
        self.keep(shard, 0)

    def keep(self, piece, turn):
        self.parts.append(piece)
        self.turns.append((turn, False))
        self.parts.append(lax.ppermute(piece, "xy", self.swap))
        self.turns.append((turn, True))

    def hop(self):
        self.step += 1
        self.ahead = lax.ppermute(self.ahead, "xy", self.hops[1])
        if self.step < self.chips // 2:
            self.back = lax.ppermute(self.back, "xy", self.hops[-1])

    def settle(self):
        self.keep(self.ahead, self.step)
        if self.step < self.chips // 2:
            self.keep(self.back, self.chips - self.step)

    def tie(self, other):
        self.ahead, self.back, other = lax.optimization_barrier((self.ahead, self.back, other))
        return other

    def hold(self, other):
        self.ahead, other = lax.optimization_barrier((self.ahead, other))
        return other


def ring_chip_int(spot, chips):
    return 2 * spot if spot < chips // 2 else 2 * (chips - 1 - spot) + 1


def fast_shards(field, spectral_weight, local_weight, bias, cotangent):
    rows, length_y, width = field.shape
    chans = local_weight.shape[0]
    planes = width // chans
    modes_x, modes_y = spectral_weight.shape[:2]
    devices = lax.axis_size("xy")
    chips = devices // 2
    half = width // 2
    me = lax.axis_index("xy")
    table_y = np_ytable(modes_y, length_y, False)
    table_yw = np_ytable(modes_y, length_y, True)
    table_y_t, table_yw_t = (np.ascontiguousarray(t.T) for t in (table_y, table_yw))
    ones = np.ones((length_y, 3), table_yw_t.dtype)
    zeros = np.zeros((length_y, -(table_yw_t.shape[1] + 3) % 16), table_yw_t.dtype)
    table_yw_t = np.concatenate([table_yw_t, ones, zeros], axis=1)
    forward, inverse = np_xtables(modes_x, rows * devices)
    me_id = me.astype(jnp.int32)[None]

    send = rows_to_modes(field, table_y, chips, half)
    pencil = exchange(send)
    tables = [jnp.asarray(t) for t in (forward, inverse, table_yw_t, table_yw, table_y_t)]
    plain, turned, block, block_t, bias_row, *tables = prepare(
        me_id, spectral_weight, local_weight, bias[None, :], tables, chips, half
    )
    forward, inverse, table_yw_t, table_yw, table_y_t = tables
    spectrum, send, *first_rows = mode_step(pencil, plain, forward, inverse, field, cotangent, chans)
    pencil = exchange(send)
    output_field, dpre, send = pointwise(
        field, cotangent, first_rows, pencil, table_yw_t, table_yw, block, bias_row, chips, half
    )
    pencil = exchange(send)
    stats = local_sums(field, dpre, chans, half)
    pencil, stats = lax.optimization_barrier((pencil, stats))
    grads, own, shared = weight_sums(spectrum, pencil, forward, chans)
    other = lax.ppermute(shared, "xy", [(i, i ^ 1) for i in range(devices)])
    shard = make_shard(me_id, own, shared, other, stats)

    ring = Ring(shard, chips)
    grads = ring.tie(grads)
    ring.hop()
    send = adjoint_step(grads, turned, inverse, chans)
    send = ring.hold(send)
    ring.settle()
    first = list(ring.parts)
    ring.hop()
    pencil = exchange(send)
    ring.settle()
    early, turns = list(ring.parts), list(ring.turns)
    sums = early_sums(first, chans)
    sums = ring.hold(sums)
    ring.hop()
    pencil, sums = lax.optimization_barrier((pencil, sums))
    ring.settle()
    ring.hop()
    field_grad = back_to_field(dpre, pencil, table_y_t, block_t, chips, half)
    early[0], field_grad = lax.optimization_barrier((early[0], field_grad))
    scr, more = assemble_first(me_id, early, len(first), turns, modes_y, chans, chips)
    scr = ring.hold(scr)
    ring.settle()
    late = ring.parts[len(early) :]
    spectral_grad, local_grad, bias_grad = assemble(
        me_id, scr, sums, more, late, ring.turns, modes_y, chans, chips
    )
    return output_field, field_grad, spectral_grad, local_grad, bias_grad.reshape(chans)


def fits(field, spectral_weight, local_weight, devices):
    rows, length_y, width = field.shape
    chans = local_weight.shape[0]
    modes_x, modes_y = spectral_weight.shape[:2]
    return (
        rows == 4
        and chans == 32
        and width == 512
        and length_y % 128 == 0
        and modes_x == 24
        and devices == 16
        and 2 * modes_y == 3 * devices
    )


def shards(field, spectral_weight, local_weight, bias, cotangent):
    if fits(field, spectral_weight, local_weight, lax.axis_size("xy")):
        return fast_shards(field, spectral_weight, local_weight, bias, cotangent)
    return general_shards(field, spectral_weight, local_weight, bias, cotangent)


def solution(mesh):
    return jax.shard_map(
        shards,
        mesh=mesh,
        in_specs=(P(("groups", "xy"), None, None), P(), P(), P(), P(("groups", "xy"), None, None)),
        out_specs=(
            P(("groups", "xy"), None, None),
            P(("groups", "xy"), None, None),
            P("groups", None, None),
            P("groups", None),
            P("groups"),
        ),
        check_vma=False,
    )
```
